32 devices in a mesh: rows: 16 (over z, x, core), heads: 2 (over y).
Axes of the slice: x: 2, y: 2, z: 4, core: 2. Of those that a mesh axis runs over, the one named last changes fastest.
Arguments:
- tokens: bfloat16 [49152, 1152], P(('rows', 'heads')), may hold values from -6 to 6
- condition: bfloat16 [128, 1152], P('rows'), may hold values from -6 to 6
- segment_ids: int32 [48, 1024], P('rows'), may hold values from 0 to 3, never falling along the last dimension, each value on 1 to 512 neighbouring positions
- tile_mask: int32 [48, 8, 8], P('rows'), may hold values 0 or 1
- image_index: int32 [48, 4], P('rows'), may hold values from 0 to 7
- w_ada: float32 [1152, 6912], P(None, 'heads'), may hold values from -0.1875 to 0.1875
- b_ada: float32 [6912], P('heads'), may hold values from -3 to 3
- w_query: float32 [1152, 1152], P('rows', 'heads'), may hold values from -0.1875 to 0.1875
- w_key: float32 [1152, 1152], P('rows', 'heads'), may hold values from -0.1875 to 0.1875
- w_value: float32 [1152, 1152], P('rows', 'heads'), may hold values from -0.1875 to 0.1875
- b_query: float32 [1152], P('heads'), may hold values from -3 to 3
- b_value: float32 [1152], P('heads'), may hold values from -3 to 3
- w_out: float32 [1152, 1152], P('rows', 'heads'), may hold values from -1.5 to 1.5
- b_out: float32 [1152], replicated, may hold values from -3 to 3
- w_up: float32 [1152, 4608], P('rows', 'heads'), may hold values from -0.1875 to 0.1875
- b_up: float32 [4608], P('heads'), may hold values from -3 to 3
- w_down: float32 [1152, 4608], P('rows', 'heads'), may hold values from -0.1875 to 0.1875
- b_down: float32 [1152], replicated, may hold values from -3 to 3
- cotangent: bfloat16 [49152, 1152], P(('rows', 'heads')), may hold values from -6 to 6
Outputs:
- output: bfloat16 [49152, 1152], P(('rows', 'heads'))
- grad_tokens: float32 [49152, 1152], P(('rows', 'heads'))
- grad_condition: float32 [128, 1152], P('rows')
- grad_w_ada: float32 [1152, 6912], P(None, 'heads')
- grad_b_ada: float32 [6912], P('heads')
- grad_w_query: float32 [1152, 1152], P('rows', 'heads')
- grad_w_key: float32 [1152, 1152], P('rows', 'heads')
- grad_w_value: float32 [1152, 1152], P('rows', 'heads')
- grad_b_query: float32 [1152], P('heads')
- grad_b_value: float32 [1152], P('heads')
- grad_w_out: float32 [1152, 1152], P('rows', 'heads')
- grad_b_out: float32 [1152], P('heads')
- grad_w_up: float32 [1152, 4608], P('rows', 'heads')
- grad_b_up: float32 [4608], P('heads')
- grad_w_down: float32 [1152, 4608], P('rows', 'heads')
- grad_b_down: float32 [1152], P('heads')
The draws below stay inside these ranges and needn't reach their ends.
All inputs are finite; a program needn't handle non-finite values. No bound on the sum of `tile_mask` on one device may be relied on, other than what follows from the above.
Results may differ from the reference program's by a relative error of at most 0.014.
The reference program's roundings to bfloat16 on the way count: a program that leaves them out, or rounds other values in their place, can miss the bound.
Values may be sent and summed in bfloat16 or wider, within the bound.
No kernel may reach another device: no remote copies, remote signals or barrier semaphores. Data moves between devices by JAX's collectives and lax.ppermute only.
A program may use at most 576 MiB of HBM per device.

```python
import math
import jax
import jax.numpy as jnp
import numpy as np
from jax import lax

D = 1152
ATTN_HEADS = 16
HEAD_DIM = 72
FF = 4608
L = 1024
TILE = 128
SEGS = 4
SEQ_DEV = 3
IMG_DEV = 8
SEQS = 48
TOKENS = 49152
IMAGES = 128


def with_ends(array, stream_key, smallest, high):
    extent = array.shape
    place = [jax.random.randint(jax.random.fold_in(stream_key, axis), (), 0, extent[axis]) for axis in range(len(extent))]
    array = array.at[tuple(place)].set(smallest)
    longest = extent.index(max(extent))
    place[longest] = (place[longest] + 1) % extent[longest]
    return array.at[tuple(place)].set(high)


def steps_of(stream_key, shape, shards, least, high):
    loudness, own = 1.0, jax.random.fold_in(stream_key, 6)
    for position, parts in shards:
        heights = jnp.exp(jax.random.uniform(jax.random.fold_in(own, position), (parts,), jnp.float32, least / len(shards), high / len(shards)))
        loudness = loudness * jnp.repeat(heights, shape[position] // parts).reshape([-1 if axis == position else 1 for axis in range(len(shape))])
    return loudness


def split_up(amount, total, bound, lean):
    portions = [(1 << 20) // math.isqrt(grade ** lean) + 1 for grade in range(2, amount + 1)]
    rest, holding = total - bound - (amount - 1), [1] * (amount - 1)
    while rest > 0:
        free = [i for i in range(amount - 1) if holding[i] < bound]
        pool, left = sum([portions[i] for i in free]), rest
        for i in free:
            addition = min(bound - holding[i], max(1, left * portions[i] // pool), rest)
            holding[i] = holding[i] + addition
            rest = rest - addition
    return np.array([bound] + holding)


def uneven(own_key, amount, total, reach, slope):
    if amount == 2:
        one = jax.random.randint(own_key, (), max(1, total - reach), min(reach, total - 1) + 1)
        return jnp.stack([one, total - one])
    lengths = jnp.asarray(split_up(amount, total, reach, slope), jnp.int32)
    twos = (amount - 1) // 2
    donor, taker = lengths[1:1 + 2 * twos:2], lengths[2:2 + 2 * twos:2]
    room = jnp.minimum(donor - 1, reach - taker)
    passed = jax.random.randint(jax.random.fold_in(own_key, 1), (twos,), 0, 1 << 20) % (room + 1)
    lengths = lengths.at[1:1 + 2 * twos:2].set(donor - passed).at[2:2 + 2 * twos:2].set(taker + passed)
    return lengths[jax.random.permutation(jax.random.fold_in(own_key, 2), amount)]


def bell_draw(rng, extent, width, limit, pieces=(), kind=jnp.bfloat16):
    array = width * jax.random.normal(rng, extent, jnp.float32)
    if pieces:
        array = array * steps_of(rng, extent, pieces, -0.22, 0.18)
    return jnp.clip(array, -limit, limit).astype(kind)


def setup_inputs(seed: int = 0) -> dict:
    keys = jax.random.split(jax.random.key(seed), 20)
    return {
        "tokens": bell_draw(keys[0], (TOKENS, D), 1.0, 6.0, ((0, 32),)),
        "condition": bell_draw(keys[1], (IMAGES, D), 1.0, 6.0, ((0, 16),)),
        "segment_ids": jax.vmap(lambda own: jnp.searchsorted(jnp.cumsum(uneven(own, SEGS, L, L // 2, 1)), jnp.arange(L), side="right"))(jax.random.split(keys[2], SEQS)).reshape((SEQS, L)).astype(jnp.int32),
        "tile_mask": with_ends((jax.random.randint(keys[3], (SEQS, L // TILE, L // TILE), 0, 2) < 1).astype(jnp.int32), jax.random.fold_in(keys[3], 1), 0, 1),
        "image_index": with_ends(jax.random.randint(keys[4], (SEQS, SEGS), 0, IMG_DEV), jax.random.fold_in(keys[4], 1), 0, IMG_DEV - 1).astype(jnp.int32),
        "w_ada": bell_draw(keys[5], (D, 6 * D), D ** -0.5, 0.1875, ((1, 2),), jnp.float32),
        "b_ada": bell_draw(keys[6], (6 * D,), 0.5, 3.0, ((0, 2),), jnp.float32),
        "w_query": bell_draw(keys[7], (D, D), D ** -0.5, 0.1875, ((0, 16), (1, 2)), jnp.float32),
        "w_key": bell_draw(keys[8], (D, D), D ** -0.5, 0.1875, ((0, 16), (1, 2)), jnp.float32),
        "w_value": bell_draw(keys[9], (D, D), D ** -0.5, 0.1875, ((0, 16), (1, 2)), jnp.float32),
        "b_query": bell_draw(keys[10], (D,), 0.3, 3.0, ((0, 2),), jnp.float32),
        "b_value": bell_draw(keys[11], (D,), 0.3, 3.0, ((0, 2),), jnp.float32),
        "w_out": bell_draw(keys[12], (D, D), (D // 64) ** -0.5, 1.5, ((0, 16), (1, 2)), jnp.float32),
        "b_out": bell_draw(keys[13], (D,), 0.3, 3.0, (), jnp.float32),
        "w_up": bell_draw(keys[14], (D, FF), D ** -0.5, 0.1875, ((0, 16), (1, 2)), jnp.float32),
        "b_up": bell_draw(keys[15], (FF,), 0.3, 3.0, ((0, 2),), jnp.float32),
        "w_down": bell_draw(keys[16], (D, FF), (FF // 4) ** -0.5, 0.1875, ((0, 16), (1, 2)), jnp.float32),
        "b_down": bell_draw(keys[17], (D,), 0.3, 3.0, (), jnp.float32),
        "cotangent": bell_draw(keys[18], (TOKENS, D), 1.0, 6.0, ((0, 32),)),
    }


EPSILON = 1e-06
MASKED_SCORE = -1e+30
PRECISE = lax.Precision.HIGHEST

@jax.custom_vjp
def low(v):
    return lax.optimization_barrier(v.astype(jnp.bfloat16)).astype(jnp.float32)

@jax.custom_vjp
def low_back(v):
    return v

def low_keep(v):
    return (low(v), None)

def low_pass(kept, grad):
    return (grad,)

def back_keep(v):
    return (v, None)

def back_low(kept, grad):
    return (low(grad),)
low.defvjp(low_keep, low_pass)
low_back.defvjp(back_keep, back_low)

def layer_norm(values):
    centred = values - lax.optimization_barrier(jnp.mean(values, axis=-1, keepdims=True))
    inverse = lax.rsqrt(lax.optimization_barrier(jnp.mean(centred * centred, axis=-1, keepdims=True)) + EPSILON)
    return centred * inverse

def reference(tokens, condition, segment_ids, tile_mask, image_index, w_ada, b_ada, w_query, w_key, w_value, b_query, b_value, w_out, b_out, w_up, b_up, w_down, b_down, cotangent):
    scaling = HEAD_DIM ** (-0.5)
    seq_total = segment_ids.shape[0]
    length = segment_ids.shape[1]
    group_of = (jnp.arange(seq_total, dtype=jnp.int32) // SEQ_DEV).astype(jnp.int32)
    global_image = (group_of[:, None] * IMG_DEV + image_index).astype(jnp.int32)
    token_image = jnp.take_along_axis(global_image, segment_ids, axis=1).astype(jnp.int32)
    tile_of = (jnp.arange(length, dtype=jnp.int32) // TILE).astype(jnp.int32)
    on_diagonal = tile_of[:, None] == tile_of[None, :]
    head_shape = (length, ATTN_HEADS, HEAD_DIM)

    def forward(tokens32, cond32, ada_weight, ada_bias, query_weight, key_weight, value_weight, query_bias, value_bias, out_weight, out_bias, up_weight, up_bias, down_weight, down_bias):
        modulation = jnp.dot(jax.nn.silu(cond32), ada_weight, precision=PRECISE) + ada_bias
        query_low = low(query_weight)
        key_low = low(key_weight)
        value_low = low(value_weight)
        out_low = low(out_weight)
        up_low = low(up_weight)
        down_low = low(down_weight)

        def one_row(item):
            seq_tokens, seq_segments, seq_tiles, seq_images = item
            per_token = jnp.take(modulation, seq_images, axis=0)
            shift_one, scale_one, gate_one, shift_two, scale_two, gate_two = jnp.split(per_token, 6, axis=1)
            hidden_one = low(layer_norm(seq_tokens) * (1.0 + scale_one) + shift_one)
            queries = low(low_back(jnp.dot(hidden_one, query_low, precision=PRECISE) + query_bias))
            keys_all = low(low_back(jnp.dot(hidden_one, key_low, precision=PRECISE)))
            values_all = low(low_back(jnp.dot(hidden_one, value_low, precision=PRECISE) + value_bias))
            raw = jnp.einsum('qhd,khd->hqk', queries.reshape(head_shape), keys_all.reshape(head_shape), precision=PRECISE)
            scores = low_back(raw * scaling)
            tile_ok = seq_tiles[tile_of][:, tile_of] > 0
            allowed = (seq_segments[:, None] == seq_segments[None, :]) & (tile_ok | on_diagonal)
            scores = jnp.where(allowed[None], scores, MASKED_SCORE)
            shifted = jnp.exp(scores - lax.optimization_barrier(jnp.max(scores, axis=-1, keepdims=True)))
            probs = shifted / lax.optimization_barrier(jnp.sum(shifted, axis=-1, keepdims=True))
            attended = jnp.einsum('hqk,khd->qhd', low(probs), values_all.reshape(head_shape), precision=PRECISE).reshape(length, D)
            attended = low(low_back(attended))
            branch_one = low_back(jnp.dot(attended, out_low.T, precision=PRECISE) + out_bias)
            middle = seq_tokens + gate_one * branch_one
            hidden_two = low(layer_norm(middle) * (1.0 + scale_two) + shift_two)
            pre_act = low_back(jnp.dot(hidden_two, up_low, precision=PRECISE) + up_bias)
            activated = low(jax.nn.gelu(pre_act, approximate=True))
            branch_two = low_back(jnp.dot(activated, down_low.T, precision=PRECISE) + down_bias)
            return middle + gate_two * branch_two
        items = (tokens32.reshape(seq_total, length, D), segment_ids, tile_mask, token_image)
        outputs = lax.map(jax.checkpoint(one_row), items)
        return outputs.reshape(seq_total * length, D)
    params = (tokens.astype(jnp.float32), condition.astype(jnp.float32), w_ada, b_ada, w_query, w_key, w_value, b_query, b_value, w_out, b_out, w_up, b_up, w_down, b_down)
    result, pullback = jax.vjp(forward, *params)
    grads = pullback(cotangent.astype(jnp.float32))
    return (result.astype(jnp.bfloat16), grads[0], grads[1], grads[2], grads[3], grads[4], grads[5], grads[6], grads[7], grads[8], grads[9], grads[10], grads[11], grads[12], grads[13], grads[14])
```

```python
from functools import partial

import jax
import jax.numpy as jnp
from jax import lax
from jax.experimental import pallas as pl
from jax.experimental.pallas import tpu as pltpu
from jax.sharding import PartitionSpec as P

HEAD_DIM = 72
TILE = 128


EPSILON = 1e-06
MASKED_SCORE = -1e30
PRECISE = lax.Precision.HIGHEST


def layer_norm(values):
    centred = values - jnp.mean(values, axis=-1, keepdims=True)
    inverse = lax.rsqrt(jnp.mean(centred * centred, axis=-1, keepdims=True) + EPSILON)
    return (centred * inverse, inverse)


def norm_back(normed, inverse, grad):
    return inverse * (
        grad
        - jnp.mean(grad, axis=-1, keepdims=True)
        - normed * jnp.mean(grad * normed, axis=-1, keepdims=True)
    )


def contract_last(left, right):
    return lax.dot_general(
        left, right, (((1,), (1,)), ((), ())), preferred_element_type=jnp.float32
    )


def contract_first(left, right):
    return lax.dot_general(
        left, right, (((0,), (0,)), ((), ())), preferred_element_type=jnp.float32
    )


def general_body(
    tokens,
    condition,
    segment_ids,
    tile_mask,
    image_index,
    w_ada,
    b_ada,
    w_query,
    w_key,
    w_value,
    b_query,
    b_value,
    w_out,
    b_out,
    w_up,
    b_up,
    w_down,
    b_down,
    cotangent,
):
    scaling = HEAD_DIM ** (-0.5)
    own_rows = tokens.shape[0]
    seq_count = segment_ids.shape[0]
    length = segment_ids.shape[1]
    group_rows = seq_count * length
    own_start = lax.axis_index("heads") * own_rows
    img_count = condition.shape[0]
    slot_count = image_index.shape[1]
    local_heads = w_query.shape[1] // HEAD_DIM
    block_rows = min(512, length)
    tile_count = length // TILE
    bfloat = jnp.bfloat16
    own_segments = lax.dynamic_slice_in_dim(segment_ids.reshape(group_rows), own_start, own_rows)
    own_seqs = (own_start + jnp.arange(own_rows, dtype=jnp.int32)) // length
    seq_match = own_seqs[:, None] == jnp.arange(seq_count, dtype=jnp.int32)[None, :]
    slot_match = own_segments[:, None] == jnp.arange(slot_count, dtype=jnp.int32)[None, :]
    own_image = jnp.sum(
        jnp.where(seq_match[:, :, None] & slot_match[:, None, :], image_index[None, :, :], 0),
        axis=(1, 2),
    )
    image_onehot = (own_image[:, None] == jnp.arange(img_count, dtype=jnp.int32)[None, :]).astype(
        jnp.float32
    )
    cond_full = condition.astype(jnp.float32)
    silu_cond = jax.nn.silu(cond_full)
    mod_cols = jnp.dot(silu_cond, w_ada, precision=PRECISE) + b_ada
    mod_full, up_bias_all = (
        lax.all_gather(mod_cols, "heads", axis=1, tiled=True),
        lax.all_gather(b_up.reshape(1, -1), "heads", axis=1, tiled=True),
    )
    per_token = jnp.dot(image_onehot, mod_full, precision=PRECISE)
    shift_one, scale_one, gate_one, shift_two, scale_two, gate_two = jnp.split(per_token, 6, axis=1)

    def gather_weights():
        return (
            lax.all_gather(w_query.astype(bfloat), "rows", axis=0, tiled=True),
            lax.all_gather(w_key.astype(bfloat), "rows", axis=0, tiled=True),
            lax.all_gather(w_value.astype(bfloat), "rows", axis=0, tiled=True),
            lax.all_gather(w_out.astype(bfloat), "rows", axis=0, tiled=True),
            lax.all_gather(w_up.astype(bfloat), "rows", axis=0, tiled=True),
            lax.all_gather(w_down.astype(bfloat), "rows", axis=0, tiled=True),
        )

    def spread_first(values):
        return lax.all_gather(values, "heads", axis=0, tiled=True)

    query_full, key_full, value_full, out_full, up_full, down_full = gather_weights()
    token_full = tokens.astype(jnp.float32)
    normed_one, inverse_one = layer_norm(token_full)
    hidden_own_one = (normed_one * (1.0 + scale_one) + shift_one).astype(bfloat)
    hidden_one = spread_first(hidden_own_one)
    head_shape = (group_rows, local_heads, HEAD_DIM)
    query_heads = (
        (jnp.dot(hidden_one, query_full, preferred_element_type=jnp.float32) + b_query)
        .astype(bfloat)
        .reshape(head_shape)
    )
    key_heads = (
        jnp.dot(hidden_one, key_full, preferred_element_type=jnp.float32)
        .astype(bfloat)
        .reshape(head_shape)
    )
    value_heads = (
        (jnp.dot(hidden_one, value_full, preferred_element_type=jnp.float32) + b_value)
        .astype(bfloat)
        .reshape(head_shape)
    )
    tile_of = jnp.arange(length, dtype=jnp.int32) // TILE

    def scores_for(seq_index, block_start):
        seq_start = seq_index * length
        block_query = query_heads[seq_start + block_start : seq_start + block_start + block_rows]
        seq_keys = key_heads[seq_start : seq_start + length]
        block_tiles = tile_mask[seq_index][block_start // TILE : (block_start + block_rows) // TILE]
        expanded = jnp.broadcast_to(
            block_tiles[:, None, :, None], (block_rows // TILE, TILE, tile_count, TILE)
        ).reshape(block_rows, length)
        seg_row = segment_ids[seq_index]
        same_image = seg_row[block_start : block_start + block_rows][:, None] == seg_row[None, :]
        diagonal = tile_of[block_start : block_start + block_rows][:, None] == tile_of[None, :]
        allowed = same_image & ((expanded > 0) | diagonal)
        raw = (
            jnp.einsum("qhd,khd->hqk", block_query, seq_keys, preferred_element_type=jnp.float32)
            * scaling
        )
        return (jnp.where(allowed[None], raw, MASKED_SCORE), block_query, seq_keys)

    attended_parts = []
    log_totals = []
    for seq_index in range(seq_count):
        seq_values = value_heads[seq_index * length : (seq_index + 1) * length]
        for block_start in range(0, length, block_rows):
            scores, block_query, seq_keys = scores_for(seq_index, block_start)
            top_score = jnp.max(scores, axis=-1, keepdims=True)
            log_total = top_score + jnp.log(
                jnp.sum(jnp.exp(scores - top_score), axis=-1, keepdims=True)
            )
            probs_low = jnp.exp(scores - log_total).astype(bfloat)
            attended_parts.append(
                jnp.einsum(
                    "hqk,khd->qhd", probs_low, seq_values, preferred_element_type=jnp.float32
                )
            )
            log_totals.append(log_total)
    attended = (
        jnp.concatenate(attended_parts, axis=0)
        .reshape(group_rows, local_heads * HEAD_DIM)
        .astype(bfloat)
    )
    branch_one = (
        lax.psum_scatter(
            contract_last(attended, out_full), "heads", scatter_dimension=0, tiled=True
        )
        + b_out
    )
    middle = token_full + gate_one * branch_one
    normed_two, inverse_two = layer_norm(middle)
    hidden_own_two = (normed_two * (1.0 + scale_two) + shift_two).astype(bfloat)
    up_all, down_all = (
        lax.all_gather(up_full, "heads", axis=1, tiled=True),
        lax.all_gather(down_full, "heads", axis=1, tiled=True),
    )
    pre_act = jnp.dot(hidden_own_two, up_all, preferred_element_type=jnp.float32) + up_bias_all[0]
    activated = jax.nn.gelu(pre_act, approximate=True).astype(bfloat)
    branch_two = contract_last(activated, down_all) + b_down
    output = (middle + gate_two * branch_two).astype(bfloat)
    query_back, key_back, value_back, out_back, up_back, down_back = gather_weights()
    hidden_one_back = spread_first(hidden_own_one)
    grad_out = cotangent.astype(jnp.float32)
    grad_branch_two = (grad_out * gate_two).astype(bfloat)
    grad_gate_two = grad_out * branch_two
    grad_down_all = contract_first(grad_branch_two, activated)
    grad_act = jnp.dot(grad_branch_two, down_all, preferred_element_type=jnp.float32)
    _, gelu_back = jax.vjp(partial(jax.nn.gelu, approximate=True), pre_act)
    grad_pre = gelu_back(grad_act)[0].astype(bfloat)
    grad_up_all = contract_first(hidden_own_two, grad_pre)
    grad_bias_all = jnp.sum(grad_pre, axis=0, dtype=jnp.float32).reshape(1, -1)
    grad_hidden_two = contract_last(grad_pre, up_all)
    grad_w_up, grad_w_down, grad_bias_cols = (
        lax.psum_scatter(grad_up_all, "heads", scatter_dimension=1, tiled=True),
        lax.psum_scatter(grad_down_all, "heads", scatter_dimension=1, tiled=True),
        lax.psum_scatter(grad_bias_all, "heads", scatter_dimension=1, tiled=True),
    )
    grad_b_up = grad_bias_cols[0]
    grad_scale_two = grad_hidden_two * normed_two
    grad_middle = grad_out + norm_back(normed_two, inverse_two, grad_hidden_two * (1.0 + scale_two))
    grad_branch_one = (grad_middle * gate_one).astype(bfloat)
    grad_gate_one = grad_middle * branch_one
    grad_one_full = lax.all_gather(grad_branch_one, "heads", axis=0, tiled=True)
    grad_w_out = contract_first(grad_one_full, attended)
    grad_attended = (
        jnp.dot(grad_one_full, out_back, preferred_element_type=jnp.float32)
        .astype(bfloat)
        .reshape(head_shape)
    )
    grad_query_parts = []
    grad_key_parts = []
    grad_value_parts = []
    block_number = 0
    for seq_index in range(seq_count):
        seq_start = seq_index * length
        seq_values = value_heads[seq_start : seq_start + length]
        key_total = jnp.zeros((length, local_heads, HEAD_DIM), jnp.float32)
        value_total = jnp.zeros((length, local_heads, HEAD_DIM), jnp.float32)
        for block_start in range(0, length, block_rows):
            scores, block_query, seq_keys = scores_for(seq_index, block_start)
            probs = jnp.exp(scores - log_totals[block_number])
            block_number += 1
            grad_block = grad_attended[
                seq_start + block_start : seq_start + block_start + block_rows
            ]
            grad_probs = jnp.einsum(
                "qhd,khd->hqk", grad_block, seq_values, preferred_element_type=jnp.float32
            )
            centre = jnp.sum(probs * grad_probs, axis=-1, keepdims=True)
            grad_scores = (probs * (grad_probs - centre)).astype(bfloat)
            grad_query_parts.append(
                (
                    jnp.einsum(
                        "hqk,khd->qhd", grad_scores, seq_keys, preferred_element_type=jnp.float32
                    )
                    * scaling
                ).astype(bfloat)
            )
            key_total = (
                key_total
                + jnp.einsum(
                    "hqk,qhd->khd", grad_scores, block_query, preferred_element_type=jnp.float32
                )
                * scaling
            )
            value_total = value_total + jnp.einsum(
                "hqk,qhd->khd", probs.astype(bfloat), grad_block, preferred_element_type=jnp.float32
            )
        grad_key_parts.append(key_total.astype(bfloat))
        grad_value_parts.append(value_total.astype(bfloat))
    flat_shape = (group_rows, local_heads * HEAD_DIM)
    grad_queries = jnp.concatenate(grad_query_parts, axis=0).reshape(flat_shape)
    grad_keys = jnp.concatenate(grad_key_parts, axis=0).reshape(flat_shape)
    grad_values = jnp.concatenate(grad_value_parts, axis=0).reshape(flat_shape)
    grad_w_query = contract_first(hidden_one_back, grad_queries)
    grad_w_key = contract_first(hidden_one_back, grad_keys)
    grad_w_value = contract_first(hidden_one_back, grad_values)
    grad_b_query = jnp.sum(grad_queries, axis=0, dtype=jnp.float32)
    grad_b_value = jnp.sum(grad_values, axis=0, dtype=jnp.float32)
    total = contract_last(grad_queries, query_back)
    total = total + contract_last(grad_keys, key_back)
    grad_hidden_one = lax.psum_scatter(
        total + contract_last(grad_values, value_back), "heads", scatter_dimension=0, tiled=True
    )
    grad_scale_one = grad_hidden_one * normed_one
    grad_tokens = grad_middle + norm_back(
        normed_one, inverse_one, grad_hidden_one * (1.0 + scale_one)
    )
    grad_mod_tokens = jnp.concatenate(
        [
            grad_hidden_one,
            grad_scale_one,
            grad_gate_one,
            grad_hidden_two,
            grad_scale_two,
            grad_gate_two,
        ],
        axis=1,
    )
    grad_mod_images = lax.dot_general(
        image_onehot,
        grad_mod_tokens,
        (((0,), (0,)), ((), ())),
        precision=PRECISE,
        preferred_element_type=jnp.float32,
    )
    bias_parts = jnp.stack(
        [
            jnp.sum(grad_branch_one, axis=0, dtype=jnp.float32),
            jnp.sum(grad_branch_two, axis=0, dtype=jnp.float32),
        ],
        axis=0,
    )
    grad_mod_cols, bias_cols = (
        lax.psum_scatter(grad_mod_images, "heads", scatter_dimension=1, tiled=True),
        lax.psum_scatter(bias_parts, "heads", scatter_dimension=1, tiled=True),
    )
    grad_w_ada = lax.dot_general(
        silu_cond,
        grad_mod_cols,
        (((0,), (0,)), ((), ())),
        precision=PRECISE,
        preferred_element_type=jnp.float32,
    )
    grad_b_ada = jnp.sum(grad_mod_cols, axis=0)
    grad_silu = lax.dot_general(
        grad_mod_cols,
        w_ada,
        (((1,), (1,)), ((), ())),
        precision=PRECISE,
        preferred_element_type=jnp.float32,
    )
    grad_silu = lax.psum(grad_silu, "heads")
    _, silu_back = jax.vjp(jax.nn.silu, cond_full)
    grad_condition = silu_back(grad_silu)[0]
    grad_w_ada, grad_b_ada, grad_b_query, grad_b_value, grad_b_up, bias_cols = lax.psum(
        (grad_w_ada, grad_b_ada, grad_b_query, grad_b_value, grad_b_up, bias_cols), "rows"
    )
    grad_w_query, grad_w_key, grad_w_value, grad_w_out, grad_w_up, grad_w_down = (
        lax.psum_scatter(grad_w_query, "rows", scatter_dimension=0, tiled=True),
        lax.psum_scatter(grad_w_key, "rows", scatter_dimension=0, tiled=True),
        lax.psum_scatter(grad_w_value, "rows", scatter_dimension=0, tiled=True),
        lax.psum_scatter(grad_w_out, "rows", scatter_dimension=0, tiled=True),
        lax.psum_scatter(grad_w_up, "rows", scatter_dimension=0, tiled=True),
        lax.psum_scatter(grad_w_down, "rows", scatter_dimension=0, tiled=True),
    )
    return (
        output,
        grad_tokens,
        grad_condition,
        grad_w_ada,
        grad_b_ada,
        grad_w_query,
        grad_w_key,
        grad_w_value,
        grad_b_query,
        grad_b_value,
        grad_w_out,
        bias_cols[0],
        grad_w_up,
        grad_b_up,
        grad_w_down,
        bias_cols[1],
    )


LOG2E = 1.4426950408889634
GELU_SLOPE = 0.7978845608028654
GELU_CUBE = 0.044715
BF = jnp.bfloat16
F32 = jnp.float32
MIB = 2**20


def rows_by_columns(left, right):
    return jnp.dot(left, right, preferred_element_type=F32)


def shape(dims, dtype):
    return jax.ShapeDtypeStruct(dims, dtype)


def params(mib=56):
    return pltpu.CompilerParams(vmem_limit_bytes=mib * MIB)


def cost(flops, bytes_accessed, transcendentals=0):
    return pl.CostEstimate(
        flops=int(flops), bytes_accessed=int(bytes_accessed), transcendentals=int(transcendentals)
    )


def three_parts(values):
    high = lax.reduce_precision(values, 8, 7)
    rest = values - high
    middle = lax.reduce_precision(rest, 8, 7)
    return jnp.concatenate([high, middle, rest - middle], axis=-2).astype(BF)


def norm_kernel(side, tok_ref, hot_ref, parts_ref, perm_ref, h_ref, ht_ref):
    width = tok_ref.shape[1]
    normed, _ = layer_norm(tok_ref[...].astype(F32))
    mod = rows_by_columns(hot_ref[...], parts_ref[0, :, : 2 * width])
    hidden = (normed * (1.0 + mod[:, width:]) + mod[:, :width]).astype(BF)
    h_ref[...] = hidden
    ht_ref[...] = contract_last(perm_ref[...], hidden).astype(BF)


def first_norm(side, tokens, hot, parts, perm, block):
    rows, width = tokens.shape
    return pl.pallas_call(
        norm_kernel,
        grid_spec=pltpu.PrefetchScalarGridSpec(
            num_scalar_prefetch=1,
            grid=(rows // block,),
            in_specs=[
                pl.BlockSpec((block, width), lambda i, y: ((i + y[0]) % 3, 0)),
                pl.BlockSpec((block, hot.shape[1]), lambda i, y: (i, 0)),
                pl.BlockSpec((1,) + parts.shape[1:], lambda i, y: (0, 0, 0)),
                pl.BlockSpec(perm.shape, lambda i, y: (0, 0)),
            ],
            out_specs=[
                pl.BlockSpec((block, width), lambda i, y: (i, 0)),
                pl.BlockSpec((width, block), lambda i, y: (0, i)),
            ],
        ),
        out_shape=[shape((rows, width), BF), shape((width, rows), BF)],
        compiler_params=params(),
        cost_estimate=cost(2 * rows * width * (width + 512), rows * width * 6),
    )(side, tokens, hot, parts, perm)


def project_kernel(side, h_ref, w_ref, bias_ref, out_ref):
    width = out_ref.shape[2]
    out_ref[0] = (rows_by_columns(h_ref[...], w_ref[0, :, :width]) + bias_ref[0]).astype(BF)


def project(side, hidden, weights, bias, block):
    rows, width = hidden.shape
    cols = bias.shape[2]
    pick = lambda a, y: a + y[0] - 2 * a * y[0]
    return pl.pallas_call(
        project_kernel,
        grid_spec=pltpu.PrefetchScalarGridSpec(
            num_scalar_prefetch=1,
            grid=(2, rows // block),
            in_specs=[
                pl.BlockSpec((block, width), lambda a, i, y: (i, 0)),
                pl.BlockSpec((1,) + weights.shape[1:], lambda a, i, y: (pick(a, y), 0, 0)),
                pl.BlockSpec((1, 1, cols), lambda a, i, y: (pick(a, y), 0, 0)),
            ],
            out_specs=pl.BlockSpec((1, block, cols), lambda a, i, y: (a, i, 0)),
        ),
        out_shape=shape((2, rows, cols), BF),
        compiler_params=params(),
        cost_estimate=cost(4 * rows * width * cols, 4 * rows * cols + 4 * width * cols),
    )(side, hidden, weights, bias)


def attend_kernel(heads, block, q_ref, kv_ref, code_ref, seg_ref, o_ref, keys, values, bias):
    i = pl.program_id(1)
    width = heads * HEAD_DIM

    @pl.when(i == 0)
    def _():
        for h in range(heads):
            at = h * HEAD_DIM
            keys[h] = kv_ref[0, :, width + at : width + at + HEAD_DIM]
            values[h] = kv_ref[0, :, 2 * width + at : 2 * width + at + HEAD_DIM]

    for t in range(block // TILE):
        code = code_ref[pl.ds(i * (block // TILE) + t, 1), :]
        seg = seg_ref[pl.ds(i * block + t * TILE, TILE), :]
        bias[t * TILE : (t + 1) * TILE, :] = jnp.where(code == seg, 0.0, MASKED_SCORE)
    parts = []
    for h in range(heads):
        query = q_ref[0, :, h * HEAD_DIM : (h + 1) * HEAD_DIM]
        scores = contract_last(query, keys[h]) * (HEAD_DIM**-0.5 * LOG2E) + bias[...]
        powers = jnp.exp2(scores - jnp.max(scores, axis=1, keepdims=True))
        probs = powers * (1.0 / jnp.sum(powers, axis=1, keepdims=True))
        parts.append(rows_by_columns(probs.astype(BF), values[h]).astype(BF))
    o_ref[0] = jnp.concatenate(parts, axis=1)


def attend(qkv, code, seg, block):
    groups, _, cols = qkv.shape
    length = code.shape[1]
    heads = cols // (3 * HEAD_DIM)
    width = heads * HEAD_DIM
    return pl.pallas_call(
        partial(attend_kernel, heads, block),
        grid=(groups, length // block),
        in_specs=[
            pl.BlockSpec((1, block, cols), lambda a, i: (a, i, 0)),
            pl.BlockSpec((1, length, cols), lambda a, i: (a, 0, 0)),
            pl.BlockSpec(code.shape, lambda a, i: (0, 0)),
            pl.BlockSpec(seg.shape, lambda a, i: (0, 0)),
        ],
        out_specs=pl.BlockSpec((1, block, width), lambda a, i: (a, i, 0)),
        out_shape=shape((groups, length, width), BF),
        scratch_shapes=[
            pltpu.VMEM((heads, length, HEAD_DIM), BF),
            pltpu.VMEM((heads, length, HEAD_DIM), BF),
            pltpu.VMEM((block, length), F32),
        ],
        compiler_params=params(),
        cost_estimate=cost(
            groups * 16 * length * length * width,
            groups * length * cols * 4,
            groups * heads * length * length,
        ),
    )(qkv, qkv, code, seg)


def attend_back_kernel(
    heads, block, qkv_ref, do_ref, code_ref, seg_ref, out_ref, keys, values, turned, dk, dv, bias
):
    i = pl.program_id(1)
    width = heads * HEAD_DIM
    scaling = HEAD_DIM**-0.5

    @pl.when(i == 0)
    def _():
        for h in range(heads):
            at = h * HEAD_DIM
            key = qkv_ref[0, :, width + at : width + at + HEAD_DIM]
            keys[h] = key
            turned[h] = key.astype(F32).T.astype(BF)
            values[h] = qkv_ref[0, :, 2 * width + at : 2 * width + at + HEAD_DIM]
        dk[...] = jnp.zeros_like(dk)
        dv[...] = jnp.zeros_like(dv)

    for t in range(block // TILE):
        tile = i * (block // TILE) + t
        seg = seg_ref[pl.ds(tile, 1), :]
        code = code_ref[pl.ds(tile, 1)].reshape(code_ref.shape[1:])
        bias[:, t * TILE : (t + 1) * TILE] = jnp.where(code == seg, 0.0, MASKED_SCORE)
    rows = pl.ds(pl.multiple_of(i * block, block), block)
    parts = []
    for h in range(heads):
        query = qkv_ref[0, rows, h * HEAD_DIM : (h + 1) * HEAD_DIM]
        grad = do_ref[0, rows, h * HEAD_DIM : (h + 1) * HEAD_DIM]
        scores = contract_last(keys[h], query) * (scaling * LOG2E) + bias[...]
        powers = jnp.exp2(scores - jnp.max(scores, axis=0, keepdims=True))
        probs = powers * (1.0 / jnp.sum(powers, axis=0, keepdims=True))
        grad_probs = contract_last(values[h], grad)
        centre = jnp.sum(probs * grad_probs, axis=0, keepdims=True)
        grad_scores = (probs * (grad_probs - centre)).astype(BF)
        dv[h] += rows_by_columns(probs.astype(BF), grad)
        dk[h] += rows_by_columns(grad_scores, query)
        parts.append((rows_by_columns(turned[h], grad_scores) * scaling).T.astype(BF))
    out_ref[0, rows, :width] = jnp.concatenate(parts, axis=1)

    @pl.when(i == pl.num_programs(1) - 1)
    def _():
        out_ref[0, :, width:] = jnp.concatenate(
            [(dk[h] * scaling).astype(BF) for h in range(heads)]
            + [dv[h].astype(BF) for h in range(heads)],
            axis=1,
        )


def attend_back(qkv, grad, code, seg, block):
    groups, _, cols = qkv.shape
    length = code.shape[1]
    heads = cols // (3 * HEAD_DIM)
    width = heads * HEAD_DIM
    return pl.pallas_call(
        partial(attend_back_kernel, heads, block),
        grid=(groups, length // block),
        in_specs=[
            pl.BlockSpec((1, length, cols), lambda a, i: (a, 0, 0)),
            pl.BlockSpec((1, length, width), lambda a, i: (a, 0, 0)),
            pl.BlockSpec(code.shape, lambda a, i: (0, 0, 0)),
            pl.BlockSpec(seg.shape, lambda a, i: (0, 0)),
        ],
        out_specs=pl.BlockSpec((1, length, cols), lambda a, i: (a, 0, 0)),
        out_shape=shape((groups, length, cols), BF),
        scratch_shapes=[
            pltpu.VMEM((heads, length, HEAD_DIM), BF),
            pltpu.VMEM((heads, length, HEAD_DIM), BF),
            pltpu.VMEM((heads, HEAD_DIM, length), BF),
            pltpu.VMEM((heads, length, HEAD_DIM), F32),
            pltpu.VMEM((heads, length, HEAD_DIM), F32),
            pltpu.VMEM((length, block), F32),
        ],
        compiler_params=params(58),
        cost_estimate=cost(
            groups * 32 * length * length * width,
            groups * length * cols * 8,
            groups * heads * length * length,
        ),
    )(qkv, grad, code, seg)


def middle_kernel(
    side, tok_ref, dy_ref, full_ref, half_ref, w_own, w_other, b_ref, hot_ref, parts_ref, perm_ref,
    branch_ref, h_ref, g_ref, ht_ref, gt_ref, gb_ref,
):
    i = pl.program_id(0)
    width = tok_ref.shape[1]
    att = jnp.where(i < 2, full_ref[...], half_ref[...])
    branch = contract_last(att[0], w_own[0]) + contract_last(att[1], w_other[0]) + b_ref[...]
    branch_ref[...] = branch
    hot = hot_ref[...]
    gate = rows_by_columns(hot, parts_ref[0, :, 2 * width :])
    mod = rows_by_columns(hot, parts_ref[1])
    normed, _ = layer_norm(tok_ref[...].astype(F32) + gate * branch)
    hidden = (normed * (1.0 + mod[:, width : 2 * width]) + mod[:, :width]).astype(BF)
    grad = (dy_ref[...].astype(F32) * mod[:, 2 * width :]).astype(BF)
    h_ref[...] = hidden
    g_ref[...] = grad
    ht_ref[...] = contract_last(perm_ref[...], hidden).astype(BF)
    gt_ref[...] = contract_last(perm_ref[...], grad).astype(BF)
    total = jnp.sum(grad.astype(F32), axis=0, keepdims=True)

    @pl.when(i == 0)
    def _():
        gb_ref[...] = total

    @pl.when(i != 0)
    def _():
        gb_ref[...] += total


def middle_part(side, tokens, cotangent, full, half, w_out, b_out, hot, parts, perm, block):
    rows, width = tokens.shape
    cols = full.shape[2]
    spec = lambda dims: pl.BlockSpec(dims, lambda i, y: (0,) * len(dims))
    placed = pl.BlockSpec((block, width), lambda i, y: ((i + y[0]) % 3, 0))
    plain = pl.BlockSpec((block, width), lambda i, y: (i, 0))
    turned = pl.BlockSpec((width, block), lambda i, y: (0, i))
    return pl.pallas_call(
        middle_kernel,
        grid_spec=pltpu.PrefetchScalarGridSpec(
            num_scalar_prefetch=1,
            grid=(rows // block,),
            in_specs=[
                placed,
                placed,
                pl.BlockSpec((2, block, cols), lambda i, y: (0, jnp.minimum(i, 1), 0)),
                spec((2, block, cols)),
                pl.BlockSpec((1, width, cols), lambda i, y: (y[0], 0, 0)),
                pl.BlockSpec((1, width, cols), lambda i, y: (1 - y[0], 0, 0)),
                spec((1, width)),
                pl.BlockSpec((block, hot.shape[1]), lambda i, y: (i, 0)),
                spec(parts.shape),
                spec(perm.shape),
            ],
            out_specs=[plain, plain, plain, turned, turned, spec((1, width))],
        ),
        out_shape=[
            shape((rows, width), F32),
            shape((rows, width), BF),
            shape((rows, width), BF),
            shape((width, rows), BF),
            shape((width, rows), BF),
            shape((1, width), F32),
        ],
        compiler_params=params(),
        cost_estimate=cost(2 * rows * width * (3 * width + 1024), rows * width * 22),
    )(side, tokens, cotangent, full, half, w_out, w_out, b_out, hot, parts, perm)


def feed_kernel(
    chunk, pick, h_ref, g_ref, ht_ref, gt_ref, up_ref, down_ref, bias_ref,
    branch_ref, back_ref, mine_ref, theirs_ref, gb_ref, act, pre,
):
    j = pl.program_id(0)
    rows = h_ref.shape[0]
    half = ht_ref.shape[0] // 2
    up = up_ref[0]
    down = down_ref[0]
    total = jnp.zeros(gb_ref.shape, F32)
    for start in range(0, rows, chunk):
        at = slice(start, start + chunk)
        u = rows_by_columns(h_ref[at], up) + bias_ref[0]
        grad = rows_by_columns(g_ref[at], down)
        cube = GELU_CUBE * u * u
        bent = jnp.tanh(GELU_SLOPE * (u + cube * u))
        part = 0.5 * (1.0 + bent)
        slope = part + 0.5 * u * (1.0 - bent * bent) * (GELU_SLOPE * (1.0 + 3.0 * cube))
        low = (u * part).astype(BF)
        back = (grad * slope).astype(BF)
        act[at] = low
        pre[at] = back
        total += jnp.sum(back.astype(F32), axis=0, keepdims=True)
        branch_part = contract_last(low, down)
        back_part = contract_last(back, up)

        @pl.when(j == 0)
        def _():
            branch_ref[at] = branch_part
            back_ref[at] = back_part

        @pl.when(j != 0)
        def _():
            branch_ref[at] += branch_part
            back_ref[at] += back_part

    gb_ref[...] = total
    mine_ref[0] = rows_by_columns(ht_ref[:half], pre[...])
    theirs_ref[0] = rows_by_columns(ht_ref[half:], pre[...]).astype(BF)
    mine_ref[1] = rows_by_columns(gt_ref[:half], act[...])
    theirs_ref[1] = rows_by_columns(gt_ref[half:], act[...]).astype(BF)


def feed(pick, hidden, grad, hidden_turned, grad_turned, up, down, bias, chunk, cols):
    rows, width = hidden.shape
    units = up.shape[2]
    half = width // 2
    whole = lambda dims: pl.BlockSpec(dims, lambda j, y: (0, 0), pipeline_mode=pl.Buffered(1))
    columns = pl.BlockSpec((1, width, cols), lambda j, y: (y[0], 0, j))
    return pl.pallas_call(
        partial(feed_kernel, chunk),
        grid_spec=pltpu.PrefetchScalarGridSpec(
            num_scalar_prefetch=1,
            grid=(units // cols,),
            in_specs=[
                whole((rows, width)),
                whole((rows, width)),
                whole((width, rows)),
                whole((width, rows)),
                columns,
                columns,
                pl.BlockSpec((1, 1, cols), lambda j, y: (y[0], 0, j)),
            ],
            out_specs=[
                whole((rows, width)),
                whole((rows, width)),
                pl.BlockSpec((2, half, cols), lambda j, y: (0, 0, j)),
                pl.BlockSpec((2, half, cols), lambda j, y: (0, 0, j)),
                pl.BlockSpec((1, cols), lambda j, y: (0, j)),
            ],
            scratch_shapes=[pltpu.VMEM((rows, cols), BF), pltpu.VMEM((rows, cols), BF)],
        ),
        out_shape=[
            shape((rows, width), F32),
            shape((rows, width), F32),
            shape((2, half, units), F32),
            shape((2, half, units), BF),
            shape((1, units), F32),
        ],
        compiler_params=params(60),
        cost_estimate=cost(
            12 * rows * width * units, rows * width * 16 + width * units * 10, rows * units
        ),
    )(pick, hidden, grad, hidden_turned, grad_turned, up, down, bias)


def image_sums(hot_turned, values):
    high = values.astype(BF)
    low = (values - high.astype(F32)).astype(BF)
    return rows_by_columns(hot_turned, high) + rows_by_columns(hot_turned, low)


def add_up(ref, value):
    @pl.when(pl.program_id(0) == 0)
    def _():
        ref[...] = value

    @pl.when(pl.program_id(0) != 0)
    def _():
        ref[...] += value


def back_two_kernel(
    side, tok_ref, dy_ref, branch_ref, two_a, two_b, b_ref, back_a, back_b, w_own, w_other, hot_ref,
    turn_ref, parts_ref, perm_ref, out_ref, middle_ref, gt_ref, att_ref, sums_ref, gb_ref,
):
    width = tok_ref.shape[1]
    hot = hot_ref[...]
    turn = turn_ref[...]
    gate = rows_by_columns(hot, parts_ref[0, :, 2 * width :])
    mod = rows_by_columns(hot, parts_ref[1])
    branch = branch_ref[...]
    middle = tok_ref[...].astype(F32) + gate * branch
    branch_two = two_a[...] + two_b[...] + b_ref[...]
    grad_hidden = back_a[...] + back_b[...]
    dy = dy_ref[...].astype(F32)
    out_ref[...] = (middle + mod[:, 2 * width :] * branch_two).astype(BF)
    normed, inverse = layer_norm(middle)
    grad_middle = dy + norm_back(normed, inverse, grad_hidden * (1.0 + mod[:, width : 2 * width]))
    middle_ref[...] = grad_middle
    grad = (grad_middle * gate).astype(BF)
    gt_ref[...] = contract_last(perm_ref[...], grad).astype(BF)
    att_ref[0] = rows_by_columns(grad, w_own[0]).astype(BF)
    att_ref[1] = rows_by_columns(grad, w_other[0]).astype(BF)
    sums = [
        image_sums(turn, grad_middle * branch),
        image_sums(turn, grad_hidden),
        image_sums(turn, grad_hidden * normed),
        image_sums(turn, dy * branch_two),
    ]
    add_up(sums_ref, jnp.stack(sums, axis=0))
    add_up(gb_ref, jnp.sum(grad.astype(F32), axis=0, keepdims=True))


def back_two(
    side, tokens, cotangent, branch, two_a, two_b, b_down, back_a, back_b, w_out, hot, turn, parts, perm,
    block, images,
):
    rows, width = tokens.shape
    cols = w_out.shape[2]
    per = rows // 3 // block
    spec = lambda dims: pl.BlockSpec(dims, lambda i, y: (0,) * len(dims))
    placed = pl.BlockSpec(
        (block, width), lambda i, y: (((i // per + y[0]) % 3) * per + i % per, 0)
    )
    plain = pl.BlockSpec((block, width), lambda i, y: (i, 0))
    return pl.pallas_call(
        back_two_kernel,
        grid_spec=pltpu.PrefetchScalarGridSpec(
            num_scalar_prefetch=1,
            grid=(rows // block,),
            in_specs=[
                placed,
                placed,
                plain,
                plain,
                plain,
                spec((1, width)),
                plain,
                plain,
                pl.BlockSpec((1, width, cols), lambda i, y: (y[0], 0, 0)),
                pl.BlockSpec((1, width, cols), lambda i, y: (1 - y[0], 0, 0)),
                pl.BlockSpec((block, hot.shape[1]), lambda i, y: (i, 0)),
                pl.BlockSpec((images, block), lambda i, y: (0, i)),
                spec(parts.shape),
                spec(perm.shape),
            ],
            out_specs=[
                placed,
                plain,
                pl.BlockSpec((width, block), lambda i, y: (0, i)),
                pl.BlockSpec((2, block, cols), lambda i, y: (0, i, 0)),
                spec((4, images, width)),
                spec((1, width)),
            ],
        ),
        out_shape=[
            shape((rows, width), BF),
            shape((rows, width), F32),
            shape((width, rows), BF),
            shape((2, rows, cols), BF),
            shape((4, images, width), F32),
            shape((1, width), F32),
        ],
        compiler_params=params(),
        cost_estimate=cost(2 * rows * width * (3 * width + 1024), rows * width * 34),
    )(side, tokens, cotangent, branch, two_a, two_b, b_down, back_a, back_b, w_out, w_out, hot, turn, parts, perm)


def outer_kernel(ht_ref, full_ref, half_ref, mine_ref, theirs_ref, sums_ref):
    length = full_ref.shape[1]
    side = mine_ref.shape[1]
    full = full_ref[0]
    rest = half_ref[0]

    def product(start):
        at = slice(start, start + side)
        return rows_by_columns(ht_ref[at, :length], full) + rows_by_columns(
            ht_ref[at, length:], rest
        )

    mine_ref[0] = product(0)
    theirs_ref[0] = product(side).astype(BF)
    sums_ref[0] = jnp.sum(full.astype(F32), axis=0, keepdims=True) + jnp.sum(
        rest.astype(F32), axis=0, keepdims=True
    )


def outer(turned, full, half):
    width, rows = turned.shape
    _, length, cols = full.shape
    side = width // 2
    block = pl.BlockSpec((1, side, cols), lambda a: (a, 0, 0))
    return pl.pallas_call(
        outer_kernel,
        grid=(2,),
        in_specs=[
            pl.BlockSpec((width, rows), lambda a: (0, 0)),
            pl.BlockSpec((1, length, cols), lambda a: (a, 0, 0)),
            pl.BlockSpec((1, half.shape[1], cols), lambda a: (a, 0, 0)),
        ],
        out_specs=[block, block, pl.BlockSpec((1, 1, cols), lambda a: (a, 0, 0))],
        out_shape=[
            shape((2, side, cols), F32),
            shape((2, side, cols), BF),
            shape((2, 1, cols), F32),
        ],
        compiler_params=params(60),
        cost_estimate=cost(4 * rows * width * cols, rows * width * 2 + rows * cols * 4),
    )(turned, full, half)


def back_one_kernel(
    side, full_ref, half_ref, w_own, w_other, tok_ref, middle_ref, hot_ref, turn_ref, parts_ref,
    out_ref, sums_ref,
):
    i = pl.program_id(0)
    width = tok_ref.shape[1]
    cols = full_ref.shape[2]
    scale = rows_by_columns(hot_ref[...], parts_ref[0, :, width : 2 * width])
    grads = jnp.where(i < 2 * pl.num_programs(0) // 3, full_ref[...], half_ref[...])
    grad_hidden = contract_last(grads[0], w_own[0, :, :cols]) + contract_last(
        grads[1], w_other[0, :, :cols]
    )
    normed, inverse = layer_norm(tok_ref[...].astype(F32))
    out_ref[...] = middle_ref[...] + norm_back(normed, inverse, grad_hidden * (1.0 + scale))
    turn = turn_ref[...]
    sums = [image_sums(turn, grad_hidden), image_sums(turn, grad_hidden * normed)]
    add_up(sums_ref, jnp.stack(sums, axis=0))


def back_one(side, full, half, weights, tokens, middle, hot, turn, parts, block, images):
    rows, width = tokens.shape
    cols = full.shape[2]
    per = rows // 3 // block
    spec = lambda dims: pl.BlockSpec(dims, lambda i, y: (0,) * len(dims))
    once = pl.Buffered(1)
    placed = pl.BlockSpec(
        (block, width), lambda i, y: (((i // per + y[0]) % 3) * per + i % per, 0)
    )
    return pl.pallas_call(
        back_one_kernel,
        grid_spec=pltpu.PrefetchScalarGridSpec(
            num_scalar_prefetch=1,
            grid=(rows // block,),
            in_specs=[
                pl.BlockSpec((2, block, cols), lambda i, y: (0, jnp.minimum(i, 2 * per - 1), 0)),
                pl.BlockSpec((2, block, cols), lambda i, y: (0, jnp.maximum(i - 2 * per, 0), 0)),
                pl.BlockSpec(
                    (1,) + weights.shape[1:], lambda i, y: (y[0], 0, 0), pipeline_mode=once
                ),
                pl.BlockSpec(
                    (1,) + weights.shape[1:], lambda i, y: (1 - y[0], 0, 0), pipeline_mode=once
                ),
                placed,
                pl.BlockSpec((block, width), lambda i, y: (i, 0)),
                pl.BlockSpec((block, hot.shape[1]), lambda i, y: (i, 0)),
                pl.BlockSpec((images, block), lambda i, y: (0, i)),
                spec(parts.shape),
            ],
            out_specs=[placed, spec((2, images, width))],
        ),
        out_shape=[shape((rows, width), F32), shape((2, images, width), F32)],
        compiler_params=params(),
        cost_estimate=cost(4 * rows * width * cols, rows * width * 10 + rows * cols * 4),
    )(side, full, half, weights, weights, tokens, middle, hot, turn, parts)


def fast_body(mesh):
    ring = mesh.shape["rows"]
    both = ("rows", "heads")

    def moves(row_of, other_heads):
        pairs = []
        for r in range(ring):
            for y in range(2):
                pairs.append((2 * r + y, 2 * row_of(r) + (1 - y if other_heads else y)))
        return pairs

    to_core = moves(lambda r: r ^ 1, False)
    to_heads = moves(lambda r: r, True)
    to_x = moves(lambda r: r ^ 2, False)
    to_corner = moves(lambda r: r ^ 2, True)
    levels = ring // 4
    to_level = [moves(lambda r, k=k: (r + 4 * k) % ring, False) for k in range(levels)]

    def send(values, pairs):
        return lax.ppermute(values, both, pairs)

    def body(
        tokens,
        condition,
        segment_ids,
        tile_mask,
        image_index,
        w_ada,
        b_ada,
        w_query,
        w_key,
        w_value,
        b_query,
        b_value,
        w_out,
        b_out,
        w_up,
        b_up,
        w_down,
        b_down,
        cotangent,
    ):
        y = lax.axis_index("heads")
        r = lax.axis_index("rows")
        rows, width = tokens.shape
        length = segment_ids.shape[1]
        third = rows // 3
        images = condition.shape[0]
        side = y.reshape(1)
        units = w_up.shape[1]
        cols = w_query.shape[1]

        attention_shard = jnp.concatenate([w_query, w_key, w_value, w_out], axis=1).astype(BF)
        gather = lambda v: lax.all_gather(v, ("heads", "rows"), axis=0, tiled=True).reshape(
            2, width, v.shape[1]
        )
        attention_weights = gather(attention_shard)
        up = gather(w_up.astype(BF))
        down = gather(w_down.astype(BF))
        all_conditions = lax.all_gather(condition, "rows", axis=0, tiled=True)

        cond = condition.astype(F32)
        mod_cols = jnp.dot(jax.nn.silu(cond), w_ada, precision=PRECISE) + b_ada
        biases = jnp.concatenate([b_up, b_query, b_value])[None]
        spread = lax.all_gather(jnp.concatenate([mod_cols, biases], axis=0)[None], "heads", axis=0, tiled=True)
        parts = three_parts(spread[:, :images])
        up_bias = spread[:, images:, :units]
        qkv_bias = jnp.concatenate(
            [
                spread[:, images:, units : units + cols],
                jnp.zeros((2, 1, cols), F32),
                spread[:, images:, units + cols :],
            ],
            axis=2,
        )

        tile_of = jnp.arange(length, dtype=jnp.int32) // TILE
        tiles = length // TILE

        def pattern(seg, tiles_on):
            on = (tiles_on > 0) | jnp.eye(tiles, dtype=bool)
            code = jnp.where(jnp.repeat(on, TILE, axis=1), seg[None, :], -1)
            return (code, seg[:, None]), (code[:, :, None], seg.reshape(tiles, TILE))

        seg_full = lax.dynamic_index_in_dim(segment_ids, 2 * y, 0, keepdims=False)
        tile_full = lax.dynamic_index_in_dim(tile_mask, 2 * y, 0, keepdims=False)
        seg_half = jnp.where(y == 0, segment_ids[1], jnp.roll(segment_ids[1], -third))
        shift = third // TILE
        tile_half = jnp.where(
            y == 0, tile_mask[1], jnp.roll(tile_mask[1], (-shift, -shift), axis=(0, 1))
        )
        full_on, full_back_on = pattern(seg_full, tile_full)
        half_on, half_back_on = pattern(seg_half, tile_half)

        def image_of(seg, index):
            slots = jnp.arange(index.shape[0], dtype=jnp.int32)
            return jnp.sum(jnp.where(seg[:, None] == slots[None, :], index[None, :], 0), axis=1)

        own_image = jnp.concatenate(
            [
                image_of(seg_full, lax.dynamic_index_in_dim(image_index, 2 * y, 0, keepdims=False)),
                image_of(seg_half[:third], image_index[1]),
            ]
        )
        chosen = jnp.arange(images, dtype=jnp.int32)
        hot = (own_image[:, None] == jnp.tile(chosen, 3)[None, :]).astype(BF)
        turn = (chosen[:, None] == own_image[None, :]).astype(BF)

        order = jnp.arange(ring, dtype=jnp.int32)
        core_of, x_of, level_of = order // (ring // 2), (order // levels) % 2, order % levels
        owner = ((r // 4 + level_of) % levels) * 4 + ((r // 2 % 2) ^ x_of) * 2 + ((r % 2) ^ core_of)
        piece = width // ring
        feature = (owner[:, None] * piece + jnp.arange(piece, dtype=jnp.int32)[None, :]).reshape(-1)
        perm = (feature[:, None] == jnp.arange(width, dtype=jnp.int32)[None, :]).astype(BF)

        hidden_one, hidden_one_turned = first_norm(side, tokens, hot, parts, perm, third)
        qkv = project(side, hidden_one, attention_weights, qkv_bias, third)
        qkv_got = send(qkv[1, 2 * third :], to_heads)
        attended_full = attend(qkv, *full_on, third)
        qkv_shared = jnp.concatenate([qkv[0, 2 * third :], qkv_got], axis=0)[None]
        attended_shared = attend(qkv_shared, *half_on, third)
        attended_got = send(attended_shared[0, third:], to_heads)
        attended_half = jnp.stack([attended_shared[0, :third], attended_got])
        w_out_all = attention_weights[:, :, 3 * cols :]
        branch_one, hidden_two, grad_two, hidden_two_turned, grad_two_turned, grad_b_down = middle_part(
            side, tokens, cotangent, attended_full, attended_half, w_out_all, b_out[None], hot, parts, perm, third
        )

        feed_args = (hidden_two, grad_two, hidden_two_turned, grad_two_turned, up, down, up_bias)
        two_b, back_b, feed_mine_b, feed_theirs_b, grad_b_up_b = feed(1 - side, *feed_args, third, 768)
        two_a, back_a, feed_mine_a, feed_theirs_a, grad_b_up_a = feed(side, *feed_args, third, 768)

        def over_cores(mine, theirs):
            return mine + send(theirs, to_core).astype(F32)

        def over_plane(own_side, other_side):
            count = own_side.shape[-2] // 2
            near, far = own_side[..., :count, :], own_side[..., count:, :].astype(BF)
            over, corner = other_side[..., :count, :].astype(BF), other_side[..., count:, :].astype(BF)
            return (
                near
                + send(far, to_x).astype(F32)
                + send(over, to_heads).astype(F32)
                + send(corner, to_corner).astype(F32)
            )

        def over_levels(values):
            total = values[..., :piece, :]
            for k in range(1, levels):
                part = values[..., k * piece : (k + 1) * piece, :].astype(BF)
                total = total + send(part, to_level[k]).astype(F32)
            return total

        feed_b = over_cores(feed_mine_b, feed_theirs_b)
        feed_a = over_cores(feed_mine_a, feed_theirs_a)
        grad_w_up, grad_w_down = over_levels(over_plane(feed_a, feed_b))

        output, grad_middle, grad_one_turned, grad_attended, sums_two, grad_b_out = back_two(
            side, tokens, cotangent, branch_one, two_a, two_b, b_down[None], back_a, back_b, w_out_all, hot, turn, parts,
            perm, third // 2, images,
        )
        grad_attended_got = send(grad_attended[1, 2 * third :], to_heads)
        out_mine, out_theirs, _ = outer(grad_one_turned, attended_full, attended_half)
        out_sum = over_cores(out_mine, out_theirs)
        grad_w_out = over_levels(over_plane(out_sum[0], out_sum[1]))
        grad_qkv_full = attend_back(qkv, grad_attended, *full_back_on, third)
        shared_grad = jnp.concatenate([grad_attended[0, 2 * third :], grad_attended_got], axis=0)[None]
        grad_qkv_shared = attend_back(qkv_shared, shared_grad, *half_back_on, third)
        grad_qkv_got = send(grad_qkv_shared[0, third:], to_heads)
        grad_qkv_half = jnp.stack([grad_qkv_shared[0, :third], grad_qkv_got])
        qkv_mine, qkv_theirs, grad_qkv_bias = outer(hidden_one_turned, grad_qkv_full, grad_qkv_half)
        qkv_sum = over_cores(qkv_mine, qkv_theirs)
        grad_w_qkv = over_levels(over_plane(qkv_sum[0], qkv_sum[1]))
        grad_tokens, sums_one = back_one(
            side, grad_qkv_full, grad_qkv_half, attention_weights, tokens, grad_middle, hot, turn, parts,
            third // 2, images,
        )

        sums = jnp.concatenate([sums_one, sums_two], axis=0).reshape(2, 3, images, width)
        sums = sums.transpose(0, 2, 1, 3).reshape(2, images, 3 * width)
        grad_b_qkv = grad_qkv_bias[:, 0]
        narrow = jnp.concatenate([grad_b_out, grad_b_down], axis=0).reshape(2, 2, cols)

        def packet(which, up_sum, qkv_sum):
            first = jnp.concatenate([up_sum[0], qkv_sum[:cols], qkv_sum[2 * cols :]])
            second = lax.dynamic_index_in_dim(narrow, which, 1, keepdims=False).reshape(-1)
            second = jnp.concatenate([second, jnp.zeros((3 * width - 2 * cols,), F32)])
            chunk = lax.dynamic_index_in_dim(sums, which, 0, keepdims=False)
            return jnp.concatenate([chunk, first[None], second[None]], axis=0)

        own_packet = packet(y, grad_b_up_a, grad_b_qkv[0]) + send(
            packet(1 - y, grad_b_up_b, grad_b_qkv[1]), to_heads
        )
        packets = lax.all_gather(own_packet[None], "rows", axis=0, tiled=True)
        grad_mod = packets[:, :images].reshape(ring * images, 3 * width)
        bias_sums = jnp.sum(packets[:, images:], axis=0)
        grad_w_ada = lax.dot_general(
            jax.nn.silu(all_conditions.astype(F32)),
            grad_mod,
            (((0,), (0,)), ((), ())),
            precision=PRECISE,
            preferred_element_type=F32,
        )
        grad_b_ada = jnp.sum(grad_mod, axis=0)
        grad_silu = lax.dot_general(
            own_packet[:images],
            w_ada,
            (((1,), (1,)), ((), ())),
            precision=PRECISE,
            preferred_element_type=F32,
        )
        grad_silu = grad_silu + send(grad_silu, to_heads)
        _, silu_back = jax.vjp(jax.nn.silu, cond)
        grad_condition = silu_back(grad_silu)[0]
        return (
            output,
            grad_tokens,
            grad_condition,
            grad_w_ada,
            grad_b_ada,
            grad_w_qkv[:, :cols],
            grad_w_qkv[:, cols : 2 * cols],
            grad_w_qkv[:, 2 * cols :],
            bias_sums[0, units : units + cols],
            bias_sums[0, units + cols :],
            grad_w_out,
            bias_sums[1, :cols],
            grad_w_up,
            bias_sums[0, :units],
            grad_w_down,
            bias_sums[1, cols : 2 * cols],
        )

    return body


def solution(mesh):
    body = fast_body(mesh) if mesh.shape["heads"] == 2 and mesh.shape["rows"] == 16 else general_body
    placed = (
        P(("rows", "heads"), None),
        P("rows", None),
        P("rows", None),
        P("rows", None, None),
        P("rows", None),
        P(None, "heads"),
        P("heads"),
        P("rows", "heads"),
        P("rows", "heads"),
        P("rows", "heads"),
        P("heads"),
        P("heads"),
        P("rows", "heads"),
        P(),
        P("rows", "heads"),
        P("heads"),
        P("rows", "heads"),
        P(),
        P(("rows", "heads"), None),
    )
    return jax.shard_map(
        body,
        mesh=mesh,
        in_specs=placed,
        out_specs=(
            P(("rows", "heads"), None),
            P(("rows", "heads"), None),
            P("rows", None),
            P(None, "heads"),
            P("heads"),
            P("rows", "heads"),
            P("rows", "heads"),
            P("rows", "heads"),
            P("heads"),
            P("heads"),
            P("rows", "heads"),
            P("heads"),
            P("rows", "heads"),
            P("heads"),
            P("rows", "heads"),
            P("heads"),
        ),
        check_vma=False,
    )
```

```python
from functools import partial

import jax
import jax.numpy as jnp
from jax import lax
from jax.experimental import pallas as pl
from jax.experimental.pallas import tpu as pltpu
from jax.sharding import PartitionSpec as P

HEAD_DIM = 72
TILE = 128


EPSILON = 1e-06
MASKED_SCORE = -1e30
PRECISE = lax.Precision.HIGHEST


def layer_norm(values):
    centred = values - jnp.mean(values, axis=-1, keepdims=True)
    inverse = lax.rsqrt(jnp.mean(centred * centred, axis=-1, keepdims=True) + EPSILON)
    return (centred * inverse, inverse)


def norm_back(normed, inverse, grad):
    return inverse * (
        grad
        - jnp.mean(grad, axis=-1, keepdims=True)
        - normed * jnp.mean(grad * normed, axis=-1, keepdims=True)
    )


def contract_last(left, right):
    return lax.dot_general(
        left, right, (((1,), (1,)), ((), ())), preferred_element_type=jnp.float32
    )


def contract_first(left, right):
    return lax.dot_general(
        left, right, (((0,), (0,)), ((), ())), preferred_element_type=jnp.float32
    )


def general_body(
    tokens,
    condition,
    segment_ids,
    tile_mask,
    image_index,
    w_ada,
    b_ada,
    w_query,
    w_key,
    w_value,
    b_query,
    b_value,
    w_out,
    b_out,
    w_up,
    b_up,
    w_down,
    b_down,
    cotangent,
):
    scaling = HEAD_DIM ** (-0.5)
    own_rows = tokens.shape[0]
    seq_count = segment_ids.shape[0]
    length = segment_ids.shape[1]
    group_rows = seq_count * length
    own_start = lax.axis_index("heads") * own_rows
    img_count = condition.shape[0]
    slot_count = image_index.shape[1]
    local_heads = w_query.shape[1] // HEAD_DIM
    block_rows = min(512, length)
    tile_count = length // TILE
    bfloat = jnp.bfloat16
    own_segments = lax.dynamic_slice_in_dim(segment_ids.reshape(group_rows), own_start, own_rows)
    own_seqs = (own_start + jnp.arange(own_rows, dtype=jnp.int32)) // length
    seq_match = own_seqs[:, None] == jnp.arange(seq_count, dtype=jnp.int32)[None, :]
    slot_match = own_segments[:, None] == jnp.arange(slot_count, dtype=jnp.int32)[None, :]
    own_image = jnp.sum(
        jnp.where(seq_match[:, :, None] & slot_match[:, None, :], image_index[None, :, :], 0),
        axis=(1, 2),
    )
    image_onehot = (own_image[:, None] == jnp.arange(img_count, dtype=jnp.int32)[None, :]).astype(
        jnp.float32
    )
    cond_full = condition.astype(jnp.float32)
    silu_cond = jax.nn.silu(cond_full)
    mod_cols = jnp.dot(silu_cond, w_ada, precision=PRECISE) + b_ada
    mod_full, up_bias_all = (
        lax.all_gather(mod_cols, "heads", axis=1, tiled=True),
        lax.all_gather(b_up.reshape(1, -1), "heads", axis=1, tiled=True),
    )
    per_token = jnp.dot(image_onehot, mod_full, precision=PRECISE)
    shift_one, scale_one, gate_one, shift_two, scale_two, gate_two = jnp.split(per_token, 6, axis=1)

    def gather_weights():
        return (
            lax.all_gather(w_query.astype(bfloat), "rows", axis=0, tiled=True),
            lax.all_gather(w_key.astype(bfloat), "rows", axis=0, tiled=True),
            lax.all_gather(w_value.astype(bfloat), "rows", axis=0, tiled=True),
            lax.all_gather(w_out.astype(bfloat), "rows", axis=0, tiled=True),
            lax.all_gather(w_up.astype(bfloat), "rows", axis=0, tiled=True),
            lax.all_gather(w_down.astype(bfloat), "rows", axis=0, tiled=True),
        )

    def spread_first(values):
        return lax.all_gather(values, "heads", axis=0, tiled=True)

    query_full, key_full, value_full, out_full, up_full, down_full = gather_weights()
    token_full = tokens.astype(jnp.float32)
    normed_one, inverse_one = layer_norm(token_full)
    hidden_own_one = (normed_one * (1.0 + scale_one) + shift_one).astype(bfloat)
    hidden_one = spread_first(hidden_own_one)
    head_shape = (group_rows, local_heads, HEAD_DIM)
    query_heads = (
        (jnp.dot(hidden_one, query_full, preferred_element_type=jnp.float32) + b_query)
        .astype(bfloat)
        .reshape(head_shape)
    )
    key_heads = (
        jnp.dot(hidden_one, key_full, preferred_element_type=jnp.float32)
        .astype(bfloat)
        .reshape(head_shape)
    )
    value_heads = (
        (jnp.dot(hidden_one, value_full, preferred_element_type=jnp.float32) + b_value)
        .astype(bfloat)
        .reshape(head_shape)
    )
    tile_of = jnp.arange(length, dtype=jnp.int32) // TILE

    def scores_for(seq_index, block_start):
        seq_start = seq_index * length
        block_query = query_heads[seq_start + block_start : seq_start + block_start + block_rows]
        seq_keys = key_heads[seq_start : seq_start + length]
        block_tiles = tile_mask[seq_index][block_start // TILE : (block_start + block_rows) // TILE]
        expanded = jnp.broadcast_to(
            block_tiles[:, None, :, None], (block_rows // TILE, TILE, tile_count, TILE)
        ).reshape(block_rows, length)
        seg_row = segment_ids[seq_index]
        same_image = seg_row[block_start : block_start + block_rows][:, None] == seg_row[None, :]
        diagonal = tile_of[block_start : block_start + block_rows][:, None] == tile_of[None, :]
        allowed = same_image & ((expanded > 0) | diagonal)
        raw = (
            jnp.einsum("qhd,khd->hqk", block_query, seq_keys, preferred_element_type=jnp.float32)
            * scaling
        )
        return (jnp.where(allowed[None], raw, MASKED_SCORE), block_query, seq_keys)

    attended_parts = []
    log_totals = []
    for seq_index in range(seq_count):
        seq_values = value_heads[seq_index * length : (seq_index + 1) * length]
        for block_start in range(0, length, block_rows):
            scores, block_query, seq_keys = scores_for(seq_index, block_start)
            top_score = jnp.max(scores, axis=-1, keepdims=True)
            log_total = top_score + jnp.log(
                jnp.sum(jnp.exp(scores - top_score), axis=-1, keepdims=True)
            )
            probs_low = jnp.exp(scores - log_total).astype(bfloat)
            attended_parts.append(
                jnp.einsum(
                    "hqk,khd->qhd", probs_low, seq_values, preferred_element_type=jnp.float32
                )
            )
            log_totals.append(log_total)
    attended = (
        jnp.concatenate(attended_parts, axis=0)
        .reshape(group_rows, local_heads * HEAD_DIM)
        .astype(bfloat)
    )
    branch_one = (
        lax.psum_scatter(
            contract_last(attended, out_full), "heads", scatter_dimension=0, tiled=True
        )
        + b_out
    )
    middle = token_full + gate_one * branch_one
    normed_two, inverse_two = layer_norm(middle)
    hidden_own_two = (normed_two * (1.0 + scale_two) + shift_two).astype(bfloat)
    up_all, down_all = (
        lax.all_gather(up_full, "heads", axis=1, tiled=True),
        lax.all_gather(down_full, "heads", axis=1, tiled=True),
    )
    pre_act = jnp.dot(hidden_own_two, up_all, preferred_element_type=jnp.float32) + up_bias_all[0]
    activated = jax.nn.gelu(pre_act, approximate=True).astype(bfloat)
    branch_two = contract_last(activated, down_all) + b_down
    output = (middle + gate_two * branch_two).astype(bfloat)
    query_back, key_back, value_back, out_back, up_back, down_back = gather_weights()
    hidden_one_back = spread_first(hidden_own_one)
    grad_out = cotangent.astype(jnp.float32)
    grad_branch_two = (grad_out * gate_two).astype(bfloat)
    grad_gate_two = grad_out * branch_two
    grad_down_all = contract_first(grad_branch_two, activated)
    grad_act = jnp.dot(grad_branch_two, down_all, preferred_element_type=jnp.float32)
    _, gelu_back = jax.vjp(partial(jax.nn.gelu, approximate=True), pre_act)
    grad_pre = gelu_back(grad_act)[0].astype(bfloat)
    grad_up_all = contract_first(hidden_own_two, grad_pre)
    grad_bias_all = jnp.sum(grad_pre, axis=0, dtype=jnp.float32).reshape(1, -1)
    grad_hidden_two = contract_last(grad_pre, up_all)
    grad_w_up, grad_w_down, grad_bias_cols = (
        lax.psum_scatter(grad_up_all, "heads", scatter_dimension=1, tiled=True),
        lax.psum_scatter(grad_down_all, "heads", scatter_dimension=1, tiled=True),
        lax.psum_scatter(grad_bias_all, "heads", scatter_dimension=1, tiled=True),
    )
    grad_b_up = grad_bias_cols[0]
    grad_scale_two = grad_hidden_two * normed_two
    grad_middle = grad_out + norm_back(normed_two, inverse_two, grad_hidden_two * (1.0 + scale_two))
    grad_branch_one = (grad_middle * gate_one).astype(bfloat)
    grad_gate_one = grad_middle * branch_one
    grad_one_full = lax.all_gather(grad_branch_one, "heads", axis=0, tiled=True)
    grad_w_out = contract_first(grad_one_full, attended)
    grad_attended = (
        jnp.dot(grad_one_full, out_back, preferred_element_type=jnp.float32)
        .astype(bfloat)
        .reshape(head_shape)
    )
    grad_query_parts = []
    grad_key_parts = []
    grad_value_parts = []
    block_number = 0
    for seq_index in range(seq_count):
        seq_start = seq_index * length
        seq_values = value_heads[seq_start : seq_start + length]
        key_total = jnp.zeros((length, local_heads, HEAD_DIM), jnp.float32)
        value_total = jnp.zeros((length, local_heads, HEAD_DIM), jnp.float32)
        for block_start in range(0, length, block_rows):
            scores, block_query, seq_keys = scores_for(seq_index, block_start)
            probs = jnp.exp(scores - log_totals[block_number])
            block_number += 1
            grad_block = grad_attended[
                seq_start + block_start : seq_start + block_start + block_rows
            ]
            grad_probs = jnp.einsum(
                "qhd,khd->hqk", grad_block, seq_values, preferred_element_type=jnp.float32
            )
            centre = jnp.sum(probs * grad_probs, axis=-1, keepdims=True)
            grad_scores = (probs * (grad_probs - centre)).astype(bfloat)
            grad_query_parts.append(
                (
                    jnp.einsum(
                        "hqk,khd->qhd", grad_scores, seq_keys, preferred_element_type=jnp.float32
                    )
                    * scaling
                ).astype(bfloat)
            )
            key_total = (
                key_total
                + jnp.einsum(
                    "hqk,qhd->khd", grad_scores, block_query, preferred_element_type=jnp.float32
                )
                * scaling
            )
            value_total = value_total + jnp.einsum(
                "hqk,qhd->khd", probs.astype(bfloat), grad_block, preferred_element_type=jnp.float32
            )
        grad_key_parts.append(key_total.astype(bfloat))
        grad_value_parts.append(value_total.astype(bfloat))
    flat_shape = (group_rows, local_heads * HEAD_DIM)
    grad_queries = jnp.concatenate(grad_query_parts, axis=0).reshape(flat_shape)
    grad_keys = jnp.concatenate(grad_key_parts, axis=0).reshape(flat_shape)
    grad_values = jnp.concatenate(grad_value_parts, axis=0).reshape(flat_shape)
    grad_w_query = contract_first(hidden_one_back, grad_queries)
    grad_w_key = contract_first(hidden_one_back, grad_keys)
    grad_w_value = contract_first(hidden_one_back, grad_values)
    grad_b_query = jnp.sum(grad_queries, axis=0, dtype=jnp.float32)
    grad_b_value = jnp.sum(grad_values, axis=0, dtype=jnp.float32)
    total = contract_last(grad_queries, query_back)
    total = total + contract_last(grad_keys, key_back)
    grad_hidden_one = lax.psum_scatter(
        total + contract_last(grad_values, value_back), "heads", scatter_dimension=0, tiled=True
    )
    grad_scale_one = grad_hidden_one * normed_one
    grad_tokens = grad_middle + norm_back(
        normed_one, inverse_one, grad_hidden_one * (1.0 + scale_one)
    )
    grad_mod_tokens = jnp.concatenate(
        [
            grad_hidden_one,
            grad_scale_one,
            grad_gate_one,
            grad_hidden_two,
            grad_scale_two,
            grad_gate_two,
        ],
        axis=1,
    )
    grad_mod_images = lax.dot_general(
        image_onehot,
        grad_mod_tokens,
        (((0,), (0,)), ((), ())),
        precision=PRECISE,
        preferred_element_type=jnp.float32,
    )
    bias_parts = jnp.stack(
        [
            jnp.sum(grad_branch_one, axis=0, dtype=jnp.float32),
            jnp.sum(grad_branch_two, axis=0, dtype=jnp.float32),
        ],
        axis=0,
    )
    grad_mod_cols, bias_cols = (
        lax.psum_scatter(grad_mod_images, "heads", scatter_dimension=1, tiled=True),
        lax.psum_scatter(bias_parts, "heads", scatter_dimension=1, tiled=True),
    )
    grad_w_ada = lax.dot_general(
        silu_cond,
        grad_mod_cols,
        (((0,), (0,)), ((), ())),
        precision=PRECISE,
        preferred_element_type=jnp.float32,
    )
    grad_b_ada = jnp.sum(grad_mod_cols, axis=0)
    grad_silu = lax.dot_general(
        grad_mod_cols,
        w_ada,
        (((1,), (1,)), ((), ())),
        precision=PRECISE,
        preferred_element_type=jnp.float32,
    )
    grad_silu = lax.psum(grad_silu, "heads")
    _, silu_back = jax.vjp(jax.nn.silu, cond_full)
    grad_condition = silu_back(grad_silu)[0]
    grad_w_ada, grad_b_ada, grad_b_query, grad_b_value, grad_b_up, bias_cols = lax.psum(
        (grad_w_ada, grad_b_ada, grad_b_query, grad_b_value, grad_b_up, bias_cols), "rows"
    )
    grad_w_query, grad_w_key, grad_w_value, grad_w_out, grad_w_up, grad_w_down = (
        lax.psum_scatter(grad_w_query, "rows", scatter_dimension=0, tiled=True),
        lax.psum_scatter(grad_w_key, "rows", scatter_dimension=0, tiled=True),
        lax.psum_scatter(grad_w_value, "rows", scatter_dimension=0, tiled=True),
        lax.psum_scatter(grad_w_out, "rows", scatter_dimension=0, tiled=True),
        lax.psum_scatter(grad_w_up, "rows", scatter_dimension=0, tiled=True),
        lax.psum_scatter(grad_w_down, "rows", scatter_dimension=0, tiled=True),
    )
    return (
        output,
        grad_tokens,
        grad_condition,
        grad_w_ada,
        grad_b_ada,
        grad_w_query,
        grad_w_key,
        grad_w_value,
        grad_b_query,
        grad_b_value,
        grad_w_out,
        bias_cols[0],
        grad_w_up,
        grad_b_up,
        grad_w_down,
        bias_cols[1],
    )


LOG2E = 1.4426950408889634
GELU_SLOPE = 0.7978845608028654
GELU_CUBE = 0.044715
BF = jnp.bfloat16
F32 = jnp.float32
MIB = 2**20


def rows_by_columns(left, right):
    return jnp.dot(left, right, preferred_element_type=F32)


def shape(dims, dtype):
    return jax.ShapeDtypeStruct(dims, dtype)


def params(mib=56):
    return pltpu.CompilerParams(vmem_limit_bytes=mib * MIB)


def cost(flops, bytes_accessed, transcendentals=0):
    return pl.CostEstimate(
        flops=int(flops), bytes_accessed=int(bytes_accessed), transcendentals=int(transcendentals)
    )


def three_parts(values):
    high = lax.reduce_precision(values, 8, 7)
    rest = values - high
    middle = lax.reduce_precision(rest, 8, 7)
    return jnp.concatenate([high, middle, rest - middle], axis=-2).astype(BF)


def norm_kernel(side, tok_ref, hot_ref, parts_ref, perm_ref, h_ref, half_ref, ht_ref):
    width = tok_ref.shape[1]
    normed, _ = layer_norm(tok_ref[...].astype(F32))
    mod = rows_by_columns(hot_ref[...], parts_ref[0, :, : 2 * width])
    hidden = (normed * (1.0 + mod[:, width:]) + mod[:, :width]).astype(BF)
    ht_ref[...] = contract_last(perm_ref[...], hidden).astype(BF)

    @pl.when(pl.program_id(0) < 2)
    def _():
        h_ref[...] = hidden

    @pl.when(pl.program_id(0) == 2)
    def _():
        half_ref[...] = hidden


def first_norm(side, tokens, hot, parts, perm, block):
    rows, width = tokens.shape
    return pl.pallas_call(
        norm_kernel,
        grid_spec=pltpu.PrefetchScalarGridSpec(
            num_scalar_prefetch=1,
            grid=(rows // block,),
            in_specs=[
                pl.BlockSpec((block, width), lambda i, y: ((i + y[0]) % 3, 0)),
                pl.BlockSpec((block, hot.shape[1]), lambda i, y: (i, 0)),
                pl.BlockSpec((1,) + parts.shape[1:], lambda i, y: (0, 0, 0)),
                pl.BlockSpec(perm.shape, lambda i, y: (0, 0)),
            ],
            out_specs=[
                pl.BlockSpec((block, width), lambda i, y: (jnp.minimum(i, 1), 0)),
                pl.BlockSpec((block, width), lambda i, y: (0, 0)),
                pl.BlockSpec((width, block), lambda i, y: (0, i)),
            ],
        ),
        out_shape=[
            shape((2 * block, width), BF),
            shape((block, width), BF),
            shape((width, rows), BF),
        ],
        compiler_params=params(),
        cost_estimate=cost(2 * rows * width * (width + 512), rows * width * 6),
    )(side, tokens, hot, parts, perm)


def project_kernel(side, full_ref, own_ref, got_ref, w_ref, bias_ref, first, second, own, got):
    block, padded = own.shape[1:]
    cols = bias_ref.shape[2]

    def found(hidden):
        value = (rows_by_columns(hidden, w_ref[0, :, :cols]) + bias_ref[0]).astype(BF)
        return jnp.concatenate([value, jnp.zeros((block, padded - cols), BF)], axis=1)

    first[0] = found(full_ref[:block])
    second[0] = found(full_ref[block:])

    @pl.when(pl.program_id(0) == 0)
    def _():
        own[0] = found(own_ref[...])
        got[0] = found(got_ref[...])


def project(side, full, own, got, weights, bias, padded):
    block, width = own.shape
    pick = lambda a, y: a + y[0] - 2 * a * y[0]
    single = pl.BlockSpec((1, block, padded), lambda a, y: (0, 0, 0))
    pair = pl.BlockSpec((1, block, padded), lambda a, y: (a, 0, 0))
    return pl.pallas_call(
        project_kernel,
        grid_spec=pltpu.PrefetchScalarGridSpec(
            num_scalar_prefetch=1,
            grid=(2,),
            in_specs=[
                pl.BlockSpec((2 * block, width), lambda a, y: (0, 0)),
                pl.BlockSpec((block, width), lambda a, y: (0, 0)),
                pl.BlockSpec((block, width), lambda a, y: (0, 0)),
                pl.BlockSpec((1,) + weights.shape[1:], lambda a, y: (pick(a, y), 0, 0)),
                pl.BlockSpec((1,) + bias.shape[1:], lambda a, y: (pick(a, y), 0, 0)),
            ],
            out_specs=[pair, pair, single, single],
        ),
        out_shape=[shape((2, block, padded), BF)] * 2 + [shape((1, block, padded), BF)] * 2,
        compiler_params=params(60),
        cost_estimate=cost(12 * block * width * padded, 12 * block * padded + 4 * width * padded),
    )(side, full, own, got, weights, bias)


MARKS = 16
DEPTH = 128
LSE_AT = HEAD_DIM + MARKS - 4
STEEP = HEAD_DIM**-0.5 * LOG2E


def split_three(values):
    high = values.astype(BF)
    rest = values - high.astype(F32)
    middle = rest.astype(BF)
    return jnp.concatenate([high, middle, (rest - middle.astype(F32)).astype(BF)], axis=1)


def at_head(h, part, heads):
    start = (part * heads + h) * HEAD_DIM
    return slice(start, start + HEAD_DIM)


def both_halves(first, second, columns):
    return jnp.concatenate([first[0, :, columns], second[0, :, columns]], axis=0)


def padded_columns(parts, width):
    found = jnp.concatenate(parts, axis=1)
    gap = width - found.shape[1]
    return jnp.concatenate([found, jnp.zeros((found.shape[0], gap), found.dtype)], axis=1)


def attend_kernel(
    heads, first, second, qm_ref, km_ref, o_first, o_second, l_first, l_second, keys, values, queries
):
    i = pl.program_id(1)

    @pl.when((i == 0) & (pl.program_id(0) == 0))
    def _():
        keys[...] = jnp.zeros_like(keys)
        queries[...] = jnp.zeros_like(queries)

    @pl.when(i == 0)
    def _():
        for h in range(heads):
            keys[h, :, :HEAD_DIM] = both_halves(first, second, at_head(h, 1, heads))
            keys[h, :, HEAD_DIM : HEAD_DIM + MARKS] = km_ref[...]
            value = both_halves(first, second, at_head(h, 2, heads))
            values[h] = value.astype(F32).T.astype(BF)

    for h in range(heads):
        columns = at_head(h, 0, heads)
        queries[h, :, :HEAD_DIM] = jnp.where(i == 0, first[0, :, columns], second[0, :, columns])
        queries[h, :, HEAD_DIM : HEAD_DIM + MARKS] = qm_ref[...]
    parts = []
    totals = []
    probs = None
    scores = contract_last(keys[0], queries[0])
    for h in range(heads):
        later = contract_last(keys[h + 1], queries[h + 1]) if h + 1 < heads else None
        top = jnp.max(scores, axis=0, keepdims=True)
        powers = jnp.exp2((scores - top) * STEEP)
        total = jnp.sum(powers, axis=0, keepdims=True)
        totals.append(top + jnp.log2(total) * (1.0 / STEEP))
        if h > 0:
            parts.append(rows_by_columns(values[h - 1], probs).T.astype(BF))
        probs = (powers * (1.0 / total)).astype(BF)
        scores = later
    parts.append(rows_by_columns(values[heads - 1], probs).T.astype(BF))
    out = padded_columns(parts, o_first.shape[2])
    log_totals = jnp.concatenate(totals, axis=0)

    @pl.when(i == 0)
    def _():
        o_first[0] = out
        l_first[0] = log_totals

    @pl.when(i == 1)
    def _():
        o_second[0] = out
        l_second[0] = log_totals


def attend(first, second, query_marks, key_marks, out_width):
    groups, half, padded = first.shape
    heads = out_width // HEAD_DIM
    pair = lambda *dims: pl.BlockSpec((1,) + dims, lambda a, i: (a, 0, 0))
    return pl.pallas_call(
        partial(attend_kernel, heads),
        grid=(groups, 2),
        in_specs=[
            pair(half, padded),
            pair(half, padded),
            pl.BlockSpec((half, MARKS), lambda a, i: (i, 0)),
            pl.BlockSpec((2 * half, MARKS), lambda a, i: (0, 0)),
        ],
        out_specs=[pair(half, out_width)] * 2 + [pair(heads, half)] * 2,
        out_shape=[shape((groups, half, out_width), BF)] * 2 + [shape((groups, heads, half), F32)] * 2,
        scratch_shapes=[
            pltpu.VMEM((heads, 2 * half, DEPTH), BF),
            pltpu.VMEM((heads, HEAD_DIM, 2 * half), BF),
            pltpu.VMEM((heads, half, DEPTH), BF),
        ],
        compiler_params=params(),
        cost_estimate=cost(groups * 15e9, groups * half * padded * 6, groups * heads * half * half),
    )(first, second, query_marks, key_marks)


def attend_back_kernel(
    heads, first, second, do_first, do_second, l_first, l_second, qm_ref, km_ref,
    out_first, out_second, keys, values, turned, queries, dk, dv,
):
    i = pl.program_id(1)
    half, padded = first.shape[1:]
    width = heads * HEAD_DIM
    scaling = HEAD_DIM**-0.5

    @pl.when((i == 0) & (pl.program_id(0) == 0))
    def _():
        keys[...] = jnp.zeros_like(keys)
        queries[...] = jnp.zeros_like(queries)

    @pl.when(i == 0)
    def _():
        for h in range(heads):
            key = both_halves(first, second, at_head(h, 1, heads))
            keys[h, :, :HEAD_DIM] = key
            keys[h, :, HEAD_DIM : HEAD_DIM + MARKS] = km_ref[...]
            turned[h] = key.astype(F32).T.astype(BF)
            values[h] = both_halves(first, second, at_head(h, 2, heads))
        dk[...] = jnp.zeros_like(dk)
        dv[...] = jnp.zeros_like(dv)

    log_totals = jnp.where(i == 0, l_first[0], l_second[0]).T
    plain = []
    for h in range(heads):
        columns = at_head(h, 0, heads)
        query = jnp.where(i == 0, first[0, :, columns], second[0, :, columns])
        grad = jnp.where(i == 0, do_first[0, :, columns], do_second[0, :, columns])
        queries[h, :, :HEAD_DIM] = query
        queries[h, :, HEAD_DIM : HEAD_DIM + MARKS] = qm_ref[...]
        queries[h, :, LSE_AT : LSE_AT + 3] = split_three(-log_totals[:, h : h + 1])
        plain.append((query, grad))

    def scores_of(h):
        return contract_last(keys[h], queries[h]), contract_last(values[h], plain[h][1])

    def finish(h, probs, grad_scores):
        query, grad = plain[h]
        dv[h] += rows_by_columns(probs, grad)
        dk[h] += rows_by_columns(grad_scores, query)
        return (rows_by_columns(turned[h], grad_scores) * scaling).T.astype(BF)

    parts = []
    before = None
    scores, grad_probs = scores_of(0)
    for h in range(heads):
        later = scores_of(h + 1) if h + 1 < heads else (None, None)
        probs = jnp.exp2(scores * STEEP)
        centre = jnp.sum(probs * grad_probs, axis=0, keepdims=True)
        grad_scores = (probs * (grad_probs - centre)).astype(BF)
        if before is not None:
            parts.append(finish(h - 1, *before))
        before = (probs.astype(BF), grad_scores)
        scores, grad_probs = later
    parts.append(finish(heads - 1, *before))
    grad_queries = jnp.concatenate(parts, axis=1)

    @pl.when(i == 0)
    def _():
        out_first[0, :, :width] = grad_queries

    @pl.when(i == 1)
    def _():
        out_second[0, :, :width] = grad_queries
        for start, ref in ((0, out_first), (half, out_second)):
            rows = slice(start, start + half)
            ref[0, :, width:] = padded_columns(
                [(dk[h, rows] * scaling).astype(BF) for h in range(heads)]
                + [dv[h, rows].astype(BF) for h in range(heads)],
                padded - width,
            )


def attend_back(first, second, do_first, do_second, l_first, l_second, query_marks, key_marks):
    groups, half, padded = first.shape
    heads = l_first.shape[1]
    out_width = do_first.shape[2]
    pair = lambda *dims: pl.BlockSpec((1,) + dims, lambda a, i: (a, 0, 0))
    return pl.pallas_call(
        partial(attend_back_kernel, heads),
        grid=(groups, 2),
        in_specs=[pair(half, padded)] * 2
        + [pair(half, out_width)] * 2
        + [pair(heads, half)] * 2
        + [
            pl.BlockSpec((half, MARKS), lambda a, i: (i, 0)),
            pl.BlockSpec((2 * half, MARKS), lambda a, i: (0, 0)),
        ],
        out_specs=[pair(half, padded)] * 2,
        out_shape=[shape((groups, half, padded), BF)] * 2,
        scratch_shapes=[
            pltpu.VMEM((heads, 2 * half, DEPTH), BF),
            pltpu.VMEM((heads, 2 * half, HEAD_DIM), BF),
            pltpu.VMEM((heads, HEAD_DIM, 2 * half), BF),
            pltpu.VMEM((heads, half, DEPTH), BF),
            pltpu.VMEM((heads, 2 * half, HEAD_DIM), F32),
            pltpu.VMEM((heads, 2 * half, HEAD_DIM), F32),
        ],
        compiler_params=params(60),
        cost_estimate=cost(groups * 12e9, groups * half * padded * 12, groups * heads * half * half),
    )(first, second, do_first, do_second, l_first, l_second, query_marks, key_marks)


def image_sums(hot_turned, values):
    high = values.astype(BF)
    low = (values - high.astype(F32)).astype(BF)
    return rows_by_columns(hot_turned, high) + rows_by_columns(hot_turned, low)


def add_up(ref, value):
    @pl.when(pl.program_id(0) == 0)
    def _():
        ref[...] = value

    @pl.when(pl.program_id(0) != 0)
    def _():
        ref[...] += value


def third_of(first, second, own, other, i, per):
    half = jnp.stack([own[0], other[0]], axis=0)
    return jnp.where(i < per, first[...], jnp.where(i < 2 * per, second[...], half))


def third_specs(block, columns, per):
    full = lambda low: pl.BlockSpec(
        (2, block, columns), lambda i, y: (0, jnp.clip(i - low * per, 0, per - 1), 0)
    )
    single = pl.BlockSpec((1, block, columns), lambda i, y: (0, jnp.clip(i - 2 * per, 0, per - 1), 0))
    return [full(0), full(1), single, single]


def out_weight_specs(width, columns):
    last = columns // (2 * width // 3) - 1
    return [
        pl.BlockSpec((1, width, 2 * width // 3), lambda i, y: (y[0], 0, last)),
        pl.BlockSpec((1, width, 2 * width // 3), lambda i, y: (1 - y[0], 0, last)),
    ]


def middle_kernel(
    side, tok_ref, dy_ref, first, second, own, other, w_own, w_other, b_ref, hot_ref, parts_ref, perm_ref,
    branch_ref, h_ref, g_ref, ht_ref, gt_ref, gb_ref,
):
    i = pl.program_id(0)
    width = tok_ref.shape[1]
    used = width // 2
    att = third_of(first, second, own, other, i, pl.num_programs(0) // 3)[:, :, :used]
    skip = w_own.shape[2] - used
    branch = (
        contract_last(att[0], w_own[0, :, skip:])
        + contract_last(att[1], w_other[0, :, skip:])
        + b_ref[...]
    )
    branch_ref[...] = branch
    hot = hot_ref[...]
    gate = rows_by_columns(hot, parts_ref[0, :, 2 * width :])
    mod = rows_by_columns(hot, parts_ref[1])
    normed, _ = layer_norm(tok_ref[...].astype(F32) + gate * branch)
    hidden = (normed * (1.0 + mod[:, width : 2 * width]) + mod[:, :width]).astype(BF)
    grad = (dy_ref[...].astype(F32) * mod[:, 2 * width :]).astype(BF)
    h_ref[...] = hidden
    g_ref[...] = grad
    ht_ref[...] = contract_last(perm_ref[...], hidden).astype(BF)
    gt_ref[...] = contract_last(perm_ref[...], grad).astype(BF)
    add_up(gb_ref, jnp.sum(grad.astype(F32), axis=0, keepdims=True))


def middle_part(side, tokens, cotangent, thirds, weights, b_out, hot, parts, perm, block):
    rows, width = tokens.shape
    per = rows // 3 // block
    spec = lambda dims: pl.BlockSpec(dims, lambda i, y: (0,) * len(dims))
    placed = pl.BlockSpec(
        (block, width), lambda i, y: (((i // per + y[0]) % 3) * per + i % per, 0)
    )
    plain = pl.BlockSpec((block, width), lambda i, y: (i, 0))
    turned = pl.BlockSpec((width, block), lambda i, y: (0, i))
    return pl.pallas_call(
        middle_kernel,
        grid_spec=pltpu.PrefetchScalarGridSpec(
            num_scalar_prefetch=1,
            grid=(rows // block,),
            in_specs=[
                placed,
                placed,
                *third_specs(block, thirds[0].shape[2], per),
                *out_weight_specs(width, weights.shape[2]),
                spec((1, width)),
                pl.BlockSpec((block, hot.shape[1]), lambda i, y: (i, 0)),
                spec(parts.shape),
                spec(perm.shape),
            ],
            out_specs=[plain, plain, plain, turned, turned, spec((1, width))],
        ),
        out_shape=[
            shape((rows, width), F32),
            shape((rows, width), BF),
            shape((rows, width), BF),
            shape((width, rows), BF),
            shape((width, rows), BF),
            shape((1, width), F32),
        ],
        compiler_params=params(),
        cost_estimate=cost(2 * rows * width * (3 * width + 1024), rows * width * 22),
    )(side, tokens, cotangent, *thirds, weights, weights, b_out, hot, parts, perm)


def feed_kernel(
    chunk, pick, h_ref, g_ref, ht_ref, gt_ref, up_ref, down_ref, bias_ref,
    branch_ref, back_ref, mine_ref, near_ref, far_ref, gb_ref, act, pre,
):
    j = pl.program_id(0)
    rows = h_ref.shape[0]
    half = ht_ref.shape[0] // 2
    up = up_ref[0, 0]
    down = down_ref[0, 0]
    total = jnp.zeros(gb_ref.shape, F32)
    for start in range(0, rows, chunk):
        at = slice(start, start + chunk)
        u = rows_by_columns(h_ref[at], up) + bias_ref[0]
        grad = rows_by_columns(g_ref[at], down)
        cube = GELU_CUBE * u * u
        bent = jnp.tanh(GELU_SLOPE * (u + cube * u))
        part = 0.5 * (1.0 + bent)
        slope = part + 0.5 * u * (1.0 - bent * bent) * (GELU_SLOPE * (1.0 + 3.0 * cube))
        low = (u * part).astype(BF)
        back = (grad * slope).astype(BF)
        act[at] = low
        pre[at] = back
        total += jnp.sum(back.astype(F32), axis=0, keepdims=True)
        branch_part = contract_last(low, down)
        back_part = contract_last(back, up)

        @pl.when(j == 0)
        def _():
            branch_ref[at] = branch_part
            back_ref[at] = back_part

        @pl.when(j != 0)
        def _():
            branch_ref[at] += branch_part
            back_ref[at] += back_part

    gb_ref[...] = total
    quarter = half // 2
    for k, (turned, value) in enumerate(((ht_ref, pre), (gt_ref, act))):
        theirs = rows_by_columns(turned[half:], value[...]).astype(BF)
        near_ref[k] = theirs[:quarter]
        far_ref[k] = theirs[quarter:]
        mine_ref[k] = rows_by_columns(turned[:half], value[...])


def feed(pick, hidden, grad, hidden_turned, grad_turned, weights, bias, chunk, cols):
    rows, width = hidden.shape
    units = weights.shape[3]
    half = width // 2
    whole = lambda dims: pl.BlockSpec(dims, lambda j, y: (0, 0), pipeline_mode=pl.Buffered(1))
    columns = lambda k: pl.BlockSpec((1, 1, width, cols), lambda j, y: (k, y[0], 0, j))
    return pl.pallas_call(
        partial(feed_kernel, chunk),
        grid_spec=pltpu.PrefetchScalarGridSpec(
            num_scalar_prefetch=1,
            grid=(units // cols,),
            in_specs=[
                whole((rows, width)),
                whole((rows, width)),
                whole((width, rows)),
                whole((width, rows)),
                columns(0),
                columns(1),
                pl.BlockSpec((1, 1, cols), lambda j, y: (y[0], 0, j)),
            ],
            out_specs=[
                whole((rows, width)),
                whole((rows, width)),
                pl.BlockSpec((2, half, cols), lambda j, y: (0, 0, j)),
                pl.BlockSpec((2, half // 2, cols), lambda j, y: (0, 0, j)),
                pl.BlockSpec((2, half // 2, cols), lambda j, y: (0, 0, j)),
                pl.BlockSpec((1, cols), lambda j, y: (0, j)),
            ],
            scratch_shapes=[pltpu.VMEM((rows, cols), BF), pltpu.VMEM((rows, cols), BF)],
        ),
        out_shape=[
            shape((rows, width), F32),
            shape((rows, width), F32),
            shape((2, half, units), F32),
            shape((2, half // 2, units), BF),
            shape((2, half // 2, units), BF),
            shape((1, units), F32),
        ],
        compiler_params=params(60),
        cost_estimate=cost(
            12 * rows * width * units, rows * width * 16 + width * units * 10, rows * units
        ),
    )(pick, hidden, grad, hidden_turned, grad_turned, weights, weights, bias)


def back_two_kernel(
    side, tok_ref, dy_ref, branch_ref, two_a, two_b, b_ref, back_a, back_b, w_own, w_other, hot_ref,
    turn_ref, parts_ref, perm_ref, first, second, half_own, half_other, out_ref, middle_ref, a_first, a_second,
    a_own, a_other, sums_ref, gb_ref, mine_ref, theirs_ref, outer_ref,
):
    width = tok_ref.shape[1]
    hot = hot_ref[...]
    turn = turn_ref[...]
    gate = rows_by_columns(hot, parts_ref[0, :, 2 * width :])
    mod = rows_by_columns(hot, parts_ref[1])
    branch = branch_ref[...]
    middle = tok_ref[...].astype(F32) + gate * branch
    branch_two = two_a[...] + two_b[...] + b_ref[...]
    grad_hidden = back_a[...] + back_b[...]
    dy = dy_ref[...].astype(F32)
    out_ref[...] = (middle + mod[:, 2 * width :] * branch_two).astype(BF)
    normed, inverse = layer_norm(middle)
    grad_middle = dy + norm_back(normed, inverse, grad_hidden * (1.0 + mod[:, width : 2 * width]))
    middle_ref[...] = grad_middle
    grad = (grad_middle * gate).astype(BF)
    turned = contract_last(perm_ref[...], grad).astype(BF)
    att = third_of(first, second, half_own, half_other, pl.program_id(0), pl.num_programs(0) // 3)
    for k in range(2):
        product = rows_by_columns(turned, att[k])

        @pl.when(pl.program_id(0) == 0)
        def _():
            outer_ref[k] = product

        @pl.when(pl.program_id(0) != 0)
        def _():
            outer_ref[k] += product

    @pl.when(pl.program_id(0) == pl.num_programs(0) - 1)
    def _():
        for k in range(2):
            mine_ref[k] = outer_ref[k, : width // 2]
            theirs_ref[k] = outer_ref[k, width // 2 :].astype(BF)

    skip = w_own.shape[2] - width // 2
    ours = padded_columns([rows_by_columns(grad, w_own[0, :, skip:]).astype(BF)], a_own.shape[2])
    theirs = padded_columns([rows_by_columns(grad, w_other[0, :, skip:]).astype(BF)], a_own.shape[2])
    i = pl.program_id(0)
    per = pl.num_programs(0) // 3
    for k, ref in enumerate((a_first, a_second)):

        @pl.when(i // per == k)
        def _(ref=ref):
            ref[0] = ours
            ref[1] = theirs

    @pl.when(i // per == 2)
    def _():
        a_own[0] = ours
        a_other[0] = theirs

    sums = [
        image_sums(turn, grad_middle * branch),
        image_sums(turn, grad_hidden),
        image_sums(turn, grad_hidden * normed),
        image_sums(turn, dy * branch_two),
    ]
    add_up(sums_ref, jnp.stack(sums, axis=0))
    add_up(gb_ref, jnp.sum(grad.astype(F32), axis=0, keepdims=True))


def back_two(
    side, tokens, cotangent, branch, two_a, two_b, b_down, back_a, back_b, weights, hot, turn, parts, perm,
    attended, block, images, out_width,
):
    rows, width = tokens.shape
    third = rows // 3
    per = rows // 3 // block
    spec = lambda dims: pl.BlockSpec(dims, lambda i, y: (0,) * len(dims))
    placed = pl.BlockSpec(
        (block, width), lambda i, y: (((i // per + y[0]) % 3) * per + i % per, 0)
    )
    plain = pl.BlockSpec((block, width), lambda i, y: (i, 0))
    return pl.pallas_call(
        back_two_kernel,
        grid_spec=pltpu.PrefetchScalarGridSpec(
            num_scalar_prefetch=1,
            grid=(rows // block,),
            in_specs=[
                placed,
                placed,
                plain,
                plain,
                plain,
                spec((1, width)),
                plain,
                plain,
                *out_weight_specs(width, weights.shape[2]),
                pl.BlockSpec((block, hot.shape[1]), lambda i, y: (i, 0)),
                pl.BlockSpec((images, block), lambda i, y: (0, i)),
                spec(parts.shape),
                spec(perm.shape),
                *third_specs(block, out_width, per),
            ],
            out_specs=[
                placed,
                plain,
                *third_specs(block, out_width, per),
                spec((4, images, width)),
                spec((1, width)),
                spec((2, width // 2, out_width)),
                spec((2, width // 2, out_width)),
            ],
            scratch_shapes=[pltpu.VMEM((2, width, out_width), F32)],
        ),
        out_shape=[
            shape((rows, width), BF),
            shape((rows, width), F32),
            *[shape((2, third, out_width), BF)] * 2,
            *[shape((1, third, out_width), BF)] * 2,
            shape((4, images, width), F32),
            shape((1, width), F32),
            shape((2, width // 2, out_width), F32),
            shape((2, width // 2, out_width), BF),
        ],
        compiler_params=params(62),
        cost_estimate=cost(2 * rows * width * (4 * width + 1024), rows * width * 34),
    )(side, tokens, cotangent, branch, two_a, two_b, b_down, back_a, back_b, weights, weights, hot, turn, parts, perm, *attended)


def outer_kernel(ht_ref, first, second, rest, mine_ref, theirs_ref, sums_ref):
    third = first.shape[1]
    grads = (first[0], second[0], rest[0])
    found = sum(
        rows_by_columns(ht_ref[:, k * third : (k + 1) * third], grad)
        for k, grad in enumerate(grads)
    )

    @pl.when(pl.program_id(0) == 0)
    def _():
        theirs_ref[...] = found.astype(BF)
        sums_ref[...] = sum(jnp.sum(grad.astype(F32), axis=0, keepdims=True) for grad in grads)

    @pl.when(pl.program_id(0) == 1)
    def _():
        mine_ref[...] = found


def outer(turned, first, second, rest, group):
    width, rows = turned.shape
    _, third, cols = first.shape
    block = pl.BlockSpec((width // 2, cols), lambda k: (0, 0))
    pair = pl.BlockSpec((1, third, cols), lambda k: (group, 0, 0))
    single = pl.BlockSpec((1, third, cols), lambda k: (0, 0, 0))
    return pl.pallas_call(
        outer_kernel,
        grid=(2,),
        in_specs=[pl.BlockSpec((width // 2, rows), lambda k: (1 - k, 0)), pair, pair, single],
        out_specs=[block, block, pl.BlockSpec((1, cols), lambda k: (0, 0))],
        out_shape=[shape((width // 2, cols), F32), shape((width // 2, cols), BF), shape((1, cols), F32)],
        compiler_params=params(60),
        cost_estimate=cost(2 * rows * width * cols, rows * width * 2 + rows * cols * 4),
    )(turned, first, second, rest)


def back_one_kernel(
    side, first, second, own, other, w_own, w_other, tok_ref, middle_ref, hot_ref, turn_ref, parts_ref,
    out_ref, sums_ref,
):
    width = tok_ref.shape[1]
    cols = 3 * width // 2
    scale = rows_by_columns(hot_ref[...], parts_ref[0, :, width : 2 * width])
    grads = third_of(first, second, own, other, pl.program_id(0), pl.num_programs(0) // 3)[:, :, :cols]
    grad_hidden = contract_last(grads[0], w_own[0, :, :cols]) + contract_last(
        grads[1], w_other[0, :, :cols]
    )
    normed, inverse = layer_norm(tok_ref[...].astype(F32))
    out_ref[...] = middle_ref[...] + norm_back(normed, inverse, grad_hidden * (1.0 + scale))
    turn = turn_ref[...]
    sums = [image_sums(turn, grad_hidden), image_sums(turn, grad_hidden * normed)]
    add_up(sums_ref, jnp.stack(sums, axis=0))


def back_one(side, thirds, weights, tokens, middle, hot, turn, parts, block, images):
    rows, width = tokens.shape
    cols = thirds[0].shape[2]
    per = rows // 3 // block
    spec = lambda dims: pl.BlockSpec(dims, lambda i, y: (0,) * len(dims))
    once = pl.Buffered(1)
    placed = pl.BlockSpec(
        (block, width), lambda i, y: (((i // per + y[0]) % 3) * per + i % per, 0)
    )
    return pl.pallas_call(
        back_one_kernel,
        grid_spec=pltpu.PrefetchScalarGridSpec(
            num_scalar_prefetch=1,
            grid=(rows // block,),
            in_specs=[
                *third_specs(block, cols, per),
                pl.BlockSpec(
                    (1,) + weights.shape[1:], lambda i, y: (y[0], 0, 0), pipeline_mode=once
                ),
                pl.BlockSpec(
                    (1,) + weights.shape[1:], lambda i, y: (1 - y[0], 0, 0), pipeline_mode=once
                ),
                placed,
                pl.BlockSpec((block, width), lambda i, y: (i, 0)),
                pl.BlockSpec((block, hot.shape[1]), lambda i, y: (i, 0)),
                pl.BlockSpec((images, block), lambda i, y: (0, i)),
                spec(parts.shape),
            ],
            out_specs=[placed, spec((2, images, width))],
        ),
        out_shape=[shape((rows, width), F32), shape((2, images, width), F32)],
        compiler_params=params(),
        cost_estimate=cost(4 * rows * width * cols, rows * width * 10 + rows * cols * 4),
    )(side, *thirds, weights, weights, tokens, middle, hot, turn, parts)


def fast_body(mesh):
    ring = mesh.shape["rows"]
    both = ("rows", "heads")

    def moves(row_of, other_heads):
        pairs = []
        for r in range(ring):
            for y in range(2):
                pairs.append((2 * r + y, 2 * row_of(r) + (1 - y if other_heads else y)))
        return pairs

    to_core = moves(lambda r: r ^ 1, False)
    to_heads = moves(lambda r: r, True)
    to_x = moves(lambda r: r ^ 2, False)
    to_corner = moves(lambda r: r ^ 2, True)
    levels = ring // 4
    to_level = [moves(lambda r, k=k: (r + 4 * k) % ring, False) for k in range(levels)]

    def send(values, pairs):
        return lax.ppermute(values, both, pairs)

    def body(
        tokens,
        condition,
        segment_ids,
        tile_mask,
        image_index,
        w_ada,
        b_ada,
        w_query,
        w_key,
        w_value,
        b_query,
        b_value,
        w_out,
        b_out,
        w_up,
        b_up,
        w_down,
        b_down,
        cotangent,
    ):
        y = lax.axis_index("heads")
        r = lax.axis_index("rows")
        rows, width = tokens.shape
        length = segment_ids.shape[1]
        third = rows // 3
        images = condition.shape[0]
        side = y.reshape(1)
        units = w_up.shape[1]
        cols = w_query.shape[1]

        attention_shard = jnp.concatenate([w_query, w_key, w_value, w_out], axis=1).astype(BF)
        attention_weights = lax.all_gather(
            attention_shard, ("heads", "rows"), axis=0, tiled=True
        ).reshape(2, width, attention_shard.shape[1])
        feed_weights = lax.all_gather(
            jnp.stack([w_up, w_down]).astype(BF), ("heads", "rows"), axis=1, tiled=True
        ).reshape(2, 2, width, units)

        cond = condition.astype(F32)
        mod_cols = jnp.dot(jax.nn.silu(cond), w_ada, precision=PRECISE) + b_ada
        flat = jnp.stack([condition] + [send(condition, to_level[k]) for k in range(1, levels)])
        flat = jnp.concatenate([flat, send(flat, to_x)], axis=0)
        flat = jnp.concatenate([flat, send(flat, to_core)], axis=0)
        silu_all = jax.nn.silu(flat.reshape(ring * images, width).astype(F32))
        biases = jnp.concatenate([b_up, b_query, b_value])[None]
        spread = lax.all_gather(jnp.concatenate([mod_cols, biases], axis=0)[None], "heads", axis=0, tiled=True)
        parts = three_parts(spread[:, :images])
        up_bias = spread[:, images:, :units]
        qkv_bias = jnp.concatenate(
            [
                spread[:, images:, units : units + cols],
                jnp.zeros((2, 1, cols), F32),
                spread[:, images:, units + cols :],
            ],
            axis=2,
        )

        tiles = length // TILE
        tile_of = jnp.arange(length, dtype=jnp.int32) // TILE
        slots = image_index.shape[1]

        def marks_of(seg, tiles_on):
            own_slot = seg[:, None] == jnp.arange(slots, dtype=jnp.int32)[None, :]
            on = (tiles_on > 0) | jnp.eye(tiles, dtype=bool)
            own_tile = tile_of[:, None] == jnp.arange(tiles, dtype=jnp.int32)[None, :]
            open_to = jnp.broadcast_to(on.T[:, None, :], (tiles, TILE, tiles)).reshape(length, tiles)
            ends = jnp.zeros((length, MARKS - slots - tiles), F32)
            query = jnp.concatenate([own_slot, own_tile, ends], axis=1).astype(BF)
            seen = jnp.concatenate([own_slot, open_to], axis=1)
            key = jnp.concatenate([jnp.where(seen, 0.0, MASKED_SCORE), ends + 1.0], axis=1).astype(BF)
            return query, key

        seg_full = lax.dynamic_index_in_dim(segment_ids, 2 * y, 0, keepdims=False)
        tile_full = lax.dynamic_index_in_dim(tile_mask, 2 * y, 0, keepdims=False)
        seg_half = jnp.where(y == 0, segment_ids[1], jnp.roll(segment_ids[1], -third))
        shift = third // TILE
        tile_half = jnp.where(
            y == 0, tile_mask[1], jnp.roll(tile_mask[1], (-shift, -shift), axis=(0, 1))
        )
        marks_full = marks_of(seg_full, tile_full)
        marks_half = marks_of(seg_half, tile_half)

        def image_of(seg, index):
            slot = jnp.arange(slots, dtype=jnp.int32)
            return jnp.sum(jnp.where(seg[:, None] == slot[None, :], index[None, :], 0), axis=1)

        own_image = jnp.concatenate(
            [
                image_of(seg_full, lax.dynamic_index_in_dim(image_index, 2 * y, 0, keepdims=False)),
                image_of(seg_half[:third], image_index[1]),
            ]
        )
        chosen = jnp.arange(images, dtype=jnp.int32)
        hot = (own_image[:, None] == jnp.tile(chosen, 3)[None, :]).astype(BF)
        turn = (chosen[:, None] == own_image[None, :]).astype(BF)

        order = jnp.arange(ring, dtype=jnp.int32)
        core_of, x_of, level_of = order // (ring // 2), (order // levels) % 2, order % levels
        owner = ((r // 4 + level_of) % levels) * 4 + ((r // 2 % 2) ^ x_of) * 2 + ((r % 2) ^ core_of)
        piece = width // ring
        feature = (owner[:, None] * piece + jnp.arange(piece, dtype=jnp.int32)[None, :]).reshape(-1)
        perm = (feature[:, None] == jnp.arange(width, dtype=jnp.int32)[None, :]).astype(BF)

        padded = -(-3 * cols // 128) * 128
        out_width = -(-cols // 128) * 128
        hidden_full, hidden_half, hidden_one_turned = first_norm(side, tokens, hot, parts, perm, third)
        hidden_got = send(hidden_half, to_heads)
        qkv_first, qkv_second, qkv_own, qkv_got = project(
            side, hidden_full, hidden_half, hidden_got, attention_weights, qkv_bias, padded
        )
        qkv_full = (qkv_first, qkv_second)
        qkv_half = (qkv_own, qkv_got)
        out_own, out_theirs, *lse_half = attend(*qkv_half, *marks_half, out_width)
        out_other = send(out_theirs, to_heads)
        qkv_first, out_own = lax.optimization_barrier((qkv_first, out_own))
        out_first, out_second, *lse_full = attend(qkv_first, qkv_second, *marks_full, out_width)
        attended = (out_first, out_second, out_own, out_other)
        branch_one, hidden_two, grad_two, hidden_two_turned, grad_two_turned, grad_b_down = middle_part(
            side, tokens, cotangent, attended, attention_weights, b_out[None], hot, parts, perm, third // 2
        )

        def added(mine, got):
            return mine + got.astype(F32)

        def level_pieces(values):
            part = lambda k: values[..., k * piece : (k + 1) * piece, :]
            return part(0), *(part(k).astype(BF) for k in range(1, levels))

        def all_added(kept, got):
            for part in got:
                kept = added(kept, part)
            return kept

        def after(value, *others):
            return lax.optimization_barrier((value, *others))

        quarter = width // 4

        def plane_pieces(mine_own, got_own, mine_other, got_other):
            near = lambda mine, got: added(mine[:quarter], got[:quarter])
            far = lambda mine, got: added(mine[quarter:], got[quarter:]).astype(BF)
            return (
                near(mine_own, got_own),
                far(mine_own, got_own),
                near(mine_other, got_other).astype(BF),
                far(mine_other, got_other),
            )

        feed_args = (hidden_two_turned, grad_two_turned, feed_weights, up_bias, third, 768)
        two_b, back_b, mine_b, near_b, far_b, grad_b_up_b = feed(
            1 - side, hidden_two, grad_two, *feed_args
        )
        far_b = added(mine_b[:, quarter:], send(far_b, to_core)).astype(BF)
        hidden_two, far_b, near_b = after(hidden_two, far_b, near_b)
        two_a, back_a, mine_a, near_a, far_a, grad_b_up_a, near_b, far_b = after(
            *feed(side, hidden_two, grad_two, *feed_args),
            send(near_b, to_core),
            send(far_b, to_x),
        )
        over_b = added(added(mine_b[:, :quarter], near_b), far_b).astype(BF)
        far_a = added(mine_a[:, quarter:], send(far_a, to_core)).astype(BF)
        two_a, over_b, far_a, near_a = after(two_a, over_b, far_a, near_a)

        output, grad_middle, *grad_attended, sums_two, grad_b_out, out_mine, out_theirs_sum, over_b, far_a, near_a = after(
            *back_two(
                side, tokens, cotangent, branch_one, two_a, two_b, b_down[None], back_a, back_b, attention_weights,
                hot, turn, parts, perm, attended, third // 2, images, out_width,
            ),
            send(over_b, to_heads),
            send(far_a, to_x),
            send(near_a, to_core),
        )
        grad_first, grad_second, grad_own, grad_theirs = grad_attended
        grad_other = send(grad_theirs, to_heads)
        out_got = send(out_theirs_sum, to_core)
        out_pieces = plane_pieces(out_mine[0], out_got[0], out_mine[1], out_got[1])
        feed_kept, *feed_sent = level_pieces(
            added(added(added(mine_a[:, :quarter], near_a), far_a), over_b)
        )
        grad_own, feed_kept, *joined = after(grad_own, feed_kept, *feed_sent, *out_pieces)
        feed_sent, out_pieces = joined[: levels - 1], joined[levels - 1 :]
        grad_qkv_own, grad_qkv_theirs, *out_pieces = after(
            *attend_back(*qkv_half, grad_own, grad_other, *lse_half, *marks_half),
            out_pieces[0],
            send(out_pieces[1], to_x),
            send(out_pieces[2], to_heads),
            send(out_pieces[3], to_corner),
        )
        out_kept, *out_sent = level_pieces(
            added(added(added(out_pieces[0], out_pieces[1]), out_pieces[2]), out_pieces[3])
        )
        grad_first, grad_qkv_theirs, feed_kept, out_kept, *joined = after(
            grad_first, grad_qkv_theirs, feed_kept, out_kept, *feed_sent, *out_sent
        )
        grad_qkv_first, grad_qkv_second, grad_qkv_other, *got = after(
            *attend_back(*qkv_full, grad_first, grad_second, *lse_full, *marks_full),
            send(grad_qkv_theirs, to_heads),
            *(send(part, to_level[k % (levels - 1) + 1]) for k, part in enumerate(joined)),
        )
        grad_w_up, grad_w_down = all_added(feed_kept, got[: levels - 1])
        grad_w_out = all_added(out_kept, got[levels - 1 :])
        qkv_mine_b, qkv_theirs_b, grad_qkv_bias_b = outer(
            hidden_one_turned, grad_qkv_first, grad_qkv_second, grad_qkv_other, 1
        )
        hidden_one_turned, qkv_theirs_b = after(hidden_one_turned, qkv_theirs_b)
        qkv_mine_a, qkv_theirs_a, grad_qkv_bias_a, qkv_got_b = after(
            *outer(hidden_one_turned, grad_qkv_first, grad_qkv_second, grad_qkv_own, 0),
            send(qkv_theirs_b, to_core),
        )
        near, *sent = plane_pieces(qkv_mine_a, send(qkv_theirs_a, to_core), qkv_mine_b, qkv_got_b)
        grad_middle, near, *sent = after(grad_middle, near, *sent)
        grad_qkv = (grad_qkv_first, grad_qkv_second, grad_qkv_own, grad_qkv_other)
        grad_tokens, sums_one, *got = after(
            *back_one(
                side, grad_qkv, attention_weights, tokens, grad_middle, hot, turn, parts, third // 2, images
            ),
            send(sent[0], to_x),
            send(sent[1], to_heads),
            send(sent[2], to_corner),
        )
        qkv_kept, *qkv_sent = level_pieces(all_added(near, got))

        sums = jnp.concatenate([sums_one, sums_two], axis=0).reshape(2, 3, images, width)
        sums = sums.transpose(0, 2, 1, 3).reshape(2, images, 3 * width)
        narrow = jnp.concatenate([grad_b_out, grad_b_down], axis=0).reshape(2, 2, cols)

        def packet(which, up_sum, qkv_sum):
            first = jnp.concatenate([up_sum[0], qkv_sum[:cols], qkv_sum[2 * cols : 3 * cols]])
            second = lax.dynamic_index_in_dim(narrow, which, 1, keepdims=False).reshape(-1)
            second = jnp.concatenate([second, jnp.zeros((3 * width - 2 * cols,), F32)])
            chunk = lax.dynamic_index_in_dim(sums, which, 0, keepdims=False)
            return jnp.concatenate([chunk, first[None], second[None]], axis=0)

        own_packet = packet(y, grad_b_up_a, grad_qkv_bias_a[0]) + send(
            packet(1 - y, grad_b_up_b, grad_qkv_bias_b[0]), to_heads
        )
        own_packet, qkv_kept, *qkv_sent = after(own_packet, qkv_kept, *qkv_sent)
        levelled = [own_packet] + [send(own_packet, to_level[k]) for k in range(1, levels)]
        qkv_kept = all_added(qkv_kept, [send(part, to_level[k + 1]) for k, part in enumerate(qkv_sent)])
        grad_w_qkv = qkv_kept
        flat = jnp.stack(levelled)
        flat = jnp.concatenate([flat, send(flat, to_x)], axis=0)
        packets = jnp.concatenate([flat, send(flat, to_core)], axis=0)
        grad_mod = packets[:, :images].reshape(ring * images, 3 * width)
        bias_sums = jnp.sum(packets[:, images : images + 2], axis=0)
        s1, s2, s3 = jnp.split(three_parts(silu_all), 3, axis=0)
        g1, g2, g3 = jnp.split(three_parts(grad_mod), 3, axis=0)
        grad_w_ada = contract_first(
            jnp.concatenate([s1, s1, s2, s1, s2, s3], axis=0),
            jnp.concatenate([g1, g2, g1, g3, g2, g1], axis=0),
        )
        grad_b_ada = jnp.sum(grad_mod, axis=0)
        grad_silu = lax.dot_general(
            own_packet[:images],
            w_ada,
            (((1,), (1,)), ((), ())),
            precision=PRECISE,
            preferred_element_type=F32,
        )
        grad_silu = grad_silu + send(grad_silu, to_heads)
        _, silu_back = jax.vjp(jax.nn.silu, cond)
        grad_condition = silu_back(grad_silu)[0]
        return (
            output,
            grad_tokens,
            grad_condition,
            grad_w_ada,
            grad_b_ada,
            grad_w_qkv[:, :cols],
            grad_w_qkv[:, cols : 2 * cols],
            grad_w_qkv[:, 2 * cols : 3 * cols],
            bias_sums[0, units : units + cols],
            bias_sums[0, units + cols :],
            grad_w_out[:, :cols],
            bias_sums[1, :cols],
            grad_w_up,
            bias_sums[0, :units],
            grad_w_down,
            bias_sums[1, cols : 2 * cols],
        )

    return body


def solution(mesh):
    body = fast_body(mesh) if mesh.shape["heads"] == 2 and mesh.shape["rows"] == 16 else general_body
    placed = (
        P(("rows", "heads"), None),
        P("rows", None),
        P("rows", None),
        P("rows", None, None),
        P("rows", None),
        P(None, "heads"),
        P("heads"),
        P("rows", "heads"),
        P("rows", "heads"),
        P("rows", "heads"),
        P("heads"),
        P("heads"),
        P("rows", "heads"),
        P(),
        P("rows", "heads"),
        P("heads"),
        P("rows", "heads"),
        P(),
        P(("rows", "heads"), None),
    )
    return jax.shard_map(
        body,
        mesh=mesh,
        in_specs=placed,
        out_specs=(
            P(("rows", "heads"), None),
            P(("rows", "heads"), None),
            P("rows", None),
            P(None, "heads"),
            P("heads"),
            P("rows", "heads"),
            P("rows", "heads"),
            P("rows", "heads"),
            P("heads"),
            P("heads"),
            P("rows", "heads"),
            P("heads"),
            P("rows", "heads"),
            P("heads"),
            P("rows", "heads"),
            P("heads"),
        ),
        check_vma=False,
    )
```

```python
from functools import partial

import jax
import jax.numpy as jnp
from jax import lax
from jax.experimental import pallas as pl
from jax.experimental.pallas import tpu as pltpu
from jax.sharding import PartitionSpec as P

HEAD_DIM = 72
TILE = 128


EPSILON = 1e-06
MASKED_SCORE = -1e30
PRECISE = lax.Precision.HIGHEST


def layer_norm(values):
    centred = values - jnp.mean(values, axis=-1, keepdims=True)
    inverse = lax.rsqrt(jnp.mean(centred * centred, axis=-1, keepdims=True) + EPSILON)
    return (centred * inverse, inverse)


def norm_back(normed, inverse, grad):
    return inverse * (
        grad
        - jnp.mean(grad, axis=-1, keepdims=True)
        - normed * jnp.mean(grad * normed, axis=-1, keepdims=True)
    )


def contract_last(left, right):
    return lax.dot_general(
        left, right, (((1,), (1,)), ((), ())), preferred_element_type=jnp.float32
    )


def contract_first(left, right):
    return lax.dot_general(
        left, right, (((0,), (0,)), ((), ())), preferred_element_type=jnp.float32
    )


def general_body(
    tokens,
    condition,
    segment_ids,
    tile_mask,
    image_index,
    w_ada,
    b_ada,
    w_query,
    w_key,
    w_value,
    b_query,
    b_value,
    w_out,
    b_out,
    w_up,
    b_up,
    w_down,
    b_down,
    cotangent,
):
    scaling = HEAD_DIM ** (-0.5)
    own_rows = tokens.shape[0]
    seq_count = segment_ids.shape[0]
    length = segment_ids.shape[1]
    group_rows = seq_count * length
    own_start = lax.axis_index("heads") * own_rows
    img_count = condition.shape[0]
    slot_count = image_index.shape[1]
    local_heads = w_query.shape[1] // HEAD_DIM
    block_rows = min(512, length)
    tile_count = length // TILE
    bfloat = jnp.bfloat16
    own_segments = lax.dynamic_slice_in_dim(segment_ids.reshape(group_rows), own_start, own_rows)
    own_seqs = (own_start + jnp.arange(own_rows, dtype=jnp.int32)) // length
    seq_match = own_seqs[:, None] == jnp.arange(seq_count, dtype=jnp.int32)[None, :]
    slot_match = own_segments[:, None] == jnp.arange(slot_count, dtype=jnp.int32)[None, :]
    own_image = jnp.sum(
        jnp.where(seq_match[:, :, None] & slot_match[:, None, :], image_index[None, :, :], 0),
        axis=(1, 2),
    )
    image_onehot = (own_image[:, None] == jnp.arange(img_count, dtype=jnp.int32)[None, :]).astype(
        jnp.float32
    )
    cond_full = condition.astype(jnp.float32)
    silu_cond = jax.nn.silu(cond_full)
    mod_cols = jnp.dot(silu_cond, w_ada, precision=PRECISE) + b_ada
    mod_full, up_bias_all = (
        lax.all_gather(mod_cols, "heads", axis=1, tiled=True),
        lax.all_gather(b_up.reshape(1, -1), "heads", axis=1, tiled=True),
    )
    per_token = jnp.dot(image_onehot, mod_full, precision=PRECISE)
    shift_one, scale_one, gate_one, shift_two, scale_two, gate_two = jnp.split(per_token, 6, axis=1)

    def gather_weights():
        return (
            lax.all_gather(w_query.astype(bfloat), "rows", axis=0, tiled=True),
            lax.all_gather(w_key.astype(bfloat), "rows", axis=0, tiled=True),
            lax.all_gather(w_value.astype(bfloat), "rows", axis=0, tiled=True),
            lax.all_gather(w_out.astype(bfloat), "rows", axis=0, tiled=True),
            lax.all_gather(w_up.astype(bfloat), "rows", axis=0, tiled=True),
            lax.all_gather(w_down.astype(bfloat), "rows", axis=0, tiled=True),
        )

    def spread_first(values):
        return lax.all_gather(values, "heads", axis=0, tiled=True)

    query_full, key_full, value_full, out_full, up_full, down_full = gather_weights()
    token_full = tokens.astype(jnp.float32)
    normed_one, inverse_one = layer_norm(token_full)
    hidden_own_one = (normed_one * (1.0 + scale_one) + shift_one).astype(bfloat)
    hidden_one = spread_first(hidden_own_one)
    head_shape = (group_rows, local_heads, HEAD_DIM)
    query_heads = (
        (jnp.dot(hidden_one, query_full, preferred_element_type=jnp.float32) + b_query)
        .astype(bfloat)
        .reshape(head_shape)
    )
    key_heads = (
        jnp.dot(hidden_one, key_full, preferred_element_type=jnp.float32)
        .astype(bfloat)
        .reshape(head_shape)
    )
    value_heads = (
        (jnp.dot(hidden_one, value_full, preferred_element_type=jnp.float32) + b_value)
        .astype(bfloat)
        .reshape(head_shape)
    )
    tile_of = jnp.arange(length, dtype=jnp.int32) // TILE

    def scores_for(seq_index, block_start):
        seq_start = seq_index * length
        block_query = query_heads[seq_start + block_start : seq_start + block_start + block_rows]
        seq_keys = key_heads[seq_start : seq_start + length]
        block_tiles = tile_mask[seq_index][block_start // TILE : (block_start + block_rows) // TILE]
        expanded = jnp.broadcast_to(
            block_tiles[:, None, :, None], (block_rows // TILE, TILE, tile_count, TILE)
        ).reshape(block_rows, length)
        seg_row = segment_ids[seq_index]
        same_image = seg_row[block_start : block_start + block_rows][:, None] == seg_row[None, :]
        diagonal = tile_of[block_start : block_start + block_rows][:, None] == tile_of[None, :]
        allowed = same_image & ((expanded > 0) | diagonal)
        raw = (
            jnp.einsum("qhd,khd->hqk", block_query, seq_keys, preferred_element_type=jnp.float32)
            * scaling
        )
        return (jnp.where(allowed[None], raw, MASKED_SCORE), block_query, seq_keys)

    attended_parts = []
    log_totals = []
    for seq_index in range(seq_count):
        seq_values = value_heads[seq_index * length : (seq_index + 1) * length]
        for block_start in range(0, length, block_rows):
            scores, block_query, seq_keys = scores_for(seq_index, block_start)
            top_score = jnp.max(scores, axis=-1, keepdims=True)
            log_total = top_score + jnp.log(
                jnp.sum(jnp.exp(scores - top_score), axis=-1, keepdims=True)
            )
            probs_low = jnp.exp(scores - log_total).astype(bfloat)
            attended_parts.append(
                jnp.einsum(
                    "hqk,khd->qhd", probs_low, seq_values, preferred_element_type=jnp.float32
                )
            )
            log_totals.append(log_total)
    attended = (
        jnp.concatenate(attended_parts, axis=0)
        .reshape(group_rows, local_heads * HEAD_DIM)
        .astype(bfloat)
    )
    branch_one = (
        lax.psum_scatter(
            contract_last(attended, out_full), "heads", scatter_dimension=0, tiled=True
        )
        + b_out
    )
    middle = token_full + gate_one * branch_one
    normed_two, inverse_two = layer_norm(middle)
    hidden_own_two = (normed_two * (1.0 + scale_two) + shift_two).astype(bfloat)
    up_all, down_all = (
        lax.all_gather(up_full, "heads", axis=1, tiled=True),
        lax.all_gather(down_full, "heads", axis=1, tiled=True),
    )
    pre_act = jnp.dot(hidden_own_two, up_all, preferred_element_type=jnp.float32) + up_bias_all[0]
    activated = jax.nn.gelu(pre_act, approximate=True).astype(bfloat)
    branch_two = contract_last(activated, down_all) + b_down
    output = (middle + gate_two * branch_two).astype(bfloat)
    query_back, key_back, value_back, out_back, up_back, down_back = gather_weights()
    hidden_one_back = spread_first(hidden_own_one)
    grad_out = cotangent.astype(jnp.float32)
    grad_branch_two = (grad_out * gate_two).astype(bfloat)
    grad_gate_two = grad_out * branch_two
    grad_down_all = contract_first(grad_branch_two, activated)
    grad_act = jnp.dot(grad_branch_two, down_all, preferred_element_type=jnp.float32)
    _, gelu_back = jax.vjp(partial(jax.nn.gelu, approximate=True), pre_act)
    grad_pre = gelu_back(grad_act)[0].astype(bfloat)
    grad_up_all = contract_first(hidden_own_two, grad_pre)
    grad_bias_all = jnp.sum(grad_pre, axis=0, dtype=jnp.float32).reshape(1, -1)
    grad_hidden_two = contract_last(grad_pre, up_all)
    grad_w_up, grad_w_down, grad_bias_cols = (
        lax.psum_scatter(grad_up_all, "heads", scatter_dimension=1, tiled=True),
        lax.psum_scatter(grad_down_all, "heads", scatter_dimension=1, tiled=True),
        lax.psum_scatter(grad_bias_all, "heads", scatter_dimension=1, tiled=True),
    )
    grad_b_up = grad_bias_cols[0]
    grad_scale_two = grad_hidden_two * normed_two
    grad_middle = grad_out + norm_back(normed_two, inverse_two, grad_hidden_two * (1.0 + scale_two))
    grad_branch_one = (grad_middle * gate_one).astype(bfloat)
    grad_gate_one = grad_middle * branch_one
    grad_one_full = lax.all_gather(grad_branch_one, "heads", axis=0, tiled=True)
    grad_w_out = contract_first(grad_one_full, attended)
    grad_attended = (
        jnp.dot(grad_one_full, out_back, preferred_element_type=jnp.float32)
        .astype(bfloat)
        .reshape(head_shape)
    )
    grad_query_parts = []
    grad_key_parts = []
    grad_value_parts = []
    block_number = 0
    for seq_index in range(seq_count):
        seq_start = seq_index * length
        seq_values = value_heads[seq_start : seq_start + length]
        key_total = jnp.zeros((length, local_heads, HEAD_DIM), jnp.float32)
        value_total = jnp.zeros((length, local_heads, HEAD_DIM), jnp.float32)
        for block_start in range(0, length, block_rows):
            scores, block_query, seq_keys = scores_for(seq_index, block_start)
            probs = jnp.exp(scores - log_totals[block_number])
            block_number += 1
            grad_block = grad_attended[
                seq_start + block_start : seq_start + block_start + block_rows
            ]
            grad_probs = jnp.einsum(
                "qhd,khd->hqk", grad_block, seq_values, preferred_element_type=jnp.float32
            )
            centre = jnp.sum(probs * grad_probs, axis=-1, keepdims=True)
            grad_scores = (probs * (grad_probs - centre)).astype(bfloat)
            grad_query_parts.append(
                (
                    jnp.einsum(
                        "hqk,khd->qhd", grad_scores, seq_keys, preferred_element_type=jnp.float32
                    )
                    * scaling
                ).astype(bfloat)
            )
            key_total = (
                key_total
                + jnp.einsum(
                    "hqk,qhd->khd", grad_scores, block_query, preferred_element_type=jnp.float32
                )
                * scaling
            )
            value_total = value_total + jnp.einsum(
                "hqk,qhd->khd", probs.astype(bfloat), grad_block, preferred_element_type=jnp.float32
            )
        grad_key_parts.append(key_total.astype(bfloat))
        grad_value_parts.append(value_total.astype(bfloat))
    flat_shape = (group_rows, local_heads * HEAD_DIM)
    grad_queries = jnp.concatenate(grad_query_parts, axis=0).reshape(flat_shape)
    grad_keys = jnp.concatenate(grad_key_parts, axis=0).reshape(flat_shape)
    grad_values = jnp.concatenate(grad_value_parts, axis=0).reshape(flat_shape)
    grad_w_query = contract_first(hidden_one_back, grad_queries)
    grad_w_key = contract_first(hidden_one_back, grad_keys)
    grad_w_value = contract_first(hidden_one_back, grad_values)
    grad_b_query = jnp.sum(grad_queries, axis=0, dtype=jnp.float32)
    grad_b_value = jnp.sum(grad_values, axis=0, dtype=jnp.float32)
    total = contract_last(grad_queries, query_back)
    total = total + contract_last(grad_keys, key_back)
    grad_hidden_one = lax.psum_scatter(
        total + contract_last(grad_values, value_back), "heads", scatter_dimension=0, tiled=True
    )
    grad_scale_one = grad_hidden_one * normed_one
    grad_tokens = grad_middle + norm_back(
        normed_one, inverse_one, grad_hidden_one * (1.0 + scale_one)
    )
    grad_mod_tokens = jnp.concatenate(
        [
            grad_hidden_one,
            grad_scale_one,
            grad_gate_one,
            grad_hidden_two,
            grad_scale_two,
            grad_gate_two,
        ],
        axis=1,
    )
    grad_mod_images = lax.dot_general(
        image_onehot,
        grad_mod_tokens,
        (((0,), (0,)), ((), ())),
        precision=PRECISE,
        preferred_element_type=jnp.float32,
    )
    bias_parts = jnp.stack(
        [
            jnp.sum(grad_branch_one, axis=0, dtype=jnp.float32),
            jnp.sum(grad_branch_two, axis=0, dtype=jnp.float32),
        ],
        axis=0,
    )
    grad_mod_cols, bias_cols = (
        lax.psum_scatter(grad_mod_images, "heads", scatter_dimension=1, tiled=True),
        lax.psum_scatter(bias_parts, "heads", scatter_dimension=1, tiled=True),
    )
    grad_w_ada = lax.dot_general(
        silu_cond,
        grad_mod_cols,
        (((0,), (0,)), ((), ())),
        precision=PRECISE,
        preferred_element_type=jnp.float32,
    )
    grad_b_ada = jnp.sum(grad_mod_cols, axis=0)
    grad_silu = lax.dot_general(
        grad_mod_cols,
        w_ada,
        (((1,), (1,)), ((), ())),
        precision=PRECISE,
        preferred_element_type=jnp.float32,
    )
    grad_silu = lax.psum(grad_silu, "heads")
    _, silu_back = jax.vjp(jax.nn.silu, cond_full)
    grad_condition = silu_back(grad_silu)[0]
    grad_w_ada, grad_b_ada, grad_b_query, grad_b_value, grad_b_up, bias_cols = lax.psum(
        (grad_w_ada, grad_b_ada, grad_b_query, grad_b_value, grad_b_up, bias_cols), "rows"
    )
    grad_w_query, grad_w_key, grad_w_value, grad_w_out, grad_w_up, grad_w_down = (
        lax.psum_scatter(grad_w_query, "rows", scatter_dimension=0, tiled=True),
        lax.psum_scatter(grad_w_key, "rows", scatter_dimension=0, tiled=True),
        lax.psum_scatter(grad_w_value, "rows", scatter_dimension=0, tiled=True),
        lax.psum_scatter(grad_w_out, "rows", scatter_dimension=0, tiled=True),
        lax.psum_scatter(grad_w_up, "rows", scatter_dimension=0, tiled=True),
        lax.psum_scatter(grad_w_down, "rows", scatter_dimension=0, tiled=True),
    )
    return (
        output,
        grad_tokens,
        grad_condition,
        grad_w_ada,
        grad_b_ada,
        grad_w_query,
        grad_w_key,
        grad_w_value,
        grad_b_query,
        grad_b_value,
        grad_w_out,
        bias_cols[0],
        grad_w_up,
        grad_b_up,
        grad_w_down,
        bias_cols[1],
    )


LOG2E = 1.4426950408889634
GELU_SLOPE = 0.7978845608028654
GELU_CUBE = 0.044715
BF = jnp.bfloat16
F32 = jnp.float32
MIB = 2**20


def rows_by_columns(left, right):
    return jnp.dot(left, right, preferred_element_type=F32)


def shape(dims, dtype):
    return jax.ShapeDtypeStruct(dims, dtype)


def params(mib=56):
    return pltpu.CompilerParams(vmem_limit_bytes=mib * MIB)


def cost(flops, bytes_accessed, transcendentals=0):
    return pl.CostEstimate(
        flops=int(flops), bytes_accessed=int(bytes_accessed), transcendentals=int(transcendentals)
    )


def three_parts(values):
    high = lax.reduce_precision(values, 8, 7)
    rest = values - high
    middle = lax.reduce_precision(rest, 8, 7)
    return jnp.concatenate([high, middle, rest - middle], axis=-2).astype(BF)


def collect_kernel(core, over_x, x_got, over_y, y_got, last, last_got, whole, sems):
    heads, levels, xs = whole.shape[:3]
    count = over_x.shape[-1]
    place_of = (lambda h, z, x: (h, x, z), lambda h, z, x: (x, h, z), lambda h, z, x: (z, h, x))
    copies = []
    for k, pair in enumerate(((over_x, x_got), (over_y, y_got), (last, last_got))):
        for got, source in enumerate(pair):
            c = core[0] if got == 0 else 1 - core[0]
            for h in range(heads):
                for z in range(levels):
                    for x in range(xs):
                        copy = pltpu.make_async_copy(
                            source.at[place_of[k](h, z, x)],
                            whole.at[h, z, x, c, :, pl.ds(k * count, count)],
                            sems.at[len(copies)],
                        )
                        copy.start()
                        copies.append(copy)
    for copy in copies:
        copy.wait()


def collected(core, over_x, x_got, over_y, y_got, last, last_got):
    levels, heads, xs, piece, count = last.shape
    whole = (heads, levels, xs, 2, piece, 3 * count)
    anywhere = pl.BlockSpec(memory_space=pl.ANY)
    return pl.pallas_call(
        collect_kernel,
        grid_spec=pltpu.PrefetchScalarGridSpec(
            num_scalar_prefetch=1,
            grid=(1,),
            in_specs=[anywhere] * 6,
            out_specs=anywhere,
            scratch_shapes=[pltpu.SemaphoreType.DMA((6 * heads * levels * xs,))],
        ),
        out_shape=shape(whole, BF),
        compiler_params=params(16),
        cost_estimate=cost(0, 24 * heads * levels * xs * piece * count),
    )(core, over_x, x_got, over_y, y_got, last, last_got)


def turn_in_order(places, turned_ref, values):
    turned = values.astype(F32).T
    piece = turned_ref.shape[1]
    for k in range(turned_ref.shape[0]):
        turned_ref[places[1 + k]] = turned[k * piece : (k + 1) * piece].astype(BF)


def norm_kernel(side, tok_ref, hot_ref, parts_ref, h_ref, half_ref, ht_ref):
    width = tok_ref.shape[1]
    normed, _ = layer_norm(tok_ref[...].astype(F32))
    mod = rows_by_columns(hot_ref[...], parts_ref[0, :, : 2 * width])
    hidden = (normed * (1.0 + mod[:, width:]) + mod[:, :width]).astype(BF)
    turn_in_order(side, ht_ref, hidden)

    @pl.when(pl.program_id(0) < 2)
    def _():
        h_ref[...] = hidden

    @pl.when(pl.program_id(0) == 2)
    def _():
        half_ref[...] = hidden


def first_norm(side, tokens, hot, parts, block):
    ring = side.shape[0] // 2
    rows, width = tokens.shape
    return pl.pallas_call(
        norm_kernel,
        grid_spec=pltpu.PrefetchScalarGridSpec(
            num_scalar_prefetch=1,
            grid=(rows // block,),
            in_specs=[
                pl.BlockSpec((block, width), lambda i, y: ((i + y[0]) % 3, 0)),
                pl.BlockSpec((block, hot.shape[1]), lambda i, y: (i, 0)),
                pl.BlockSpec((1,) + parts.shape[1:], lambda i, y: (0, 0, 0)),
            ],
            out_specs=[
                pl.BlockSpec((block, width), lambda i, y: (jnp.minimum(i, 1), 0)),
                pl.BlockSpec((block, width), lambda i, y: (0, 0)),
                pl.BlockSpec((ring, width // ring, block), lambda i, y: (0, 0, i)),
            ],
        ),
        out_shape=[
            shape((2 * block, width), BF),
            shape((block, width), BF),
            shape((ring, width // ring, rows), BF),
        ],
        compiler_params=params(),
        cost_estimate=cost(2 * rows * width * (width + 512), rows * width * 6),
    )(side, tokens, hot, parts)


def project_kernel(side, full_ref, own_ref, got_ref, w_ref, bias_ref, first, second, own, got):
    block, padded = own.shape[1:]
    cols = bias_ref.shape[2]

    def found(hidden):
        value = (rows_by_columns(hidden, w_ref[0, :, :cols]) + bias_ref[0]).astype(BF)
        return jnp.concatenate([value, jnp.zeros((block, padded - cols), BF)], axis=1)

    first[0] = found(full_ref[:block])
    second[0] = found(full_ref[block:])

    @pl.when(pl.program_id(0) == 0)
    def _():
        own[0] = found(own_ref[...])
        got[0] = found(got_ref[...])


def project(side, full, own, got, weights, bias, padded):
    block, width = own.shape
    pick = lambda a, y: a + y[0] - 2 * a * y[0]
    single = pl.BlockSpec((1, block, padded), lambda a, y: (0, 0, 0))
    pair = pl.BlockSpec((1, block, padded), lambda a, y: (a, 0, 0))
    return pl.pallas_call(
        project_kernel,
        grid_spec=pltpu.PrefetchScalarGridSpec(
            num_scalar_prefetch=1,
            grid=(2,),
            in_specs=[
                pl.BlockSpec((2 * block, width), lambda a, y: (0, 0)),
                pl.BlockSpec((block, width), lambda a, y: (0, 0)),
                pl.BlockSpec((block, width), lambda a, y: (0, 0)),
                pl.BlockSpec((1,) + weights.shape[1:], lambda a, y: (pick(a, y), 0, 0)),
                pl.BlockSpec((1,) + bias.shape[1:], lambda a, y: (pick(a, y), 0, 0)),
            ],
            out_specs=[pair, pair, single, single],
        ),
        out_shape=[shape((2, block, padded), BF)] * 2 + [shape((1, block, padded), BF)] * 2,
        compiler_params=params(60),
        cost_estimate=cost(12 * block * width * padded, 12 * block * padded + 4 * width * padded),
    )(side, full, own, got, weights, bias)


MARKS = 16
DEPTH = 128
LSE_AT = HEAD_DIM + MARKS - 4
STEEP = HEAD_DIM**-0.5 * LOG2E


def split_three(values):
    high = values.astype(BF)
    rest = values - high.astype(F32)
    middle = rest.astype(BF)
    return jnp.concatenate([high, middle, (rest - middle.astype(F32)).astype(BF)], axis=1)


def at_head(h, part, heads):
    start = (part * heads + h) * HEAD_DIM
    return slice(start, start + HEAD_DIM)


def both_halves(first, second, columns):
    return jnp.concatenate([first[0, :, columns], second[0, :, columns]], axis=0)


def padded_columns(parts, width):
    found = jnp.concatenate(parts, axis=1)
    gap = width - found.shape[1]
    return jnp.concatenate([found, jnp.zeros((found.shape[0], gap), found.dtype)], axis=1)


def attend_kernel(
    heads, first, second, qm_ref, km_ref, o_first, o_second, l_first, l_second, keys, values, queries
):
    i = pl.program_id(1)

    @pl.when((i == 0) & (pl.program_id(0) == 0))
    def _():
        keys[...] = jnp.zeros_like(keys)
        queries[...] = jnp.zeros_like(queries)

    @pl.when(i == 0)
    def _():
        for h in range(heads):
            keys[h, :, :HEAD_DIM] = both_halves(first, second, at_head(h, 1, heads))
            keys[h, :, HEAD_DIM : HEAD_DIM + MARKS] = km_ref[...]
            value = both_halves(first, second, at_head(h, 2, heads))
            values[h] = value.astype(F32).T.astype(BF)

    for h in range(heads):
        columns = at_head(h, 0, heads)
        queries[h, :, :HEAD_DIM] = jnp.where(i == 0, first[0, :, columns], second[0, :, columns])
        queries[h, :, HEAD_DIM : HEAD_DIM + MARKS] = qm_ref[...]
    parts = []
    totals = []
    probs = None
    scores = contract_last(keys[0], queries[0])
    for h in range(heads):
        later = contract_last(keys[h + 1], queries[h + 1]) if h + 1 < heads else None
        top = jnp.max(scores, axis=0, keepdims=True)
        powers = jnp.exp2((scores - top) * STEEP)
        total = jnp.sum(powers, axis=0, keepdims=True)
        totals.append(top + jnp.log2(total) * (1.0 / STEEP))
        if h > 0:
            parts.append(rows_by_columns(values[h - 1], probs).T.astype(BF))
        probs = (powers * (1.0 / total)).astype(BF)
        scores = later
    parts.append(rows_by_columns(values[heads - 1], probs).T.astype(BF))
    out = padded_columns(parts, o_first.shape[2])
    log_totals = jnp.concatenate(totals, axis=0)

    @pl.when(i == 0)
    def _():
        o_first[0] = out
        l_first[0] = log_totals

    @pl.when(i == 1)
    def _():
        o_second[0] = out
        l_second[0] = log_totals


def attend(first, second, query_marks, key_marks, out_width):
    groups, half, padded = first.shape
    heads = out_width // HEAD_DIM
    pair = lambda *dims: pl.BlockSpec((1,) + dims, lambda a, i: (a, 0, 0))
    return pl.pallas_call(
        partial(attend_kernel, heads),
        grid=(groups, 2),
        in_specs=[
            pair(half, padded),
            pair(half, padded),
            pl.BlockSpec((half, MARKS), lambda a, i: (i, 0)),
            pl.BlockSpec((2 * half, MARKS), lambda a, i: (0, 0)),
        ],
        out_specs=[pair(half, out_width)] * 2 + [pair(heads, half)] * 2,
        out_shape=[shape((groups, half, out_width), BF)] * 2 + [shape((groups, heads, half), F32)] * 2,
        scratch_shapes=[
            pltpu.VMEM((heads, 2 * half, DEPTH), BF),
            pltpu.VMEM((heads, HEAD_DIM, 2 * half), BF),
            pltpu.VMEM((heads, half, DEPTH), BF),
        ],
        compiler_params=params(),
        cost_estimate=cost(groups * 15e9, groups * half * padded * 6, groups * heads * half * half),
    )(first, second, query_marks, key_marks)


def attend_back_kernel(
    heads, first, second, do_first, do_second, l_first, l_second, qm_ref, km_ref,
    out_first, out_second, keys, values, turned, queries, dk, dv,
):
    i = pl.program_id(1)
    half, padded = first.shape[1:]
    width = heads * HEAD_DIM
    scaling = HEAD_DIM**-0.5

    @pl.when((i == 0) & (pl.program_id(0) == 0))
    def _():
        keys[...] = jnp.zeros_like(keys)
        queries[...] = jnp.zeros_like(queries)

    @pl.when(i == 0)
    def _():
        for h in range(heads):
            key = both_halves(first, second, at_head(h, 1, heads))
            keys[h, :, :HEAD_DIM] = key
            keys[h, :, HEAD_DIM : HEAD_DIM + MARKS] = km_ref[...]
            turned[h] = key.astype(F32).T.astype(BF)
            values[h] = both_halves(first, second, at_head(h, 2, heads))
        dk[...] = jnp.zeros_like(dk)
        dv[...] = jnp.zeros_like(dv)

    log_totals = jnp.where(i == 0, l_first[0], l_second[0]).T
    plain = []
    for h in range(heads):
        columns = at_head(h, 0, heads)
        query = jnp.where(i == 0, first[0, :, columns], second[0, :, columns])
        grad = jnp.where(i == 0, do_first[0, :, columns], do_second[0, :, columns])
        queries[h, :, :HEAD_DIM] = query
        queries[h, :, HEAD_DIM : HEAD_DIM + MARKS] = qm_ref[...]
        queries[h, :, LSE_AT : LSE_AT + 3] = split_three(-log_totals[:, h : h + 1])
        plain.append((query, grad))

    def scores_of(h):
        return contract_last(keys[h], queries[h]), contract_last(values[h], plain[h][1])

    def finish(h, probs, grad_scores):
        query, grad = plain[h]
        dv[h] += rows_by_columns(probs, grad)
        dk[h] += rows_by_columns(grad_scores, query)
        return (rows_by_columns(turned[h], grad_scores) * scaling).T.astype(BF)

    parts = []
    before = None
    scores, grad_probs = scores_of(0)
    for h in range(heads):
        later = scores_of(h + 1) if h + 1 < heads else (None, None)
        probs = jnp.exp2(scores * STEEP)
        centre = jnp.sum(probs * grad_probs, axis=0, keepdims=True)
        grad_scores = (probs * (grad_probs - centre)).astype(BF)
        if before is not None:
            parts.append(finish(h - 1, *before))
        before = (probs.astype(BF), grad_scores)
        scores, grad_probs = later
    parts.append(finish(heads - 1, *before))
    grad_queries = jnp.concatenate(parts, axis=1)

    @pl.when(i == 0)
    def _():
        out_first[0, :, :width] = grad_queries

    @pl.when(i == 1)
    def _():
        out_second[0, :, :width] = grad_queries
        for start, ref in ((0, out_first), (half, out_second)):
            rows = slice(start, start + half)
            ref[0, :, width:] = padded_columns(
                [(dk[h, rows] * scaling).astype(BF) for h in range(heads)]
                + [dv[h, rows].astype(BF) for h in range(heads)],
                padded - width,
            )


def attend_back(first, second, do_first, do_second, l_first, l_second, query_marks, key_marks):
    groups, half, padded = first.shape
    heads = l_first.shape[1]
    out_width = do_first.shape[2]
    pair = lambda *dims: pl.BlockSpec((1,) + dims, lambda a, i: (a, 0, 0))
    return pl.pallas_call(
        partial(attend_back_kernel, heads),
        grid=(groups, 2),
        in_specs=[pair(half, padded)] * 2
        + [pair(half, out_width)] * 2
        + [pair(heads, half)] * 2
        + [
            pl.BlockSpec((half, MARKS), lambda a, i: (i, 0)),
            pl.BlockSpec((2 * half, MARKS), lambda a, i: (0, 0)),
        ],
        out_specs=[pair(half, padded)] * 2,
        out_shape=[shape((groups, half, padded), BF)] * 2,
        scratch_shapes=[
            pltpu.VMEM((heads, 2 * half, DEPTH), BF),
            pltpu.VMEM((heads, 2 * half, HEAD_DIM), BF),
            pltpu.VMEM((heads, HEAD_DIM, 2 * half), BF),
            pltpu.VMEM((heads, half, DEPTH), BF),
            pltpu.VMEM((heads, 2 * half, HEAD_DIM), F32),
            pltpu.VMEM((heads, 2 * half, HEAD_DIM), F32),
        ],
        compiler_params=params(60),
        cost_estimate=cost(groups * 12e9, groups * half * padded * 12, groups * heads * half * half),
    )(first, second, do_first, do_second, l_first, l_second, query_marks, key_marks)


def image_sums(hot_turned, values):
    high = values.astype(BF)
    low = (values - high.astype(F32)).astype(BF)
    return rows_by_columns(hot_turned, high) + rows_by_columns(hot_turned, low)


def add_up(ref, value):
    @pl.when(pl.program_id(0) == 0)
    def _():
        ref[...] = value

    @pl.when(pl.program_id(0) != 0)
    def _():
        ref[...] += value


def third_of(first, second, own, other, i, per):
    half = jnp.stack([own[0], other[0]], axis=0)
    return jnp.where(i < per, first[...], jnp.where(i < 2 * per, second[...], half))


def third_specs(block, columns, per):
    full = lambda low: pl.BlockSpec(
        (2, block, columns), lambda i, y: (0, jnp.clip(i - low * per, 0, per - 1), 0)
    )
    single = pl.BlockSpec((1, block, columns), lambda i, y: (0, jnp.clip(i - 2 * per, 0, per - 1), 0))
    return [full(0), full(1), single, single]


def out_weight_specs(width, columns):
    last = columns // (2 * width // 3) - 1
    return [
        pl.BlockSpec((1, width, 2 * width // 3), lambda i, y: (y[0], 0, last)),
        pl.BlockSpec((1, width, 2 * width // 3), lambda i, y: (1 - y[0], 0, last)),
    ]


def middle_kernel(
    side, tok_ref, dy_ref, first, second, own, other, w_own, w_other, b_ref, hot_ref, parts_ref,
    branch_ref, h_ref, g_ref, ht_ref, gt_ref, gb_ref,
):
    i = pl.program_id(0)
    width = tok_ref.shape[1]
    used = width // 2
    att = third_of(first, second, own, other, i, pl.num_programs(0) // 3)[:, :, :used]
    skip = w_own.shape[2] - used
    branch = (
        contract_last(att[0], w_own[0, :, skip:])
        + contract_last(att[1], w_other[0, :, skip:])
        + b_ref[...]
    )
    branch_ref[...] = branch
    hot = hot_ref[...]
    gate = rows_by_columns(hot, parts_ref[0, :, 2 * width :])
    mod = rows_by_columns(hot, parts_ref[1])
    normed, _ = layer_norm(tok_ref[...].astype(F32) + gate * branch)
    hidden = (normed * (1.0 + mod[:, width : 2 * width]) + mod[:, :width]).astype(BF)
    grad = (dy_ref[...].astype(F32) * mod[:, 2 * width :]).astype(BF)
    h_ref[...] = hidden
    g_ref[...] = grad
    turn_in_order(side, ht_ref, hidden)
    turn_in_order(side, gt_ref, grad)
    add_up(gb_ref, jnp.sum(grad.astype(F32), axis=0, keepdims=True))


def middle_part(side, tokens, cotangent, thirds, weights, b_out, hot, parts, block):
    ring = side.shape[0] // 2
    rows, width = tokens.shape
    per = rows // 3 // block
    spec = lambda dims: pl.BlockSpec(dims, lambda i, y: (0,) * len(dims))
    placed = pl.BlockSpec(
        (block, width), lambda i, y: (((i // per + y[0]) % 3) * per + i % per, 0)
    )
    plain = pl.BlockSpec((block, width), lambda i, y: (i, 0))
    turned = pl.BlockSpec((ring, width // ring, block), lambda i, y: (0, 0, i))
    return pl.pallas_call(
        middle_kernel,
        grid_spec=pltpu.PrefetchScalarGridSpec(
            num_scalar_prefetch=1,
            grid=(rows // block,),
            in_specs=[
                placed,
                placed,
                *third_specs(block, thirds[0].shape[2], per),
                *out_weight_specs(width, weights.shape[2]),
                spec((1, width)),
                pl.BlockSpec((block, hot.shape[1]), lambda i, y: (i, 0)),
                spec(parts.shape),
            ],
            out_specs=[plain, plain, plain, turned, turned, spec((1, width))],
        ),
        out_shape=[
            shape((rows, width), F32),
            shape((rows, width), BF),
            shape((rows, width), BF),
            shape((ring, width // ring, rows), BF),
            shape((ring, width // ring, rows), BF),
            shape((1, width), F32),
        ],
        compiler_params=params(),
        cost_estimate=cost(2 * rows * width * (3 * width + 1024), rows * width * 22),
    )(side, tokens, cotangent, *thirds, weights, weights, b_out, hot, parts)


def feed_kernel(
    chunk, pick, h_ref, g_ref, ht_ref, gt_ref, up_ref, down_ref, bias_ref,
    branch_ref, back_ref, mine_ref, near_ref, far_ref, gb_ref, act, pre,
):
    j = pl.program_id(0)
    rows = h_ref.shape[0]
    half = ht_ref.shape[0] // 2
    up = up_ref[0, 0]
    down = down_ref[0, 0]
    total = jnp.zeros(gb_ref.shape, F32)
    for start in range(0, rows, chunk):
        at = slice(start, start + chunk)
        u = rows_by_columns(h_ref[at], up) + bias_ref[0]
        grad = rows_by_columns(g_ref[at], down)
        cube = GELU_CUBE * u * u
        bent = jnp.tanh(GELU_SLOPE * (u + cube * u))
        part = 0.5 * (1.0 + bent)
        slope = part + 0.5 * u * (1.0 - bent * bent) * (GELU_SLOPE * (1.0 + 3.0 * cube))
        low = (u * part).astype(BF)
        back = (grad * slope).astype(BF)
        act[at] = low
        pre[at] = back
        total += jnp.sum(back.astype(F32), axis=0, keepdims=True)
        branch_part = contract_last(low, down)
        back_part = contract_last(back, up)

        @pl.when(j == 0)
        def _():
            branch_ref[at] = branch_part
            back_ref[at] = back_part

        @pl.when(j != 0)
        def _():
            branch_ref[at] += branch_part
            back_ref[at] += back_part

    gb_ref[...] = total
    quarter = half // 2
    for k, (turned, value) in enumerate(((ht_ref, pre), (gt_ref, act))):
        theirs = rows_by_columns(turned[half:], value[...]).astype(BF)
        near_ref[k] = theirs[:quarter]
        far_ref[k] = theirs[quarter:]
        mine_ref[k] = rows_by_columns(turned[:half], value[...])


def feed(pick, hidden, grad, hidden_turned, grad_turned, weights, bias, chunk, cols):
    rows, width = hidden.shape
    units = weights.shape[3]
    half = width // 2
    whole = lambda dims: pl.BlockSpec(dims, lambda j, y: (0, 0), pipeline_mode=pl.Buffered(1))
    columns = lambda k: pl.BlockSpec((1, 1, width, cols), lambda j, y: (k, y[0], 0, j))
    return pl.pallas_call(
        partial(feed_kernel, chunk),
        grid_spec=pltpu.PrefetchScalarGridSpec(
            num_scalar_prefetch=1,
            grid=(units // cols,),
            in_specs=[
                whole((rows, width)),
                whole((rows, width)),
                whole((width, rows)),
                whole((width, rows)),
                columns(0),
                columns(1),
                pl.BlockSpec((1, 1, cols), lambda j, y: (y[0], 0, j)),
            ],
            out_specs=[
                whole((rows, width)),
                whole((rows, width)),
                pl.BlockSpec((2, half, cols), lambda j, y: (0, 0, j)),
                pl.BlockSpec((2, half // 2, cols), lambda j, y: (0, 0, j)),
                pl.BlockSpec((2, half // 2, cols), lambda j, y: (0, 0, j)),
                pl.BlockSpec((1, cols), lambda j, y: (0, j)),
            ],
            scratch_shapes=[pltpu.VMEM((rows, cols), BF), pltpu.VMEM((rows, cols), BF)],
        ),
        out_shape=[
            shape((rows, width), F32),
            shape((rows, width), F32),
            shape((2, half, units), F32),
            shape((2, half // 2, units), BF),
            shape((2, half // 2, units), BF),
            shape((1, units), F32),
        ],
        compiler_params=params(60),
        cost_estimate=cost(
            12 * rows * width * units, rows * width * 16 + width * units * 10, rows * units
        ),
    )(pick, hidden, grad, hidden_turned, grad_turned, weights, weights, bias)


def back_two_kernel(
    side, tok_ref, dy_ref, branch_ref, two_a, two_b, b_ref, back_a, back_b, w_own, w_other, hot_ref,
    turn_ref, parts_ref, first, second, half_own, half_other, out_ref, middle_ref, a_first, a_second,
    a_own, a_other, sums_ref, gb_ref, mine_ref, theirs_ref, outer_ref,
):
    width = tok_ref.shape[1]
    hot = hot_ref[...]
    turn = turn_ref[...]
    gate = rows_by_columns(hot, parts_ref[0, :, 2 * width :])
    mod = rows_by_columns(hot, parts_ref[1])
    branch = branch_ref[...]
    middle = tok_ref[...].astype(F32) + gate * branch
    branch_two = two_a[...] + two_b[...] + b_ref[...]
    grad_hidden = back_a[...] + back_b[...]
    dy = dy_ref[...].astype(F32)
    out_ref[...] = (middle + mod[:, 2 * width :] * branch_two).astype(BF)
    normed, inverse = layer_norm(middle)
    grad_middle = dy + norm_back(normed, inverse, grad_hidden * (1.0 + mod[:, width : 2 * width]))
    middle_ref[...] = grad_middle
    grad = (grad_middle * gate).astype(BF)
    turned = grad.astype(F32).T.astype(BF)
    att = third_of(first, second, half_own, half_other, pl.program_id(0), pl.num_programs(0) // 3)
    for k in range(2):
        product = rows_by_columns(turned, att[k])

        @pl.when(pl.program_id(0) == 0)
        def _():
            outer_ref[k] = product

        @pl.when(pl.program_id(0) != 0)
        def _():
            outer_ref[k] += product

    @pl.when(pl.program_id(0) == pl.num_programs(0) - 1)
    def _():
        ring = side.shape[0] // 2
        piece = width // ring
        for k in range(2):
            pieces = [
                outer_ref[k, pl.ds(pl.multiple_of(side[1 + ring + j] * piece, 8), piece)]
                for j in range(ring)
            ]
            mine_ref[k] = jnp.concatenate(pieces[: ring // 2], axis=0)
            theirs_ref[k] = jnp.concatenate(pieces[ring // 2 :], axis=0).astype(BF)

    skip = w_own.shape[2] - width // 2
    ours = padded_columns([rows_by_columns(grad, w_own[0, :, skip:]).astype(BF)], a_own.shape[2])
    theirs = padded_columns([rows_by_columns(grad, w_other[0, :, skip:]).astype(BF)], a_own.shape[2])
    i = pl.program_id(0)
    per = pl.num_programs(0) // 3
    for k, ref in enumerate((a_first, a_second)):

        @pl.when(i // per == k)
        def _(ref=ref):
            ref[0] = ours
            ref[1] = theirs

    @pl.when(i // per == 2)
    def _():
        a_own[0] = ours
        a_other[0] = theirs

    sums = [
        image_sums(turn, grad_middle * branch),
        image_sums(turn, grad_hidden),
        image_sums(turn, grad_hidden * normed),
        image_sums(turn, dy * branch_two),
    ]
    add_up(sums_ref, jnp.stack(sums, axis=0))
    add_up(gb_ref, jnp.sum(grad.astype(F32), axis=0, keepdims=True))


def back_two(
    side, tokens, cotangent, branch, two_a, two_b, b_down, back_a, back_b, weights, hot, turn, parts,
    attended, block, images, out_width,
):
    rows, width = tokens.shape
    third = rows // 3
    per = rows // 3 // block
    spec = lambda dims: pl.BlockSpec(dims, lambda i, y: (0,) * len(dims))
    placed = pl.BlockSpec(
        (block, width), lambda i, y: (((i // per + y[0]) % 3) * per + i % per, 0)
    )
    plain = pl.BlockSpec((block, width), lambda i, y: (i, 0))
    return pl.pallas_call(
        back_two_kernel,
        grid_spec=pltpu.PrefetchScalarGridSpec(
            num_scalar_prefetch=1,
            grid=(rows // block,),
            in_specs=[
                placed,
                placed,
                plain,
                plain,
                plain,
                spec((1, width)),
                plain,
                plain,
                *out_weight_specs(width, weights.shape[2]),
                pl.BlockSpec((block, hot.shape[1]), lambda i, y: (i, 0)),
                pl.BlockSpec((images, block), lambda i, y: (0, i)),
                spec(parts.shape),
                *third_specs(block, out_width, per),
            ],
            out_specs=[
                placed,
                plain,
                *third_specs(block, out_width, per),
                spec((4, images, width)),
                spec((1, width)),
                spec((2, width // 2, out_width)),
                spec((2, width // 2, out_width)),
            ],
            scratch_shapes=[pltpu.VMEM((2, width, out_width), F32)],
        ),
        out_shape=[
            shape((rows, width), BF),
            shape((rows, width), F32),
            *[shape((2, third, out_width), BF)] * 2,
            *[shape((1, third, out_width), BF)] * 2,
            shape((4, images, width), F32),
            shape((1, width), F32),
            shape((2, width // 2, out_width), F32),
            shape((2, width // 2, out_width), BF),
        ],
        compiler_params=params(62),
        cost_estimate=cost(2 * rows * width * (4 * width + 1024), rows * width * 34),
    )(side, tokens, cotangent, branch, two_a, two_b, b_down, back_a, back_b, weights, weights, hot, turn, parts, *attended)


def outer_kernel(ht_ref, first, second, rest, mine_ref, theirs_ref, sums_ref):
    third = first.shape[1]
    grads = (first[0], second[0], rest[0])
    found = sum(
        rows_by_columns(ht_ref[:, k * third : (k + 1) * third], grad)
        for k, grad in enumerate(grads)
    )

    @pl.when(pl.program_id(0) == 0)
    def _():
        theirs_ref[...] = found.astype(BF)
        sums_ref[...] = sum(jnp.sum(grad.astype(F32), axis=0, keepdims=True) for grad in grads)

    @pl.when(pl.program_id(0) == 1)
    def _():
        mine_ref[...] = found


def outer(turned, first, second, rest, group):
    width, rows = turned.shape
    _, third, cols = first.shape
    block = pl.BlockSpec((width // 2, cols), lambda k: (0, 0))
    pair = pl.BlockSpec((1, third, cols), lambda k: (group, 0, 0))
    single = pl.BlockSpec((1, third, cols), lambda k: (0, 0, 0))
    return pl.pallas_call(
        outer_kernel,
        grid=(2,),
        in_specs=[pl.BlockSpec((width // 2, rows), lambda k: (1 - k, 0)), pair, pair, single],
        out_specs=[block, block, pl.BlockSpec((1, cols), lambda k: (0, 0))],
        out_shape=[shape((width // 2, cols), F32), shape((width // 2, cols), BF), shape((1, cols), F32)],
        compiler_params=params(60),
        cost_estimate=cost(2 * rows * width * cols, rows * width * 2 + rows * cols * 4),
    )(turned, first, second, rest)


def back_one_kernel(
    side, first, second, own, other, w_own, w_other, tok_ref, middle_ref, hot_ref, turn_ref, parts_ref,
    out_ref, sums_ref,
):
    width = tok_ref.shape[1]
    cols = 3 * width // 2
    scale = rows_by_columns(hot_ref[...], parts_ref[0, :, width : 2 * width])
    grads = third_of(first, second, own, other, pl.program_id(0), pl.num_programs(0) // 3)[:, :, :cols]
    grad_hidden = contract_last(grads[0], w_own[0, :, :cols]) + contract_last(
        grads[1], w_other[0, :, :cols]
    )
    normed, inverse = layer_norm(tok_ref[...].astype(F32))
    out_ref[...] = middle_ref[...] + norm_back(normed, inverse, grad_hidden * (1.0 + scale))
    turn = turn_ref[...]
    sums = [image_sums(turn, grad_hidden), image_sums(turn, grad_hidden * normed)]
    add_up(sums_ref, jnp.stack(sums, axis=0))


def back_one(side, thirds, weights, tokens, middle, hot, turn, parts, block, images):
    rows, width = tokens.shape
    cols = thirds[0].shape[2]
    per = rows // 3 // block
    spec = lambda dims: pl.BlockSpec(dims, lambda i, y: (0,) * len(dims))
    once = pl.Buffered(1)
    placed = pl.BlockSpec(
        (block, width), lambda i, y: (((i // per + y[0]) % 3) * per + i % per, 0)
    )
    return pl.pallas_call(
        back_one_kernel,
        grid_spec=pltpu.PrefetchScalarGridSpec(
            num_scalar_prefetch=1,
            grid=(rows // block,),
            in_specs=[
                *third_specs(block, cols, per),
                pl.BlockSpec(
                    (1,) + weights.shape[1:], lambda i, y: (y[0], 0, 0), pipeline_mode=once
                ),
                pl.BlockSpec(
                    (1,) + weights.shape[1:], lambda i, y: (1 - y[0], 0, 0), pipeline_mode=once
                ),
                placed,
                pl.BlockSpec((block, width), lambda i, y: (i, 0)),
                pl.BlockSpec((block, hot.shape[1]), lambda i, y: (i, 0)),
                pl.BlockSpec((images, block), lambda i, y: (0, i)),
                spec(parts.shape),
            ],
            out_specs=[placed, spec((2, images, width))],
        ),
        out_shape=[shape((rows, width), F32), shape((2, images, width), F32)],
        compiler_params=params(),
        cost_estimate=cost(4 * rows * width * cols, rows * width * 10 + rows * cols * 4),
    )(side, *thirds, weights, weights, tokens, middle, hot, turn, parts)


def fast_body(mesh):
    ring = mesh.shape["rows"]
    both = ("rows", "heads")

    def moves(row_of, other_heads):
        pairs = []
        for r in range(ring):
            for y in range(2):
                pairs.append((2 * r + y, 2 * row_of(r) + (1 - y if other_heads else y)))
        return pairs

    to_core = moves(lambda r: r ^ 1, False)
    to_heads = moves(lambda r: r, True)
    to_x = moves(lambda r: r ^ 2, False)
    to_corner = moves(lambda r: r ^ 2, True)
    levels = ring // 4
    to_level = [moves(lambda r, k=k: (r + 4 * k) % ring, False) for k in range(levels)]

    def send(values, pairs):
        return lax.ppermute(values, both, pairs)

    def after(*values):
        return lax.optimization_barrier(values)

    def body(
        tokens,
        condition,
        segment_ids,
        tile_mask,
        image_index,
        w_ada,
        b_ada,
        w_query,
        w_key,
        w_value,
        b_query,
        b_value,
        w_out,
        b_out,
        w_up,
        b_up,
        w_down,
        b_down,
        cotangent,
    ):
        y = lax.axis_index("heads")
        r = lax.axis_index("rows")
        rows, width = tokens.shape
        length = segment_ids.shape[1]
        third = rows // 3
        images = condition.shape[0]
        units = w_up.shape[1]
        cols = w_query.shape[1]

        tiles = length // TILE
        tile_of = jnp.arange(length, dtype=jnp.int32) // TILE
        slots = image_index.shape[1]

        def marks_of(seg, tiles_on):
            own_slot = seg[:, None] == jnp.arange(slots, dtype=jnp.int32)[None, :]
            on = (tiles_on > 0) | jnp.eye(tiles, dtype=bool)
            own_tile = tile_of[:, None] == jnp.arange(tiles, dtype=jnp.int32)[None, :]
            open_to = jnp.broadcast_to(on.T[:, None, :], (tiles, TILE, tiles)).reshape(length, tiles)
            ends = jnp.zeros((length, MARKS - slots - tiles), F32)
            query = jnp.concatenate([own_slot, own_tile, ends], axis=1).astype(BF)
            seen = jnp.concatenate([own_slot, open_to], axis=1)
            key = jnp.concatenate([jnp.where(seen, 0.0, MASKED_SCORE), ends + 1.0], axis=1).astype(BF)
            return query, key

        seg_full = lax.dynamic_index_in_dim(segment_ids, 2 * y, 0, keepdims=False)
        tile_full = lax.dynamic_index_in_dim(tile_mask, 2 * y, 0, keepdims=False)
        seg_half = jnp.where(y == 0, segment_ids[1], jnp.roll(segment_ids[1], -third))
        shift = third // TILE
        tile_half = jnp.where(
            y == 0, tile_mask[1], jnp.roll(tile_mask[1], (-shift, -shift), axis=(0, 1))
        )
        marks_full = marks_of(seg_full, tile_full)
        marks_half = marks_of(seg_half, tile_half)

        def image_of(seg, index):
            slot = jnp.arange(slots, dtype=jnp.int32)
            return jnp.sum(jnp.where(seg[:, None] == slot[None, :], index[None, :], 0), axis=1)

        own_image = jnp.concatenate(
            [
                image_of(seg_full, lax.dynamic_index_in_dim(image_index, 2 * y, 0, keepdims=False)),
                image_of(seg_half[:third], image_index[1]),
            ]
        )
        chosen = jnp.arange(images, dtype=jnp.int32)
        hot = (own_image[:, None] == jnp.tile(chosen, 3)[None, :]).astype(BF)
        turn = (chosen[:, None] == own_image[None, :]).astype(BF)

        order = jnp.arange(ring, dtype=jnp.int32)
        core_of, x_of, level_of = order // (ring // 2), (order // levels) % 2, order % levels
        owner = ((r // 4 + level_of) % levels) * 4 + ((r // 2 % 2) ^ x_of) * 2 + ((r % 2) ^ core_of)
        piece = width // ring
        place = jnp.sum(jnp.where(owner[None, :] == order[:, None], order[None, :], 0), axis=1)
        side = jnp.concatenate([y.reshape(1), place, owner])

        padded = -(-3 * cols // 128) * 128
        out_width = -(-cols // 128) * 128
        level, x_bit, core_bit = r // 4, (r // 2) % 2, r % 2
        next_level = to_level[levels - 1]

        def placed(bit, own, got):
            return jnp.where(bit == 0, jnp.stack([own, got]), jnp.stack([got, own]))

        def round_of(found):
            return lax.dynamic_slice_in_dim(
                jnp.stack(found + found), (levels - level) % levels, levels, axis=0
            )

        shard = jnp.concatenate([w_query, w_key, w_value, w_out], axis=1).astype(BF)
        count = shard.shape[1] // 3
        steps = [shard[:, : 2 * count]]
        last = shard[:, 2 * count :]
        cond = condition.astype(F32)
        mod_cols, got, last_got = after(
            jnp.dot(jax.nn.silu(cond), w_ada, precision=PRECISE) + b_ada,
            send(steps[0], next_level),
            send(last, to_x),
        )
        steps.append(got)
        last = placed(x_bit, last, last_got)
        biases = jnp.concatenate([b_up, b_query, b_value])[None]
        own_spread = jnp.concatenate([mod_cols, biases], axis=0)
        got_spread, got, last_got, hot, turn, side, *marks = after(
            send(own_spread, to_heads),
            send(steps[1], next_level),
            send(last, to_heads),
            hot,
            turn,
            side,
            *marks_full,
            *marks_half,
        )
        marks_full, marks_half = marks[:2], marks[2:]
        steps.append(got)
        last = [placed(y, last, last_got)]
        spread = placed(y, own_spread, got_spread)
        parts = three_parts(spread[:, :images])
        up_bias = spread[:, images:, :units]
        qkv_bias = jnp.concatenate(
            [
                spread[:, images:, units : units + cols],
                jnp.zeros((2, 1, cols), F32),
                spread[:, images:, units + cols :],
            ],
            axis=2,
        )
        hidden_full, hidden_half, hidden_one_turned, got, last_got = after(
            *first_norm(side, tokens, hot, parts, third),
            send(steps[2], next_level),
            send(last[0], next_level),
        )
        first = round_of([*steps, got])
        last.append(last_got)
        over_x, over_y = first[..., :count], first[..., count:]
        x_got, y_got, last_got = after(
            send(over_x, to_x), send(over_y, to_heads), send(last[1], next_level)
        )
        over_x, over_y = placed(x_bit, over_x, x_got), placed(y, over_y, y_got)
        last.append(last_got)
        hidden_got, x_got, y_got, last_got = after(
            send(hidden_half, to_heads),
            send(over_x, to_heads),
            send(over_y, to_x),
            send(last[2], next_level),
        )
        over_x, over_y = placed(y, over_x, x_got), placed(x_bit, over_y, y_got)
        last = round_of([*last, last_got])
        feed_shard = jnp.stack([w_up, w_down]).astype(BF)
        over_x, over_y, last, feed_shard = after(over_x, over_y, last, feed_shard)
        feed_weights = lax.all_gather(
            feed_shard, ("heads", "rows"), axis=1, tiled=True
        ).reshape(2, 2, width, units)
        x_got, y_got, last_got = after(
            send(over_x, to_core), send(over_y, to_core), send(last, to_core)
        )
        attention_weights = collected(
            core_bit.reshape(1), over_x, x_got, over_y, y_got, last, last_got
        ).reshape(2, width, shard.shape[1])

        qkv_first, qkv_second, qkv_own, qkv_got, *got = after(
            *project(
                side, hidden_full, hidden_half, hidden_got, attention_weights, qkv_bias, padded
            ),
            *(send(condition, to_level[k]) for k in range(1, levels)),
        )
        flat = jnp.stack([condition, *got])
        qkv_full = (qkv_first, qkv_second)
        qkv_half = (qkv_own, qkv_got)
        out_own, out_theirs, *lse_half, got = after(
            *attend(*qkv_half, *marks_half, out_width), send(flat, to_x)
        )
        flat = jnp.concatenate([flat, got], axis=0)
        qkv_first, out_theirs, flat = after(qkv_first, out_theirs, flat)
        out_first, out_second, *lse_full, out_other, got = after(
            *attend(qkv_first, qkv_second, *marks_full, out_width),
            send(out_theirs, to_heads),
            send(flat, to_core),
        )
        flat = jnp.concatenate([flat, got], axis=0)
        silu_all = jax.nn.silu(flat.reshape(ring * images, width).astype(F32))
        attended = (out_first, out_second, out_own, out_other)
        branch_one, hidden_two, grad_two, hidden_two_turned, grad_two_turned, grad_b_down = middle_part(
            side, tokens, cotangent, attended, attention_weights, b_out[None], hot, parts, third // 2
        )

        def added(mine, got):
            return mine + got.astype(F32)

        def level_pieces(values):
            part = lambda k: values[..., k * piece : (k + 1) * piece, :]
            return part(0), *(part(k).astype(BF) for k in range(1, levels))

        def all_added(kept, got):
            for part in got:
                kept = added(kept, part)
            return kept

        quarter = width // 4

        def plane_pieces(mine_own, got_own, mine_other, got_other):
            near = lambda mine, got: added(mine[:quarter], got[:quarter])
            far = lambda mine, got: added(mine[quarter:], got[quarter:]).astype(BF)
            return (
                near(mine_own, got_own),
                far(mine_own, got_own),
                near(mine_other, got_other).astype(BF),
                far(mine_other, got_other),
            )

        flat_turned = lambda values: values.reshape(width, rows)
        hidden_one_turned = flat_turned(hidden_one_turned)
        feed_args = (flat_turned(hidden_two_turned), flat_turned(grad_two_turned), feed_weights, up_bias, third, 768)
        two_b, back_b, mine_b, near_b, far_b, grad_b_up_b = feed(
            1 - y.reshape(1), hidden_two, grad_two, *feed_args
        )
        far_b = added(mine_b[:, quarter:], send(far_b, to_core)).astype(BF)
        hidden_two, far_b, near_b = after(hidden_two, far_b, near_b)
        two_a, back_a, mine_a, near_a, far_a, grad_b_up_a, near_b, far_b = after(
            *feed(y.reshape(1), hidden_two, grad_two, *feed_args),
            send(near_b, to_core),
            send(far_b, to_x),
        )
        over_b = added(added(mine_b[:, :quarter], near_b), far_b).astype(BF)
        far_a = added(mine_a[:, quarter:], send(far_a, to_core)).astype(BF)
        two_a, over_b, far_a, near_a = after(two_a, over_b, far_a, near_a)

        output, grad_middle, *grad_attended, sums_two, grad_b_out, out_mine, out_theirs_sum, over_b, far_a, near_a = after(
            *back_two(
                side, tokens, cotangent, branch_one, two_a, two_b, b_down[None], back_a, back_b, attention_weights,
                hot, turn, parts, attended, third // 2, images, out_width,
            ),
            send(over_b, to_heads),
            send(far_a, to_x),
            send(near_a, to_core),
        )
        grad_first, grad_second, grad_own, grad_theirs = grad_attended
        grad_other = send(grad_theirs, to_heads)
        out_got = send(out_theirs_sum, to_core)
        out_pieces = plane_pieces(out_mine[0], out_got[0], out_mine[1], out_got[1])
        feed_kept, *feed_sent = level_pieces(
            added(added(added(mine_a[:, :quarter], near_a), far_a), over_b)
        )
        grad_own, feed_kept, *joined = after(grad_own, feed_kept, *feed_sent, *out_pieces)
        feed_sent, out_pieces = joined[: levels - 1], joined[levels - 1 :]
        grad_qkv_own, grad_qkv_theirs = attend_back(
            *qkv_half, grad_own, grad_other, *lse_half, *marks_half
        )
        grad_first, grad_qkv_theirs, feed_kept, *joined = after(
            grad_first, grad_qkv_theirs, feed_kept, *feed_sent, *out_pieces
        )
        feed_sent, out_pieces = joined[: levels - 1], joined[levels - 1 :]
        grad_qkv_first, grad_qkv_second, grad_qkv_other, *got = after(
            *attend_back(*qkv_full, grad_first, grad_second, *lse_full, *marks_full),
            send(grad_qkv_theirs, to_heads),
            *(send(part, to_level[k + 1]) for k, part in enumerate(feed_sent)),
        )
        grad_w_up, grad_w_down = all_added(feed_kept, got)
        qkv_mine_b, qkv_theirs_b, grad_qkv_bias_b, *got = after(
            *outer(hidden_one_turned, grad_qkv_first, grad_qkv_second, grad_qkv_other, 1),
            send(out_pieces[1], to_x),
            send(out_pieces[2], to_heads),
            send(out_pieces[3], to_corner),
        )
        out_kept, *out_sent = level_pieces(all_added(out_pieces[0], got))
        hidden_one_turned, qkv_theirs_b, out_kept, *out_sent = after(
            hidden_one_turned, qkv_theirs_b, out_kept, *out_sent
        )
        qkv_mine_a, qkv_theirs_a, grad_qkv_bias_a, qkv_got_b, *got = after(
            *outer(hidden_one_turned, grad_qkv_first, grad_qkv_second, grad_qkv_own, 0),
            send(qkv_theirs_b, to_core),
            *(send(part, to_level[k + 1]) for k, part in enumerate(out_sent)),
        )
        grad_w_out = all_added(out_kept, got)
        near, *sent = plane_pieces(qkv_mine_a, send(qkv_theirs_a, to_core), qkv_mine_b, qkv_got_b)
        grad_middle, near, *sent = after(grad_middle, near, *sent)
        grad_qkv = (grad_qkv_first, grad_qkv_second, grad_qkv_own, grad_qkv_other)
        grad_tokens, sums_one, *got = after(
            *back_one(
                side, grad_qkv, attention_weights, tokens, grad_middle, hot, turn, parts, third // 2, images
            ),
            send(sent[0], to_x),
            send(sent[1], to_heads),
            send(sent[2], to_corner),
        )
        qkv_kept, *qkv_sent = level_pieces(all_added(near, got))

        sums = jnp.concatenate([sums_one, sums_two], axis=0).reshape(2, 3, images, width)
        sums = sums.transpose(0, 2, 1, 3).reshape(2, images, 3 * width)
        narrow = jnp.concatenate([grad_b_out, grad_b_down], axis=0).reshape(2, 2, cols)

        def packet(which, up_sum, qkv_sum):
            second = lax.dynamic_index_in_dim(narrow, which, 1, keepdims=False).reshape(-1)
            short = [up_sum[0], qkv_sum[:cols], qkv_sum[2 * cols : 3 * cols], second]
            short = jnp.concatenate(short).reshape(images, -1)
            chunk = lax.dynamic_index_in_dim(sums, which, 0, keepdims=False)
            gap = -(chunk.shape[1] + short.shape[1]) % 128
            return jnp.concatenate([chunk, short, jnp.zeros((images, gap), F32)], axis=1)

        own_packet = packet(y, grad_b_up_a, grad_qkv_bias_a[0]) + send(
            packet(1 - y, grad_b_up_b, grad_qkv_bias_b[0]), to_heads
        )
        own_packet, qkv_kept, *qkv_sent = after(own_packet, qkv_kept, *qkv_sent)
        grad_silu = lax.dot_general(
            own_packet[:, : 3 * width],
            w_ada,
            (((1,), (1,)), ((), ())),
            precision=PRECISE,
            preferred_element_type=F32,
        )
        grad_silu, *got = after(
            grad_silu, *(send(own_packet, to_level[k]) for k in range(1, levels))
        )
        flat = jnp.concatenate([own_packet, *got], axis=0)
        flat, *qkv_sent = after(flat, *qkv_sent)
        silu_got, flat_got, *got = after(
            send(grad_silu, to_heads),
            send(flat, to_x),
            *(send(part, to_level[k + 1]) for k, part in enumerate(qkv_sent)),
        )
        grad_w_qkv = all_added(qkv_kept, got)
        flat = jnp.concatenate([flat, flat_got], axis=0)
        packets = jnp.concatenate([flat, send(flat, to_core)], axis=0)
        grad_mod = packets[:, : 3 * width]
        count = units + 4 * cols
        short = packets[:, 3 * width : 3 * width + count // images]
        bias_sums = jnp.sum(short.reshape(ring, images, count // images), axis=0).reshape(-1)
        s1, s2, _ = jnp.split(three_parts(silu_all), 3, axis=0)
        g1, g2, _ = jnp.split(three_parts(grad_mod), 3, axis=0)
        grad_w_ada = contract_first(
            jnp.concatenate([s1, s1, s2], axis=0), jnp.concatenate([g1, g2, g1], axis=0)
        )
        grad_b_ada = jnp.sum(grad_mod, axis=0)
        grad_silu = grad_silu + silu_got
        _, silu_back = jax.vjp(jax.nn.silu, cond)
        grad_condition = silu_back(grad_silu)[0]
        return (
            output,
            grad_tokens,
            grad_condition,
            grad_w_ada,
            grad_b_ada,
            grad_w_qkv[:, :cols],
            grad_w_qkv[:, cols : 2 * cols],
            grad_w_qkv[:, 2 * cols : 3 * cols],
            bias_sums[units : units + cols],
            bias_sums[units + cols : units + 2 * cols],
            grad_w_out[:, :cols],
            bias_sums[units + 2 * cols : units + 3 * cols],
            grad_w_up,
            bias_sums[:units],
            grad_w_down,
            bias_sums[units + 3 * cols :],
        )

    return body


def solution(mesh):
    body = fast_body(mesh) if mesh.shape["heads"] == 2 and mesh.shape["rows"] == 16 else general_body
    placed = (
        P(("rows", "heads"), None),
        P("rows", None),
        P("rows", None),
        P("rows", None, None),
        P("rows", None),
        P(None, "heads"),
        P("heads"),
        P("rows", "heads"),
        P("rows", "heads"),
        P("rows", "heads"),
        P("heads"),
        P("heads"),
        P("rows", "heads"),
        P(),
        P("rows", "heads"),
        P("heads"),
        P("rows", "heads"),
        P(),
        P(("rows", "heads"), None),
    )
    return jax.shard_map(
        body,
        mesh=mesh,
        in_specs=placed,
        out_specs=(
            P(("rows", "heads"), None),
            P(("rows", "heads"), None),
            P("rows", None),
            P(None, "heads"),
            P("heads"),
            P("rows", "heads"),
            P("rows", "heads"),
            P("rows", "heads"),
            P("heads"),
            P("heads"),
            P("rows", "heads"),
            P("heads"),
            P("rows", "heads"),
            P("heads"),
            P("rows", "heads"),
            P("heads"),
        ),
        check_vma=False,
    )
```

```python
from functools import partial

import jax
import jax.numpy as jnp
from jax import lax
from jax.experimental import pallas as pl
from jax.experimental.pallas import tpu as pltpu
from jax.sharding import PartitionSpec as P

HEAD_DIM = 72
TILE = 128


EPSILON = 1e-06
MASKED_SCORE = -1e30
PRECISE = lax.Precision.HIGHEST


def layer_norm(values):
    centred = values - jnp.mean(values, axis=-1, keepdims=True)
    inverse = lax.rsqrt(jnp.mean(centred * centred, axis=-1, keepdims=True) + EPSILON)
    return (centred * inverse, inverse)


def norm_back(normed, inverse, grad):
    return inverse * (
        grad
        - jnp.mean(grad, axis=-1, keepdims=True)
        - normed * jnp.mean(grad * normed, axis=-1, keepdims=True)
    )


def contract_last(left, right):
    return lax.dot_general(
        left, right, (((1,), (1,)), ((), ())), preferred_element_type=jnp.float32
    )


def contract_first(left, right):
    return lax.dot_general(
        left, right, (((0,), (0,)), ((), ())), preferred_element_type=jnp.float32
    )


def general_body(
    tokens,
    condition,
    segment_ids,
    tile_mask,
    image_index,
    w_ada,
    b_ada,
    w_query,
    w_key,
    w_value,
    b_query,
    b_value,
    w_out,
    b_out,
    w_up,
    b_up,
    w_down,
    b_down,
    cotangent,
):
    scaling = HEAD_DIM ** (-0.5)
    own_rows = tokens.shape[0]
    seq_count = segment_ids.shape[0]
    length = segment_ids.shape[1]
    group_rows = seq_count * length
    own_start = lax.axis_index("heads") * own_rows
    img_count = condition.shape[0]
    slot_count = image_index.shape[1]
    local_heads = w_query.shape[1] // HEAD_DIM
    block_rows = min(512, length)
    tile_count = length // TILE
    bfloat = jnp.bfloat16
    own_segments = lax.dynamic_slice_in_dim(segment_ids.reshape(group_rows), own_start, own_rows)
    own_seqs = (own_start + jnp.arange(own_rows, dtype=jnp.int32)) // length
    seq_match = own_seqs[:, None] == jnp.arange(seq_count, dtype=jnp.int32)[None, :]
    slot_match = own_segments[:, None] == jnp.arange(slot_count, dtype=jnp.int32)[None, :]
    own_image = jnp.sum(
        jnp.where(seq_match[:, :, None] & slot_match[:, None, :], image_index[None, :, :], 0),
        axis=(1, 2),
    )
    image_onehot = (own_image[:, None] == jnp.arange(img_count, dtype=jnp.int32)[None, :]).astype(
        jnp.float32
    )
    cond_full = condition.astype(jnp.float32)
    silu_cond = jax.nn.silu(cond_full)
    mod_cols = jnp.dot(silu_cond, w_ada, precision=PRECISE) + b_ada
    mod_full, up_bias_all = (
        lax.all_gather(mod_cols, "heads", axis=1, tiled=True),
        lax.all_gather(b_up.reshape(1, -1), "heads", axis=1, tiled=True),
    )
    per_token = jnp.dot(image_onehot, mod_full, precision=PRECISE)
    shift_one, scale_one, gate_one, shift_two, scale_two, gate_two = jnp.split(per_token, 6, axis=1)

    def gather_weights():
        return (
            lax.all_gather(w_query.astype(bfloat), "rows", axis=0, tiled=True),
            lax.all_gather(w_key.astype(bfloat), "rows", axis=0, tiled=True),
            lax.all_gather(w_value.astype(bfloat), "rows", axis=0, tiled=True),
            lax.all_gather(w_out.astype(bfloat), "rows", axis=0, tiled=True),
            lax.all_gather(w_up.astype(bfloat), "rows", axis=0, tiled=True),
            lax.all_gather(w_down.astype(bfloat), "rows", axis=0, tiled=True),
        )

    def spread_first(values):
        return lax.all_gather(values, "heads", axis=0, tiled=True)

    query_full, key_full, value_full, out_full, up_full, down_full = gather_weights()
    token_full = tokens.astype(jnp.float32)
    normed_one, inverse_one = layer_norm(token_full)
    hidden_own_one = (normed_one * (1.0 + scale_one) + shift_one).astype(bfloat)
    hidden_one = spread_first(hidden_own_one)
    head_shape = (group_rows, local_heads, HEAD_DIM)
    query_heads = (
        (jnp.dot(hidden_one, query_full, preferred_element_type=jnp.float32) + b_query)
        .astype(bfloat)
        .reshape(head_shape)
    )
    key_heads = (
        jnp.dot(hidden_one, key_full, preferred_element_type=jnp.float32)
        .astype(bfloat)
        .reshape(head_shape)
    )
    value_heads = (
        (jnp.dot(hidden_one, value_full, preferred_element_type=jnp.float32) + b_value)
        .astype(bfloat)
        .reshape(head_shape)
    )
    tile_of = jnp.arange(length, dtype=jnp.int32) // TILE

    def scores_for(seq_index, block_start):
        seq_start = seq_index * length
        block_query = query_heads[seq_start + block_start : seq_start + block_start + block_rows]
        seq_keys = key_heads[seq_start : seq_start + length]
        block_tiles = tile_mask[seq_index][block_start // TILE : (block_start + block_rows) // TILE]
        expanded = jnp.broadcast_to(
            block_tiles[:, None, :, None], (block_rows // TILE, TILE, tile_count, TILE)
        ).reshape(block_rows, length)
        seg_row = segment_ids[seq_index]
        same_image = seg_row[block_start : block_start + block_rows][:, None] == seg_row[None, :]
        diagonal = tile_of[block_start : block_start + block_rows][:, None] == tile_of[None, :]
        allowed = same_image & ((expanded > 0) | diagonal)
        raw = (
            jnp.einsum("qhd,khd->hqk", block_query, seq_keys, preferred_element_type=jnp.float32)
            * scaling
        )
        return (jnp.where(allowed[None], raw, MASKED_SCORE), block_query, seq_keys)

    attended_parts = []
    log_totals = []
    for seq_index in range(seq_count):
        seq_values = value_heads[seq_index * length : (seq_index + 1) * length]
        for block_start in range(0, length, block_rows):
            scores, block_query, seq_keys = scores_for(seq_index, block_start)
            top_score = jnp.max(scores, axis=-1, keepdims=True)
            log_total = top_score + jnp.log(
                jnp.sum(jnp.exp(scores - top_score), axis=-1, keepdims=True)
            )
            probs_low = jnp.exp(scores - log_total).astype(bfloat)
            attended_parts.append(
                jnp.einsum(
                    "hqk,khd->qhd", probs_low, seq_values, preferred_element_type=jnp.float32
                )
            )
            log_totals.append(log_total)
    attended = (
        jnp.concatenate(attended_parts, axis=0)
        .reshape(group_rows, local_heads * HEAD_DIM)
        .astype(bfloat)
    )
    branch_one = (
        lax.psum_scatter(
            contract_last(attended, out_full), "heads", scatter_dimension=0, tiled=True
        )
        + b_out
    )
    middle = token_full + gate_one * branch_one
    normed_two, inverse_two = layer_norm(middle)
    hidden_own_two = (normed_two * (1.0 + scale_two) + shift_two).astype(bfloat)
    up_all, down_all = (
        lax.all_gather(up_full, "heads", axis=1, tiled=True),
        lax.all_gather(down_full, "heads", axis=1, tiled=True),
    )
    pre_act = jnp.dot(hidden_own_two, up_all, preferred_element_type=jnp.float32) + up_bias_all[0]
    activated = jax.nn.gelu(pre_act, approximate=True).astype(bfloat)
    branch_two = contract_last(activated, down_all) + b_down
    output = (middle + gate_two * branch_two).astype(bfloat)
    query_back, key_back, value_back, out_back, up_back, down_back = gather_weights()
    hidden_one_back = spread_first(hidden_own_one)
    grad_out = cotangent.astype(jnp.float32)
    grad_branch_two = (grad_out * gate_two).astype(bfloat)
    grad_gate_two = grad_out * branch_two
    grad_down_all = contract_first(grad_branch_two, activated)
    grad_act = jnp.dot(grad_branch_two, down_all, preferred_element_type=jnp.float32)
    _, gelu_back = jax.vjp(partial(jax.nn.gelu, approximate=True), pre_act)
    grad_pre = gelu_back(grad_act)[0].astype(bfloat)
    grad_up_all = contract_first(hidden_own_two, grad_pre)
    grad_bias_all = jnp.sum(grad_pre, axis=0, dtype=jnp.float32).reshape(1, -1)
    grad_hidden_two = contract_last(grad_pre, up_all)
    grad_w_up, grad_w_down, grad_bias_cols = (
        lax.psum_scatter(grad_up_all, "heads", scatter_dimension=1, tiled=True),
        lax.psum_scatter(grad_down_all, "heads", scatter_dimension=1, tiled=True),
        lax.psum_scatter(grad_bias_all, "heads", scatter_dimension=1, tiled=True),
    )
    grad_b_up = grad_bias_cols[0]
    grad_scale_two = grad_hidden_two * normed_two
    grad_middle = grad_out + norm_back(normed_two, inverse_two, grad_hidden_two * (1.0 + scale_two))
    grad_branch_one = (grad_middle * gate_one).astype(bfloat)
    grad_gate_one = grad_middle * branch_one
    grad_one_full = lax.all_gather(grad_branch_one, "heads", axis=0, tiled=True)
    grad_w_out = contract_first(grad_one_full, attended)
    grad_attended = (
        jnp.dot(grad_one_full, out_back, preferred_element_type=jnp.float32)
        .astype(bfloat)
        .reshape(head_shape)
    )
    grad_query_parts = []
    grad_key_parts = []
    grad_value_parts = []
    block_number = 0
    for seq_index in range(seq_count):
        seq_start = seq_index * length
        seq_values = value_heads[seq_start : seq_start + length]
        key_total = jnp.zeros((length, local_heads, HEAD_DIM), jnp.float32)
        value_total = jnp.zeros((length, local_heads, HEAD_DIM), jnp.float32)
        for block_start in range(0, length, block_rows):
            scores, block_query, seq_keys = scores_for(seq_index, block_start)
            probs = jnp.exp(scores - log_totals[block_number])
            block_number += 1
            grad_block = grad_attended[
                seq_start + block_start : seq_start + block_start + block_rows
            ]
            grad_probs = jnp.einsum(
                "qhd,khd->hqk", grad_block, seq_values, preferred_element_type=jnp.float32
            )
            centre = jnp.sum(probs * grad_probs, axis=-1, keepdims=True)
            grad_scores = (probs * (grad_probs - centre)).astype(bfloat)
            grad_query_parts.append(
                (
                    jnp.einsum(
                        "hqk,khd->qhd", grad_scores, seq_keys, preferred_element_type=jnp.float32
                    )
                    * scaling
                ).astype(bfloat)
            )
            key_total = (
                key_total
                + jnp.einsum(
                    "hqk,qhd->khd", grad_scores, block_query, preferred_element_type=jnp.float32
                )
                * scaling
            )
            value_total = value_total + jnp.einsum(
                "hqk,qhd->khd", probs.astype(bfloat), grad_block, preferred_element_type=jnp.float32
            )
        grad_key_parts.append(key_total.astype(bfloat))
        grad_value_parts.append(value_total.astype(bfloat))
    flat_shape = (group_rows, local_heads * HEAD_DIM)
    grad_queries = jnp.concatenate(grad_query_parts, axis=0).reshape(flat_shape)
    grad_keys = jnp.concatenate(grad_key_parts, axis=0).reshape(flat_shape)
    grad_values = jnp.concatenate(grad_value_parts, axis=0).reshape(flat_shape)
    grad_w_query = contract_first(hidden_one_back, grad_queries)
    grad_w_key = contract_first(hidden_one_back, grad_keys)
    grad_w_value = contract_first(hidden_one_back, grad_values)
    grad_b_query = jnp.sum(grad_queries, axis=0, dtype=jnp.float32)
    grad_b_value = jnp.sum(grad_values, axis=0, dtype=jnp.float32)
    total = contract_last(grad_queries, query_back)
    total = total + contract_last(grad_keys, key_back)
    grad_hidden_one = lax.psum_scatter(
        total + contract_last(grad_values, value_back), "heads", scatter_dimension=0, tiled=True
    )
    grad_scale_one = grad_hidden_one * normed_one
    grad_tokens = grad_middle + norm_back(
        normed_one, inverse_one, grad_hidden_one * (1.0 + scale_one)
    )
    grad_mod_tokens = jnp.concatenate(
        [
            grad_hidden_one,
            grad_scale_one,
            grad_gate_one,
            grad_hidden_two,
            grad_scale_two,
            grad_gate_two,
        ],
        axis=1,
    )
    grad_mod_images = lax.dot_general(
        image_onehot,
        grad_mod_tokens,
        (((0,), (0,)), ((), ())),
        precision=PRECISE,
        preferred_element_type=jnp.float32,
    )
    bias_parts = jnp.stack(
        [
            jnp.sum(grad_branch_one, axis=0, dtype=jnp.float32),
            jnp.sum(grad_branch_two, axis=0, dtype=jnp.float32),
        ],
        axis=0,
    )
    grad_mod_cols, bias_cols = (
        lax.psum_scatter(grad_mod_images, "heads", scatter_dimension=1, tiled=True),
        lax.psum_scatter(bias_parts, "heads", scatter_dimension=1, tiled=True),
    )
    grad_w_ada = lax.dot_general(
        silu_cond,
        grad_mod_cols,
        (((0,), (0,)), ((), ())),
        precision=PRECISE,
        preferred_element_type=jnp.float32,
    )
    grad_b_ada = jnp.sum(grad_mod_cols, axis=0)
    grad_silu = lax.dot_general(
        grad_mod_cols,
        w_ada,
        (((1,), (1,)), ((), ())),
        precision=PRECISE,
        preferred_element_type=jnp.float32,
    )
    grad_silu = lax.psum(grad_silu, "heads")
    _, silu_back = jax.vjp(jax.nn.silu, cond_full)
    grad_condition = silu_back(grad_silu)[0]
    grad_w_ada, grad_b_ada, grad_b_query, grad_b_value, grad_b_up, bias_cols = lax.psum(
        (grad_w_ada, grad_b_ada, grad_b_query, grad_b_value, grad_b_up, bias_cols), "rows"
    )
    grad_w_query, grad_w_key, grad_w_value, grad_w_out, grad_w_up, grad_w_down = (
        lax.psum_scatter(grad_w_query, "rows", scatter_dimension=0, tiled=True),
        lax.psum_scatter(grad_w_key, "rows", scatter_dimension=0, tiled=True),
        lax.psum_scatter(grad_w_value, "rows", scatter_dimension=0, tiled=True),
        lax.psum_scatter(grad_w_out, "rows", scatter_dimension=0, tiled=True),
        lax.psum_scatter(grad_w_up, "rows", scatter_dimension=0, tiled=True),
        lax.psum_scatter(grad_w_down, "rows", scatter_dimension=0, tiled=True),
    )
    return (
        output,
        grad_tokens,
        grad_condition,
        grad_w_ada,
        grad_b_ada,
        grad_w_query,
        grad_w_key,
        grad_w_value,
        grad_b_query,
        grad_b_value,
        grad_w_out,
        bias_cols[0],
        grad_w_up,
        grad_b_up,
        grad_w_down,
        bias_cols[1],
    )


LOG2E = 1.4426950408889634
GELU_SLOPE = 0.7978845608028654
GELU_CUBE = 0.044715
BF = jnp.bfloat16
F32 = jnp.float32
MIB = 2**20


def rows_by_columns(left, right):
    return jnp.dot(left, right, preferred_element_type=F32)


def shape(dims, dtype):
    return jax.ShapeDtypeStruct(dims, dtype)


def params(mib=56):
    return pltpu.CompilerParams(vmem_limit_bytes=mib * MIB)


def cost(flops, bytes_accessed, transcendentals=0):
    return pl.CostEstimate(
        flops=int(flops), bytes_accessed=int(bytes_accessed), transcendentals=int(transcendentals)
    )


def three_parts(values):
    high = lax.reduce_precision(values, 8, 7)
    rest = values - high
    middle = lax.reduce_precision(rest, 8, 7)
    return jnp.concatenate([high, middle, rest - middle], axis=-2).astype(BF)


def collect_kernel(here, *refs):
    sources, whole, sems = refs[:10], refs[10], refs[11]
    levels, xs = whole.shape[2:4]
    count = sources[0].shape[-1]
    y, level, x, core = (here[k] for k in range(4))
    flip = lambda bit, other: bit + other - 2 * bit * other
    copies = []
    for dc in range(2):
        x_near, x_far, y_near, y_far, last = sources[5 * dc : 5 * dc + 5]
        for dz in range(levels):
            for i in range(2):
                for j in range(2):
                    at = (flip(y, i), lax.rem(level + dz, levels), flip(x, j), flip(core, dc))
                    found = (
                        (x_near, x_far)[i].at[j, dz],
                        (y_near, y_far)[j].at[i, dz],
                        last.at[dz, i, j],
                    )
                    for k, source in enumerate(found):
                        place = whole.at[(slice(None), *at, slice(None), pl.ds(k * count, count))]
                        copies.append(pltpu.make_async_copy(source, place, sems.at[len(copies)]))
                        copies[-1].start()
    for copy in copies:
        copy.wait()


def collected(here, sources):
    levels, heads, xs, parts, piece, count = sources[4].shape
    whole = (parts, heads, levels, xs, 2, piece, 3 * count)
    anywhere = pl.BlockSpec(memory_space=pl.ANY)
    return pl.pallas_call(
        collect_kernel,
        grid_spec=pltpu.PrefetchScalarGridSpec(
            num_scalar_prefetch=1,
            grid=(1,),
            in_specs=[anywhere] * 10,
            out_specs=anywhere,
            scratch_shapes=[pltpu.SemaphoreType.DMA((6 * heads * levels * xs,))],
        ),
        out_shape=shape(whole, BF),
        compiler_params=params(16),
        cost_estimate=cost(0, 24 * parts * heads * levels * xs * piece * count),
    )(here, *sources)


def turn_in_order(places, turned_ref, values):
    turned = values.astype(F32).T
    piece = turned_ref.shape[1]
    for k in range(turned_ref.shape[0]):
        turned_ref[places[1 + k]] = turned[k * piece : (k + 1) * piece].astype(BF)


def norm_kernel(side, tok_ref, hot_ref, parts_ref, h_ref, half_ref, ht_ref):
    width = tok_ref.shape[1]
    normed, _ = layer_norm(tok_ref[...].astype(F32))
    mod = rows_by_columns(hot_ref[...], parts_ref[0, :, : 2 * width])
    hidden = (normed * (1.0 + mod[:, width:]) + mod[:, :width]).astype(BF)
    turn_in_order(side, ht_ref, hidden)

    @pl.when(pl.program_id(0) < 2)
    def _():
        h_ref[...] = hidden

    @pl.when(pl.program_id(0) == 2)
    def _():
        half_ref[...] = hidden


def first_norm(side, tokens, hot, parts, block):
    ring = side.shape[0] // 2
    rows, width = tokens.shape
    return pl.pallas_call(
        norm_kernel,
        grid_spec=pltpu.PrefetchScalarGridSpec(
            num_scalar_prefetch=1,
            grid=(rows // block,),
            in_specs=[
                pl.BlockSpec((block, width), lambda i, y: ((i + y[0]) % 3, 0)),
                pl.BlockSpec((block, hot.shape[1]), lambda i, y: (i, 0)),
                pl.BlockSpec((1,) + parts.shape[1:], lambda i, y: (0, 0, 0)),
            ],
            out_specs=[
                pl.BlockSpec((block, width), lambda i, y: (jnp.minimum(i, 1), 0)),
                pl.BlockSpec((block, width), lambda i, y: (0, 0)),
                pl.BlockSpec((ring, width // ring, block), lambda i, y: (0, 0, i)),
            ],
        ),
        out_shape=[
            shape((2 * block, width), BF),
            shape((block, width), BF),
            shape((ring, width // ring, rows), BF),
        ],
        compiler_params=params(),
        cost_estimate=cost(2 * rows * width * (width + 512), rows * width * 6),
    )(side, tokens, hot, parts)


def project_kernel(side, first_in, second_in, w_ref, bias_ref, first, second):
    padded = first.shape[2]
    cols = bias_ref.shape[2]
    for hidden, ref in ((first_in, first), (second_in, second)):
        value = (rows_by_columns(hidden[...], w_ref[0, :, :cols]) + bias_ref[0]).astype(BF)
        ref[0] = jnp.concatenate([value, jnp.zeros((value.shape[0], padded - cols), BF)], axis=1)


def project(side, first, second, weights, bias, padded, block, groups):
    width = first.shape[1]
    pick = lambda a, y: a + y[0] - 2 * a * y[0]
    last = second.shape[0] // block - 1
    pair = pl.BlockSpec((1, block, padded), lambda a, y: (a, 0, 0))
    return pl.pallas_call(
        project_kernel,
        grid_spec=pltpu.PrefetchScalarGridSpec(
            num_scalar_prefetch=1,
            grid=(groups,),
            in_specs=[
                pl.BlockSpec((block, width), lambda a, y: (0, 0)),
                pl.BlockSpec((block, width), lambda a, y: (last, 0)),
                pl.BlockSpec((1,) + weights.shape[1:], lambda a, y: (pick(a, y), 0, 0)),
                pl.BlockSpec((1,) + bias.shape[1:], lambda a, y: (pick(a, y), 0, 0)),
            ],
            out_specs=[pair, pair],
        ),
        out_shape=[shape((groups, block, padded), BF)] * 2,
        compiler_params=params(60),
        cost_estimate=cost(
            4 * groups * block * width * padded, 4 * groups * (block + width) * padded
        ),
    )(side, first, second, weights, bias)


MARKS = 16
DEPTH = 128
LSE_AT = HEAD_DIM + MARKS - 4
STEEP = HEAD_DIM**-0.5 * LOG2E


def marks_kernel(*refs):
    count = len(refs) // 4
    for n in range(count):
        seg_ref, open_ref = refs[2 * n : 2 * n + 2]
        query_ref, key_ref = refs[2 * count + 2 * n : 2 * count + 2 * n + 2]
        tiles, length = open_ref.shape
        slots = MARKS - 4 - tiles
        slot = lax.broadcasted_iota(jnp.int32, (slots, length), 0)
        own_slot = slot == seg_ref[...]
        tile = lax.broadcasted_iota(jnp.int32, (tiles, length), 0)
        own_tile = tile == lax.broadcasted_iota(jnp.int32, (tiles, length), 1) // TILE
        seen = jnp.concatenate(
            [jnp.where(own_slot, 0.0, MASKED_SCORE), jnp.where(open_ref[...] > 0, 0.0, MASKED_SCORE)],
            axis=0,
        )
        chosen = jnp.concatenate(
            [jnp.where(own_slot, 1.0, 0.0), jnp.where(own_tile, 1.0, 0.0)], axis=0
        )
        rest = (MARKS - slots - tiles, length)
        query_ref[...] = jnp.concatenate([chosen, jnp.zeros(rest, F32)], axis=0).T.astype(BF)
        key_ref[...] = jnp.concatenate([seen, jnp.ones(rest, F32)], axis=0).T.astype(BF)


def marks_of(*rows):
    length = rows[1].shape[1]
    return pl.pallas_call(
        marks_kernel,
        out_shape=[shape((length, MARKS), BF)] * len(rows),
        compiler_params=params(16),
    )(*rows)


def split_three(values):
    high = values.astype(BF)
    rest = values - high.astype(F32)
    middle = rest.astype(BF)
    return jnp.concatenate([high, middle, (rest - middle.astype(F32)).astype(BF)], axis=1)


def at_head(h, part, heads):
    start = (part * heads + h) * HEAD_DIM
    return slice(start, start + HEAD_DIM)


def both_halves(first, second, columns):
    return jnp.concatenate([first[0, :, columns], second[0, :, columns]], axis=0)


def padded_columns(parts, width):
    found = jnp.concatenate(parts, axis=1)
    gap = width - found.shape[1]
    return jnp.concatenate([found, jnp.zeros((found.shape[0], gap), found.dtype)], axis=1)


def attend_kernel(
    heads, first, second, qm_ref, km_ref, o_first, o_second, l_first, l_second, keys, values, queries
):
    i = pl.program_id(1)

    @pl.when((i == 0) & (pl.program_id(0) == 0))
    def _():
        keys[...] = jnp.zeros_like(keys)
        queries[...] = jnp.zeros_like(queries)

    @pl.when(i == 0)
    def _():
        for h in range(heads):
            keys[h, :, :HEAD_DIM] = both_halves(first, second, at_head(h, 1, heads))
            keys[h, :, HEAD_DIM : HEAD_DIM + MARKS] = km_ref[...]
            value = both_halves(first, second, at_head(h, 2, heads))
            values[h] = value.astype(F32).T.astype(BF)

    for h in range(heads):
        columns = at_head(h, 0, heads)
        queries[h, :, :HEAD_DIM] = jnp.where(i == 0, first[0, :, columns], second[0, :, columns])
        queries[h, :, HEAD_DIM : HEAD_DIM + MARKS] = qm_ref[...]
    parts = []
    totals = []
    probs = None
    scores = contract_last(keys[0], queries[0])
    for h in range(heads):
        later = contract_last(keys[h + 1], queries[h + 1]) if h + 1 < heads else None
        top = jnp.max(scores, axis=0, keepdims=True)
        powers = jnp.exp2((scores - top) * STEEP)
        total = jnp.sum(powers, axis=0, keepdims=True)
        totals.append(top + jnp.log2(total) * (1.0 / STEEP))
        if h > 0:
            parts.append(rows_by_columns(values[h - 1], probs).T.astype(BF))
        probs = (powers * (1.0 / total)).astype(BF)
        scores = later
    parts.append(rows_by_columns(values[heads - 1], probs).T.astype(BF))
    out = padded_columns(parts, o_first.shape[2])
    log_totals = jnp.concatenate(totals, axis=0)

    @pl.when(i == 0)
    def _():
        o_first[0] = out
        l_first[0] = log_totals

    @pl.when(i == 1)
    def _():
        o_second[0] = out
        l_second[0] = log_totals


def attend(first, second, query_marks, key_marks, out_width):
    groups, half, padded = first.shape
    heads = out_width // HEAD_DIM
    pair = lambda *dims: pl.BlockSpec((1,) + dims, lambda a, i: (a, 0, 0))
    return pl.pallas_call(
        partial(attend_kernel, heads),
        grid=(groups, 2),
        in_specs=[
            pair(half, padded),
            pair(half, padded),
            pl.BlockSpec((half, MARKS), lambda a, i: (i, 0)),
            pl.BlockSpec((2 * half, MARKS), lambda a, i: (0, 0)),
        ],
        out_specs=[pair(half, out_width)] * 2 + [pair(heads, half)] * 2,
        out_shape=[shape((groups, half, out_width), BF)] * 2 + [shape((groups, heads, half), F32)] * 2,
        scratch_shapes=[
            pltpu.VMEM((heads, 2 * half, DEPTH), BF),
            pltpu.VMEM((heads, HEAD_DIM, 2 * half), BF),
            pltpu.VMEM((heads, half, DEPTH), BF),
        ],
        compiler_params=params(),
        cost_estimate=cost(groups * 15e9, groups * half * padded * 6, groups * heads * half * half),
    )(first, second, query_marks, key_marks)


def attend_back_kernel(
    heads, first, second, do_first, do_second, l_first, l_second, qm_ref, km_ref,
    out_first, out_second, keys, values, turned, queries, dk, dv,
):
    i = pl.program_id(1)
    half, padded = first.shape[1:]
    width = heads * HEAD_DIM
    scaling = HEAD_DIM**-0.5

    @pl.when((i == 0) & (pl.program_id(0) == 0))
    def _():
        keys[...] = jnp.zeros_like(keys)
        queries[...] = jnp.zeros_like(queries)

    @pl.when(i == 0)
    def _():
        for h in range(heads):
            key = both_halves(first, second, at_head(h, 1, heads))
            keys[h, :, :HEAD_DIM] = key
            keys[h, :, HEAD_DIM : HEAD_DIM + MARKS] = km_ref[...]
            turned[h] = key.astype(F32).T.astype(BF)
            values[h] = both_halves(first, second, at_head(h, 2, heads))
        dk[...] = jnp.zeros_like(dk)
        dv[...] = jnp.zeros_like(dv)

    log_totals = jnp.where(i == 0, l_first[0], l_second[0]).T
    plain = []
    for h in range(heads):
        columns = at_head(h, 0, heads)
        query = jnp.where(i == 0, first[0, :, columns], second[0, :, columns])
        grad = jnp.where(i == 0, do_first[0, :, columns], do_second[0, :, columns])
        queries[h, :, :HEAD_DIM] = query
        queries[h, :, HEAD_DIM : HEAD_DIM + MARKS] = qm_ref[...]
        queries[h, :, LSE_AT : LSE_AT + 3] = split_three(-log_totals[:, h : h + 1])
        plain.append((query, grad))

    def scores_of(h):
        return contract_last(keys[h], queries[h]), contract_last(values[h], plain[h][1])

    def finish(h, probs, grad_scores):
        query, grad = plain[h]
        dv[h] += rows_by_columns(probs, grad)
        dk[h] += rows_by_columns(grad_scores, query)
        return (rows_by_columns(turned[h], grad_scores) * scaling).T.astype(BF)

    parts = []
    before = None
    scores, grad_probs = scores_of(0)
    for h in range(heads):
        later = scores_of(h + 1) if h + 1 < heads else (None, None)
        probs = jnp.exp2(scores * STEEP)
        centre = jnp.sum(probs * grad_probs, axis=0, keepdims=True)
        grad_scores = (probs * (grad_probs - centre)).astype(BF)
        if before is not None:
            parts.append(finish(h - 1, *before))
        before = (probs.astype(BF), grad_scores)
        scores, grad_probs = later
    parts.append(finish(heads - 1, *before))
    grad_queries = jnp.concatenate(parts, axis=1)

    @pl.when(i == 0)
    def _():
        out_first[0, :, :width] = grad_queries

    @pl.when(i == 1)
    def _():
        out_second[0, :, :width] = grad_queries
        for start, ref in ((0, out_first), (half, out_second)):
            rows = slice(start, start + half)
            ref[0, :, width:] = padded_columns(
                [(dk[h, rows] * scaling).astype(BF) for h in range(heads)]
                + [dv[h, rows].astype(BF) for h in range(heads)],
                padded - width,
            )


def attend_back(first, second, do_first, do_second, l_first, l_second, query_marks, key_marks):
    groups, half, padded = first.shape
    heads = l_first.shape[1]
    out_width = do_first.shape[2]
    pair = lambda *dims: pl.BlockSpec((1,) + dims, lambda a, i: (a, 0, 0))
    return pl.pallas_call(
        partial(attend_back_kernel, heads),
        grid=(groups, 2),
        in_specs=[pair(half, padded)] * 2
        + [pair(half, out_width)] * 2
        + [pair(heads, half)] * 2
        + [
            pl.BlockSpec((half, MARKS), lambda a, i: (i, 0)),
            pl.BlockSpec((2 * half, MARKS), lambda a, i: (0, 0)),
        ],
        out_specs=[pair(half, padded)] * 2,
        out_shape=[shape((groups, half, padded), BF)] * 2,
        scratch_shapes=[
            pltpu.VMEM((heads, 2 * half, DEPTH), BF),
            pltpu.VMEM((heads, 2 * half, HEAD_DIM), BF),
            pltpu.VMEM((heads, HEAD_DIM, 2 * half), BF),
            pltpu.VMEM((heads, half, DEPTH), BF),
            pltpu.VMEM((heads, 2 * half, HEAD_DIM), F32),
            pltpu.VMEM((heads, 2 * half, HEAD_DIM), F32),
        ],
        compiler_params=params(60),
        cost_estimate=cost(groups * 12e9, groups * half * padded * 12, groups * heads * half * half),
    )(first, second, do_first, do_second, l_first, l_second, query_marks, key_marks)


def image_sums(hot_turned, values):
    high = values.astype(BF)
    low = (values - high.astype(F32)).astype(BF)
    return rows_by_columns(hot_turned, high) + rows_by_columns(hot_turned, low)


def add_up(ref, value):
    @pl.when(pl.program_id(0) == 0)
    def _():
        ref[...] = value

    @pl.when(pl.program_id(0) != 0)
    def _():
        ref[...] += value


def third_of(first, second, own, other, i, per):
    half = jnp.stack([own[0], other[0]], axis=0)
    return jnp.where(i < per, first[...], jnp.where(i < 2 * per, second[...], half))


def third_specs(block, columns, per):
    full = lambda low: pl.BlockSpec(
        (2, block, columns), lambda i, y: (0, jnp.clip(i - low * per, 0, per - 1), 0)
    )
    single = pl.BlockSpec((1, block, columns), lambda i, y: (0, jnp.clip(i - 2 * per, 0, per - 1), 0))
    return [full(0), full(1), single, single]


def out_weight_specs(width, columns):
    last = columns // (2 * width // 3) - 1
    return [
        pl.BlockSpec((1, width, 2 * width // 3), lambda i, y: (y[0], 0, last)),
        pl.BlockSpec((1, width, 2 * width // 3), lambda i, y: (1 - y[0], 0, last)),
    ]


def middle_kernel(
    side, tok_ref, dy_ref, first, second, own, other, w_own, w_other, b_ref, hot_ref, parts_ref,
    branch_ref, h_ref, g_ref, ht_ref, gt_ref, gb_ref,
):
    i = pl.program_id(0)
    width = tok_ref.shape[1]
    used = width // 2
    att = third_of(first, second, own, other, i, pl.num_programs(0) // 3)[:, :, :used]
    skip = w_own.shape[2] - used
    branch = (
        contract_last(att[0], w_own[0, :, skip:])
        + contract_last(att[1], w_other[0, :, skip:])
        + b_ref[...]
    )
    branch_ref[...] = branch
    hot = hot_ref[...]
    gate = rows_by_columns(hot, parts_ref[0, :, 2 * width :])
    mod = rows_by_columns(hot, parts_ref[1])
    normed, _ = layer_norm(tok_ref[...].astype(F32) + gate * branch)
    hidden = (normed * (1.0 + mod[:, width : 2 * width]) + mod[:, :width]).astype(BF)
    grad = (dy_ref[...].astype(F32) * mod[:, 2 * width :]).astype(BF)
    h_ref[...] = hidden
    g_ref[...] = grad
    turn_in_order(side, ht_ref, hidden)
    turn_in_order(side, gt_ref, grad)
    add_up(gb_ref, jnp.sum(grad.astype(F32), axis=0, keepdims=True))


def middle_part(side, tokens, cotangent, thirds, weights, b_out, hot, parts, block):
    ring = side.shape[0] // 2
    rows, width = tokens.shape
    per = rows // 3 // block
    spec = lambda dims: pl.BlockSpec(dims, lambda i, y: (0,) * len(dims))
    placed = pl.BlockSpec(
        (block, width), lambda i, y: (((i // per + y[0]) % 3) * per + i % per, 0)
    )
    plain = pl.BlockSpec((block, width), lambda i, y: (i, 0))
    turned = pl.BlockSpec((ring, width // ring, block), lambda i, y: (0, 0, i))
    return pl.pallas_call(
        middle_kernel,
        grid_spec=pltpu.PrefetchScalarGridSpec(
            num_scalar_prefetch=1,
            grid=(rows // block,),
            in_specs=[
                placed,
                placed,
                *third_specs(block, thirds[0].shape[2], per),
                *out_weight_specs(width, weights.shape[2]),
                spec((1, width)),
                pl.BlockSpec((block, hot.shape[1]), lambda i, y: (i, 0)),
                spec(parts.shape),
            ],
            out_specs=[plain, plain, plain, turned, turned, spec((1, width))],
        ),
        out_shape=[
            shape((rows, width), F32),
            shape((rows, width), BF),
            shape((rows, width), BF),
            shape((ring, width // ring, rows), BF),
            shape((ring, width // ring, rows), BF),
            shape((1, width), F32),
        ],
        compiler_params=params(),
        cost_estimate=cost(2 * rows * width * (3 * width + 1024), rows * width * 22),
    )(side, tokens, cotangent, *thirds, weights, weights, b_out, hot, parts)


def feed_kernel(
    chunk, pick, h_ref, g_ref, ht_ref, gt_ref, up_ref, down_ref, bias_ref,
    branch_ref, back_ref, mine_ref, near_ref, far_ref, gb_ref, act, pre,
):
    j = pl.program_id(0)
    rows = h_ref.shape[0]
    half = ht_ref.shape[0] // 2
    up = up_ref[0, 0]
    down = down_ref[0, 0]
    total = jnp.zeros(gb_ref.shape, F32)
    for start in range(0, rows, chunk):
        at = slice(start, start + chunk)
        u = rows_by_columns(h_ref[at], up) + bias_ref[0]
        grad = rows_by_columns(g_ref[at], down)
        cube = GELU_CUBE * u * u
        bent = jnp.tanh(GELU_SLOPE * (u + cube * u))
        part = 0.5 * (1.0 + bent)
        slope = part + 0.5 * u * (1.0 - bent * bent) * (GELU_SLOPE * (1.0 + 3.0 * cube))
        low = (u * part).astype(BF)
        back = (grad * slope).astype(BF)
        act[at] = low
        pre[at] = back
        total += jnp.sum(back.astype(F32), axis=0, keepdims=True)
        branch_part = contract_last(low, down)
        back_part = contract_last(back, up)

        @pl.when(j == 0)
        def _():
            branch_ref[at] = branch_part
            back_ref[at] = back_part

        @pl.when(j != 0)
        def _():
            branch_ref[at] += branch_part
            back_ref[at] += back_part

    gb_ref[...] = total
    quarter = half // 2
    for k, (turned, value) in enumerate(((ht_ref, pre), (gt_ref, act))):
        theirs = rows_by_columns(turned[half:], value[...]).astype(BF)
        near_ref[k] = theirs[:quarter]
        far_ref[k] = theirs[quarter:]
        mine_ref[k] = rows_by_columns(turned[:half], value[...])


def feed(pick, hidden, grad, hidden_turned, grad_turned, weights, bias, chunk, cols):
    rows, width = hidden.shape
    units = weights.shape[3]
    half = width // 2
    whole = lambda dims: pl.BlockSpec(dims, lambda j, y: (0, 0), pipeline_mode=pl.Buffered(1))
    columns = lambda k: pl.BlockSpec((1, 1, width, cols), lambda j, y: (k, y[0], 0, j))
    return pl.pallas_call(
        partial(feed_kernel, chunk),
        grid_spec=pltpu.PrefetchScalarGridSpec(
            num_scalar_prefetch=1,
            grid=(units // cols,),
            in_specs=[
                whole((rows, width)),
                whole((rows, width)),
                whole((width, rows)),
                whole((width, rows)),
                columns(0),
                columns(1),
                pl.BlockSpec((1, 1, cols), lambda j, y: (y[0], 0, j)),
            ],
            out_specs=[
                whole((rows, width)),
                whole((rows, width)),
                pl.BlockSpec((2, half, cols), lambda j, y: (0, 0, j)),
                pl.BlockSpec((2, half // 2, cols), lambda j, y: (0, 0, j)),
                pl.BlockSpec((2, half // 2, cols), lambda j, y: (0, 0, j)),
                pl.BlockSpec((1, cols), lambda j, y: (0, j)),
            ],
            scratch_shapes=[pltpu.VMEM((rows, cols), BF), pltpu.VMEM((rows, cols), BF)],
        ),
        out_shape=[
            shape((rows, width), F32),
            shape((rows, width), F32),
            shape((2, half, units), F32),
            shape((2, half // 2, units), BF),
            shape((2, half // 2, units), BF),
            shape((1, units), F32),
        ],
        compiler_params=params(60),
        cost_estimate=cost(
            12 * rows * width * units, rows * width * 16 + width * units * 10, rows * units
        ),
    )(pick, hidden, grad, hidden_turned, grad_turned, weights, weights, bias)


def back_two_kernel(
    side, tok_ref, dy_ref, branch_ref, two_a, two_b, b_ref, back_a, back_b, w_own, w_other, hot_ref,
    turn_ref, parts_ref, first, second, half_own, half_other, out_ref, middle_ref, a_first, a_second,
    a_own, a_other, sums_ref, gb_ref, mine_ref, theirs_ref, outer_ref,
):
    width = tok_ref.shape[1]
    hot = hot_ref[...]
    turn = turn_ref[...]
    gate = rows_by_columns(hot, parts_ref[0, :, 2 * width :])
    mod = rows_by_columns(hot, parts_ref[1])
    branch = branch_ref[...]
    middle = tok_ref[...].astype(F32) + gate * branch
    branch_two = two_a[...] + two_b[...] + b_ref[...]
    grad_hidden = back_a[...] + back_b[...]
    dy = dy_ref[...].astype(F32)
    out_ref[...] = (middle + mod[:, 2 * width :] * branch_two).astype(BF)
    normed, inverse = layer_norm(middle)
    grad_middle = dy + norm_back(normed, inverse, grad_hidden * (1.0 + mod[:, width : 2 * width]))
    middle_ref[...] = grad_middle
    grad = (grad_middle * gate).astype(BF)
    turned = grad.astype(F32).T.astype(BF)
    att = third_of(first, second, half_own, half_other, pl.program_id(0), pl.num_programs(0) // 3)
    for k in range(2):
        product = rows_by_columns(turned, att[k])

        @pl.when(pl.program_id(0) == 0)
        def _():
            outer_ref[k] = product

        @pl.when(pl.program_id(0) != 0)
        def _():
            outer_ref[k] += product

    @pl.when(pl.program_id(0) == pl.num_programs(0) - 1)
    def _():
        ring = side.shape[0] // 2
        piece = width // ring
        for k in range(2):
            pieces = [
                outer_ref[k, pl.ds(pl.multiple_of(side[1 + ring + j] * piece, 8), piece)]
                for j in range(ring)
            ]
            mine_ref[k] = jnp.concatenate(pieces[: ring // 2], axis=0)
            theirs_ref[k] = jnp.concatenate(pieces[ring // 2 :], axis=0).astype(BF)

    skip = w_own.shape[2] - width // 2
    ours = padded_columns([rows_by_columns(grad, w_own[0, :, skip:]).astype(BF)], a_own.shape[2])
    theirs = padded_columns([rows_by_columns(grad, w_other[0, :, skip:]).astype(BF)], a_own.shape[2])
    i = pl.program_id(0)
    per = pl.num_programs(0) // 3
    for k, ref in enumerate((a_first, a_second)):

        @pl.when(i // per == k)
        def _(ref=ref):
            ref[0] = ours
            ref[1] = theirs

    @pl.when(i // per == 2)
    def _():
        a_own[0] = ours
        a_other[0] = theirs

    sums = [
        image_sums(turn, grad_middle * branch),
        image_sums(turn, grad_hidden),
        image_sums(turn, grad_hidden * normed),
        image_sums(turn, dy * branch_two),
    ]
    add_up(sums_ref, jnp.stack(sums, axis=0))
    add_up(gb_ref, jnp.sum(grad.astype(F32), axis=0, keepdims=True))


def back_two(
    side, tokens, cotangent, branch, two_a, two_b, b_down, back_a, back_b, weights, hot, turn, parts,
    attended, block, images, out_width,
):
    rows, width = tokens.shape
    third = rows // 3
    per = rows // 3 // block
    spec = lambda dims: pl.BlockSpec(dims, lambda i, y: (0,) * len(dims))
    placed = pl.BlockSpec(
        (block, width), lambda i, y: (((i // per + y[0]) % 3) * per + i % per, 0)
    )
    plain = pl.BlockSpec((block, width), lambda i, y: (i, 0))
    return pl.pallas_call(
        back_two_kernel,
        grid_spec=pltpu.PrefetchScalarGridSpec(
            num_scalar_prefetch=1,
            grid=(rows // block,),
            in_specs=[
                placed,
                placed,
                plain,
                plain,
                plain,
                spec((1, width)),
                plain,
                plain,
                *out_weight_specs(width, weights.shape[2]),
                pl.BlockSpec((block, hot.shape[1]), lambda i, y: (i, 0)),
                pl.BlockSpec((images, block), lambda i, y: (0, i)),
                spec(parts.shape),
                *third_specs(block, out_width, per),
            ],
            out_specs=[
                placed,
                plain,
                *third_specs(block, out_width, per),
                spec((4, images, width)),
                spec((1, width)),
                spec((2, width // 2, out_width)),
                spec((2, width // 2, out_width)),
            ],
            scratch_shapes=[pltpu.VMEM((2, width, out_width), F32)],
        ),
        out_shape=[
            shape((rows, width), BF),
            shape((rows, width), F32),
            *[shape((2, third, out_width), BF)] * 2,
            *[shape((1, third, out_width), BF)] * 2,
            shape((4, images, width), F32),
            shape((1, width), F32),
            shape((2, width // 2, out_width), F32),
            shape((2, width // 2, out_width), BF),
        ],
        compiler_params=params(62),
        cost_estimate=cost(2 * rows * width * (4 * width + 1024), rows * width * 34),
    )(side, tokens, cotangent, branch, two_a, two_b, b_down, back_a, back_b, weights, weights, hot, turn, parts, *attended)


def outer_kernel(ht_ref, first, second, rest, mine_ref, theirs_ref, sums_ref):
    third = first.shape[1]
    grads = (first[0], second[0], rest[0])
    found = sum(
        rows_by_columns(ht_ref[:, k * third : (k + 1) * third], grad)
        for k, grad in enumerate(grads)
    )

    @pl.when(pl.program_id(0) == 0)
    def _():
        theirs_ref[...] = found.astype(BF)
        sums_ref[...] = sum(jnp.sum(grad.astype(F32), axis=0, keepdims=True) for grad in grads)

    @pl.when(pl.program_id(0) == 1)
    def _():
        mine_ref[...] = found


def outer(turned, first, second, rest, group):
    width, rows = turned.shape
    _, third, cols = first.shape
    block = pl.BlockSpec((width // 2, cols), lambda k: (0, 0))
    pair = pl.BlockSpec((1, third, cols), lambda k: (group, 0, 0))
    single = pl.BlockSpec((1, third, cols), lambda k: (0, 0, 0))
    return pl.pallas_call(
        outer_kernel,
        grid=(2,),
        in_specs=[pl.BlockSpec((width // 2, rows), lambda k: (1 - k, 0)), pair, pair, single],
        out_specs=[block, block, pl.BlockSpec((1, cols), lambda k: (0, 0))],
        out_shape=[shape((width // 2, cols), F32), shape((width // 2, cols), BF), shape((1, cols), F32)],
        compiler_params=params(60),
        cost_estimate=cost(2 * rows * width * cols, rows * width * 2 + rows * cols * 4),
    )(turned, first, second, rest)


def back_one_kernel(
    side, first, second, own, other, w_own, w_other, tok_ref, middle_ref, hot_ref, turn_ref, parts_ref,
    out_ref, sums_ref,
):
    width = tok_ref.shape[1]
    cols = 3 * width // 2
    scale = rows_by_columns(hot_ref[...], parts_ref[0, :, width : 2 * width])
    grads = third_of(first, second, own, other, pl.program_id(0), pl.num_programs(0) // 3)[:, :, :cols]
    grad_hidden = contract_last(grads[0], w_own[0, :, :cols]) + contract_last(
        grads[1], w_other[0, :, :cols]
    )
    normed, inverse = layer_norm(tok_ref[...].astype(F32))
    out_ref[...] = middle_ref[...] + norm_back(normed, inverse, grad_hidden * (1.0 + scale))
    turn = turn_ref[...]
    sums = [image_sums(turn, grad_hidden), image_sums(turn, grad_hidden * normed)]
    add_up(sums_ref, jnp.stack(sums, axis=0))


def back_one(side, thirds, weights, tokens, middle, hot, turn, parts, block, images):
    rows, width = tokens.shape
    cols = thirds[0].shape[2]
    per = rows // 3 // block
    spec = lambda dims: pl.BlockSpec(dims, lambda i, y: (0,) * len(dims))
    once = pl.Buffered(1)
    placed = pl.BlockSpec(
        (block, width), lambda i, y: (((i // per + y[0]) % 3) * per + i % per, 0)
    )
    return pl.pallas_call(
        back_one_kernel,
        grid_spec=pltpu.PrefetchScalarGridSpec(
            num_scalar_prefetch=1,
            grid=(rows // block,),
            in_specs=[
                *third_specs(block, cols, per),
                pl.BlockSpec(
                    (1,) + weights.shape[1:], lambda i, y: (y[0], 0, 0), pipeline_mode=once
                ),
                pl.BlockSpec(
                    (1,) + weights.shape[1:], lambda i, y: (1 - y[0], 0, 0), pipeline_mode=once
                ),
                placed,
                pl.BlockSpec((block, width), lambda i, y: (i, 0)),
                pl.BlockSpec((block, hot.shape[1]), lambda i, y: (i, 0)),
                pl.BlockSpec((images, block), lambda i, y: (0, i)),
                spec(parts.shape),
            ],
            out_specs=[placed, spec((2, images, width))],
        ),
        out_shape=[shape((rows, width), F32), shape((2, images, width), F32)],
        compiler_params=params(),
        cost_estimate=cost(4 * rows * width * cols, rows * width * 10 + rows * cols * 4),
    )(side, *thirds, weights, weights, tokens, middle, hot, turn, parts)


def fast_body(mesh):
    ring = mesh.shape["rows"]
    both = ("rows", "heads")

    def moves(row_of, other_heads):
        pairs = []
        for r in range(ring):
            for y in range(2):
                pairs.append((2 * r + y, 2 * row_of(r) + (1 - y if other_heads else y)))
        return pairs

    to_core = moves(lambda r: r ^ 1, False)
    to_heads = moves(lambda r: r, True)
    to_x = moves(lambda r: r ^ 2, False)
    to_corner = moves(lambda r: r ^ 2, True)
    levels = ring // 4
    to_level = [moves(lambda r, k=k: (r + 4 * k) % ring, False) for k in range(levels)]

    def send(values, pairs):
        return lax.ppermute(values, both, pairs)

    def after(*values):
        return lax.optimization_barrier(values)

    def body(
        tokens,
        condition,
        segment_ids,
        tile_mask,
        image_index,
        w_ada,
        b_ada,
        w_query,
        w_key,
        w_value,
        b_query,
        b_value,
        w_out,
        b_out,
        w_up,
        b_up,
        w_down,
        b_down,
        cotangent,
    ):
        y = lax.axis_index("heads")
        r = lax.axis_index("rows")
        rows, width = tokens.shape
        length = segment_ids.shape[1]
        third = rows // 3
        images = condition.shape[0]
        units = w_up.shape[1]
        cols = w_query.shape[1]

        tiles = length // TILE
        slots = image_index.shape[1]

        def open_to(tiles_on):
            on = (tiles_on > 0) | jnp.eye(tiles, dtype=bool)
            return jnp.repeat(on.astype(jnp.int32), TILE, axis=1)

        seg_full = lax.dynamic_index_in_dim(segment_ids, 2 * y, 0, keepdims=False)
        tile_full = lax.dynamic_index_in_dim(tile_mask, 2 * y, 0, keepdims=False)
        seg_half = jnp.where(y == 0, segment_ids[1], jnp.roll(segment_ids[1], -third))
        shift = third // TILE
        tile_half = jnp.where(
            y == 0, tile_mask[1], jnp.roll(tile_mask[1], (-shift, -shift), axis=(0, 1))
        )
        marks = marks_of(seg_full[None], open_to(tile_full), seg_half[None], open_to(tile_half))

        def image_of(seg, index):
            slot = jnp.arange(slots, dtype=jnp.int32)
            return jnp.sum(jnp.where(seg[:, None] == slot[None, :], index[None, :], 0), axis=1)

        own_image = jnp.concatenate(
            [
                image_of(seg_full, lax.dynamic_index_in_dim(image_index, 2 * y, 0, keepdims=False)),
                image_of(seg_half[:third], image_index[1]),
            ]
        )
        chosen = jnp.arange(images, dtype=jnp.int32)
        hot = (own_image[:, None] == jnp.tile(chosen, 3)[None, :]).astype(BF)
        turn = (chosen[:, None] == own_image[None, :]).astype(BF)

        order = jnp.arange(ring, dtype=jnp.int32)
        core_of, x_of, level_of = order // (ring // 2), (order // levels) % 2, order % levels
        owner = ((r // 4 + level_of) % levels) * 4 + ((r // 2 % 2) ^ x_of) * 2 + ((r % 2) ^ core_of)
        piece = width // ring
        place = jnp.sum(jnp.where(owner[None, :] == order[:, None], order[None, :], 0), axis=1)
        side = jnp.concatenate([y.reshape(1), place, owner])

        padded = -(-3 * cols // 128) * 128
        out_width = -(-cols // 128) * 128
        here = jnp.stack([y, r // 4, (r // 2) % 2, r % 2]).astype(jnp.int32)
        next_level = to_level[levels - 1]

        class Tree:
            def __init__(self, shard):
                self.count = shard.shape[-1] // 3
                self.first = [shard[..., : 2 * self.count]]
                self.last = [shard[..., 2 * self.count :]]
                self.step = 0

            def sends(self):
                moves = (
                    (next_level, to_x),
                    (next_level, to_heads),
                    (next_level, next_level),
                    (to_x, to_heads, next_level),
                    (to_heads, to_x, next_level),
                    (to_core,) * 5,
                )[self.step]
                if self.step < 3:
                    self.sent = (self.first[-1], self.last[-1])
                elif self.step < 5:
                    self.sent = (self.over_x, self.over_y, self.last[-1])
                else:
                    self.sent = (*self.over_x, *self.over_y, self.last)
                return [send(value, move) for value, move in zip(self.sent, moves)]

            def take(self, got):
                if self.step < 2:
                    self.first.append(got[0])
                    self.last = [jnp.stack([self.last[0], got[1]])]
                elif self.step == 2:
                    whole = jnp.stack([*self.first, got[0]])
                    self.over_x, self.over_y = whole[..., : self.count], whole[..., self.count :]
                    self.last.append(got[1])
                elif self.step == 3:
                    self.over_x = jnp.stack([self.over_x, got[0]])
                    self.over_y = jnp.stack([self.over_y, got[1]])
                    self.last.append(got[2])
                elif self.step == 4:
                    self.over_x = (self.over_x, got[0])
                    self.over_y = (self.over_y, got[1])
                    self.last = jnp.stack([*self.last, got[2]])
                else:
                    self.whole = collected(here, (*self.sent, *got))
                self.step += 1

        shard = jnp.concatenate([w_query, w_key, w_value, w_out], axis=1).astype(BF)
        tree = Tree(shard[None])
        cond = condition.astype(F32)
        mod_cols, *got = after(
            jnp.dot(jax.nn.silu(cond), w_ada, precision=PRECISE) + b_ada, *tree.sends()
        )
        tree.take(got)
        biases = jnp.concatenate([b_up, b_query, b_value])[None]
        own_spread = jnp.concatenate([mod_cols, biases], axis=0)
        got_spread, hot, turn, side, *joined = after(
            send(own_spread, to_heads), hot, turn, side, *marks, *tree.sends()
        )
        marks_full, marks_half = joined[:2], joined[2:4]
        tree.take(joined[4:])
        spread = jnp.where(
            y == 0, jnp.stack([own_spread, got_spread]), jnp.stack([got_spread, own_spread])
        )
        parts = three_parts(spread[:, :images])
        up_bias = spread[:, images:, :units]
        qkv_bias = jnp.concatenate(
            [
                spread[:, images:, units : units + cols],
                jnp.zeros((2, 1, cols), F32),
                spread[:, images:, units + cols :],
            ],
            axis=2,
        )
        hidden_full, hidden_half, hidden_one_turned, qkv_bias, up_bias, *got = after(
            *first_norm(side, tokens, hot, parts, third), qkv_bias, up_bias, *tree.sends()
        )
        tree.take(got)
        feed_shard = jnp.stack([w_up, w_down]).astype(BF)
        hidden_full, hidden_half, feed_shard, *got = after(
            hidden_full, hidden_half, feed_shard, *tree.sends()
        )
        tree.take(got)
        hidden_full, hidden_half, *got = after(hidden_full, hidden_half, *tree.sends())
        tree.take(got)
        feed_weights = lax.all_gather(
            feed_shard, ("heads", "rows"), axis=1, tiled=True
        ).reshape(2, 2, width, units)
        hidden_full, hidden_half, *got = after(hidden_full, hidden_half, *tree.sends())
        tree.take(got)
        attention_weights = tree.whole.reshape(2, width, shard.shape[1])

        qkv_first, qkv_second, hidden_got = after(
            *project(
                side, hidden_full, hidden_full, attention_weights, qkv_bias, padded, third, 2
            ),
            send(hidden_half, to_heads),
        )
        qkv_full = (qkv_first, qkv_second)
        qkv_half = project(
            side, hidden_half, hidden_got, attention_weights, qkv_bias, padded, third, 1
        )
        qkv_own, qkv_got, condition = after(*qkv_half, condition)
        qkv_half = (qkv_own, qkv_got)
        out_own, out_theirs, l_own, l_other, *got = after(
            *attend(*qkv_half, *marks_half, out_width),
            *(send(condition, to_level[k]) for k in range(1, levels)),
        )
        lse_half = (l_own, l_other)
        qkv_first, out_theirs, flat = after(qkv_first, out_theirs, jnp.stack([condition, *got]))
        out_first, out_second, *lse_full, out_other, got = after(
            *attend(qkv_first, qkv_second, *marks_full, out_width),
            send(out_theirs, to_heads),
            send(flat, to_x),
        )
        out_first, flat = after(out_first, jnp.concatenate([flat, got], axis=0))
        attended = (out_first, out_second, out_own, out_other)
        branch_one, hidden_two, grad_two, hidden_two_turned, grad_two_turned, grad_b_down, got = after(
            *middle_part(
                side, tokens, cotangent, attended, attention_weights, b_out[None], hot, parts, third // 2
            ),
            send(flat, to_core),
        )
        flat = jnp.concatenate([flat, got], axis=0)
        silu_all = jax.nn.silu(flat.reshape(ring * images, width).astype(F32))

        def added(mine, got):
            return mine + got.astype(F32)

        def level_pieces(values):
            part = lambda k: values[..., k * piece : (k + 1) * piece, :]
            return part(0), *(part(k).astype(BF) for k in range(1, levels))

        def all_added(kept, got):
            for part in got:
                kept = added(kept, part)
            return kept

        quarter = width // 4

        def plane_pieces(mine_own, got_own, mine_other, got_other):
            near = lambda mine, got: added(mine[:quarter], got[:quarter])
            far = lambda mine, got: added(mine[quarter:], got[quarter:]).astype(BF)
            return (
                near(mine_own, got_own),
                far(mine_own, got_own),
                near(mine_other, got_other).astype(BF),
                far(mine_other, got_other),
            )

        flat_turned = lambda values: values.reshape(width, rows)
        hidden_one_turned = flat_turned(hidden_one_turned)
        feed_args = (flat_turned(hidden_two_turned), flat_turned(grad_two_turned), feed_weights, up_bias, third, 768)
        two_b, back_b, mine_b, near_b, far_b, grad_b_up_b = feed(
            1 - y.reshape(1), hidden_two, grad_two, *feed_args
        )
        far_b = added(mine_b[:, quarter:], send(far_b, to_core)).astype(BF)
        hidden_two, far_b, near_b = after(hidden_two, far_b, near_b)
        two_a, back_a, mine_a, near_a, far_a, grad_b_up_a, near_b, far_b = after(
            *feed(y.reshape(1), hidden_two, grad_two, *feed_args),
            send(near_b, to_core),
            send(far_b, to_x),
        )
        over_b = added(added(mine_b[:, :quarter], near_b), far_b).astype(BF)
        far_a = added(mine_a[:, quarter:], send(far_a, to_core)).astype(BF)
        two_a, over_b, far_a, near_a = after(two_a, over_b, far_a, near_a)

        output, grad_middle, *grad_attended, sums_two, grad_b_out, out_mine, out_theirs_sum, over_b, far_a, near_a = after(
            *back_two(
                side, tokens, cotangent, branch_one, two_a, two_b, b_down[None], back_a, back_b, attention_weights,
                hot, turn, parts, attended, third // 2, images, out_width,
            ),
            send(over_b, to_heads),
            send(far_a, to_x),
            send(near_a, to_core),
        )
        grad_first, grad_second, grad_own, grad_theirs = grad_attended
        grad_other = send(grad_theirs, to_heads)
        out_got = send(out_theirs_sum, to_core)
        out_pieces = plane_pieces(out_mine[0], out_got[0], out_mine[1], out_got[1])
        feed_kept, *feed_sent = level_pieces(
            added(added(added(mine_a[:, :quarter], near_a), far_a), over_b)
        )
        grad_own, feed_kept, *joined = after(grad_own, feed_kept, *feed_sent, *out_pieces)
        feed_sent, out_pieces = joined[: levels - 1], joined[levels - 1 :]
        grad_qkv_own, grad_qkv_theirs = attend_back(
            *qkv_half, grad_own, grad_other, *lse_half, *marks_half
        )
        grad_first, grad_qkv_theirs, feed_kept, *joined = after(
            grad_first, grad_qkv_theirs, feed_kept, *feed_sent, *out_pieces
        )
        feed_sent, out_pieces = joined[: levels - 1], joined[levels - 1 :]
        grad_qkv_first, grad_qkv_second, grad_qkv_other, *got = after(
            *attend_back(*qkv_full, grad_first, grad_second, *lse_full, *marks_full),
            send(grad_qkv_theirs, to_heads),
            *(send(part, to_level[k + 1]) for k, part in enumerate(feed_sent)),
        )
        grad_w_up, grad_w_down = all_added(feed_kept, got)
        qkv_mine_b, qkv_theirs_b, grad_qkv_bias_b, *got = after(
            *outer(hidden_one_turned, grad_qkv_first, grad_qkv_second, grad_qkv_other, 1),
            send(out_pieces[1], to_x),
            send(out_pieces[2], to_heads),
            send(out_pieces[3], to_corner),
        )
        out_kept, *out_sent = level_pieces(all_added(out_pieces[0], got))
        hidden_one_turned, qkv_theirs_b, out_kept, *out_sent = after(
            hidden_one_turned, qkv_theirs_b, out_kept, *out_sent
        )
        qkv_mine_a, qkv_theirs_a, grad_qkv_bias_a, qkv_got_b, *got = after(
            *outer(hidden_one_turned, grad_qkv_first, grad_qkv_second, grad_qkv_own, 0),
            send(qkv_theirs_b, to_core),
            *(send(part, to_level[k + 1]) for k, part in enumerate(out_sent)),
        )
        grad_w_out = all_added(out_kept, got)
        near, *sent = plane_pieces(qkv_mine_a, send(qkv_theirs_a, to_core), qkv_mine_b, qkv_got_b)
        grad_middle, near, *sent = after(grad_middle, near, *sent)
        grad_qkv = (grad_qkv_first, grad_qkv_second, grad_qkv_own, grad_qkv_other)
        grad_tokens, sums_one, *got = after(
            *back_one(
                side, grad_qkv, attention_weights, tokens, grad_middle, hot, turn, parts, third // 2, images
            ),
            send(sent[0], to_x),
            send(sent[1], to_heads),
            send(sent[2], to_corner),
        )
        qkv_kept, *qkv_sent = level_pieces(all_added(near, got))

        sums = jnp.concatenate([sums_one, sums_two], axis=0).reshape(2, 3, images, width)
        sums = sums.transpose(0, 2, 1, 3).reshape(2, images, 3 * width)
        narrow = jnp.concatenate([grad_b_out, grad_b_down], axis=0).reshape(2, 2, cols)

        def packet(which, up_sum, qkv_sum):
            second = lax.dynamic_index_in_dim(narrow, which, 1, keepdims=False).reshape(-1)
            short = [up_sum[0], qkv_sum[:cols], qkv_sum[2 * cols : 3 * cols], second]
            short = jnp.concatenate(short).reshape(images, -1)
            chunk = lax.dynamic_index_in_dim(sums, which, 0, keepdims=False)
            gap = -(chunk.shape[1] + short.shape[1]) % 128
            return jnp.concatenate([chunk, short, jnp.zeros((images, gap), F32)], axis=1)

        own_packet = packet(y, grad_b_up_a, grad_qkv_bias_a[0]) + send(
            packet(1 - y, grad_b_up_b, grad_qkv_bias_b[0]), to_heads
        )
        own_packet, qkv_kept, *qkv_sent = after(own_packet, qkv_kept, *qkv_sent)
        grad_silu = lax.dot_general(
            own_packet[:, : 3 * width],
            w_ada,
            (((1,), (1,)), ((), ())),
            precision=PRECISE,
            preferred_element_type=F32,
        )
        grad_silu, *got = after(
            grad_silu, *(send(own_packet, to_level[k]) for k in range(1, levels))
        )
        flat = jnp.concatenate([own_packet, *got], axis=0)
        flat, *qkv_sent = after(flat, *qkv_sent)
        silu_got, flat_got, *got = after(
            send(grad_silu, to_heads),
            send(flat, to_x),
            *(send(part, to_level[k + 1]) for k, part in enumerate(qkv_sent)),
        )
        grad_w_qkv = all_added(qkv_kept, got)
        flat = jnp.concatenate([flat, flat_got], axis=0)
        packets = jnp.concatenate([flat, send(flat, to_core)], axis=0)
        grad_mod = packets[:, : 3 * width]
        count = units + 4 * cols
        short = packets[:, 3 * width : 3 * width + count // images]
        bias_sums = jnp.sum(short.reshape(ring, images, count // images), axis=0).reshape(-1)
        s1, s2, _ = jnp.split(three_parts(silu_all), 3, axis=0)
        g1, g2, _ = jnp.split(three_parts(grad_mod), 3, axis=0)
        grad_w_ada = contract_first(
            jnp.concatenate([s1, s1, s2], axis=0), jnp.concatenate([g1, g2, g1], axis=0)
        )
        grad_b_ada = jnp.sum(grad_mod, axis=0)
        grad_silu = grad_silu + silu_got
        _, silu_back = jax.vjp(jax.nn.silu, cond)
        grad_condition = silu_back(grad_silu)[0]
        return (
            output,
            grad_tokens,
            grad_condition,
            grad_w_ada,
            grad_b_ada,
            grad_w_qkv[:, :cols],
            grad_w_qkv[:, cols : 2 * cols],
            grad_w_qkv[:, 2 * cols : 3 * cols],
            bias_sums[units : units + cols],
            bias_sums[units + cols : units + 2 * cols],
            grad_w_out[:, :cols],
            bias_sums[units + 2 * cols : units + 3 * cols],
            grad_w_up,
            bias_sums[:units],
            grad_w_down,
            bias_sums[units + 3 * cols :],
        )

    return body


def solution(mesh):
    body = fast_body(mesh) if mesh.shape["heads"] == 2 and mesh.shape["rows"] == 16 else general_body
    placed = (
        P(("rows", "heads"), None),
        P("rows", None),
        P("rows", None),
        P("rows", None, None),
        P("rows", None),
        P(None, "heads"),
        P("heads"),
        P("rows", "heads"),
        P("rows", "heads"),
        P("rows", "heads"),
        P("heads"),
        P("heads"),
        P("rows", "heads"),
        P(),
        P("rows", "heads"),
        P("heads"),
        P("rows", "heads"),
        P(),
        P(("rows", "heads"), None),
    )
    return jax.shard_map(
        body,
        mesh=mesh,
        in_specs=placed,
        out_specs=(
            P(("rows", "heads"), None),
            P(("rows", "heads"), None),
            P("rows", None),
            P(None, "heads"),
            P("heads"),
            P("rows", "heads"),
            P("rows", "heads"),
            P("rows", "heads"),
            P("heads"),
            P("heads"),
            P("rows", "heads"),
            P("heads"),
            P("rows", "heads"),
            P("heads"),
            P("rows", "heads"),
            P("heads"),
        ),
        check_vma=False,
    )
```

```python
from functools import partial

import jax
import jax.numpy as jnp
from jax import lax
from jax.experimental import pallas as pl
from jax.experimental.pallas import tpu as pltpu
from jax.sharding import PartitionSpec as P

HEAD_DIM = 72
TILE = 128


EPSILON = 1e-06
MASKED_SCORE = -1e30
PRECISE = lax.Precision.HIGHEST


def layer_norm(values):
    centred = values - jnp.mean(values, axis=-1, keepdims=True)
    inverse = lax.rsqrt(jnp.mean(centred * centred, axis=-1, keepdims=True) + EPSILON)
    return (centred * inverse, inverse)


def norm_back(normed, inverse, grad):
    return inverse * (
        grad
        - jnp.mean(grad, axis=-1, keepdims=True)
        - normed * jnp.mean(grad * normed, axis=-1, keepdims=True)
    )


def contract_last(left, right):
    return lax.dot_general(
        left, right, (((1,), (1,)), ((), ())), preferred_element_type=jnp.float32
    )


def contract_first(left, right):
    return lax.dot_general(
        left, right, (((0,), (0,)), ((), ())), preferred_element_type=jnp.float32
    )


def general_body(
    tokens,
    condition,
    segment_ids,
    tile_mask,
    image_index,
    w_ada,
    b_ada,
    w_query,
    w_key,
    w_value,
    b_query,
    b_value,
    w_out,
    b_out,
    w_up,
    b_up,
    w_down,
    b_down,
    cotangent,
):
    scaling = HEAD_DIM ** (-0.5)
    own_rows = tokens.shape[0]
    seq_count = segment_ids.shape[0]
    length = segment_ids.shape[1]
    group_rows = seq_count * length
    own_start = lax.axis_index("heads") * own_rows
    img_count = condition.shape[0]
    slot_count = image_index.shape[1]
    local_heads = w_query.shape[1] // HEAD_DIM
    block_rows = min(512, length)
    tile_count = length // TILE
    bfloat = jnp.bfloat16
    own_segments = lax.dynamic_slice_in_dim(segment_ids.reshape(group_rows), own_start, own_rows)
    own_seqs = (own_start + jnp.arange(own_rows, dtype=jnp.int32)) // length
    seq_match = own_seqs[:, None] == jnp.arange(seq_count, dtype=jnp.int32)[None, :]
    slot_match = own_segments[:, None] == jnp.arange(slot_count, dtype=jnp.int32)[None, :]
    own_image = jnp.sum(
        jnp.where(seq_match[:, :, None] & slot_match[:, None, :], image_index[None, :, :], 0),
        axis=(1, 2),
    )
    image_onehot = (own_image[:, None] == jnp.arange(img_count, dtype=jnp.int32)[None, :]).astype(
        jnp.float32
    )
    cond_full = condition.astype(jnp.float32)
    silu_cond = jax.nn.silu(cond_full)
    mod_cols = jnp.dot(silu_cond, w_ada, precision=PRECISE) + b_ada
    mod_full, up_bias_all = (
        lax.all_gather(mod_cols, "heads", axis=1, tiled=True),
        lax.all_gather(b_up.reshape(1, -1), "heads", axis=1, tiled=True),
    )
    per_token = jnp.dot(image_onehot, mod_full, precision=PRECISE)
    shift_one, scale_one, gate_one, shift_two, scale_two, gate_two = jnp.split(per_token, 6, axis=1)

    def gather_weights():
        return (
            lax.all_gather(w_query.astype(bfloat), "rows", axis=0, tiled=True),
            lax.all_gather(w_key.astype(bfloat), "rows", axis=0, tiled=True),
            lax.all_gather(w_value.astype(bfloat), "rows", axis=0, tiled=True),
            lax.all_gather(w_out.astype(bfloat), "rows", axis=0, tiled=True),
            lax.all_gather(w_up.astype(bfloat), "rows", axis=0, tiled=True),
            lax.all_gather(w_down.astype(bfloat), "rows", axis=0, tiled=True),
        )

    def spread_first(values):
        return lax.all_gather(values, "heads", axis=0, tiled=True)

    query_full, key_full, value_full, out_full, up_full, down_full = gather_weights()
    token_full = tokens.astype(jnp.float32)
    normed_one, inverse_one = layer_norm(token_full)
    hidden_own_one = (normed_one * (1.0 + scale_one) + shift_one).astype(bfloat)
    hidden_one = spread_first(hidden_own_one)
    head_shape = (group_rows, local_heads, HEAD_DIM)
    query_heads = (
        (jnp.dot(hidden_one, query_full, preferred_element_type=jnp.float32) + b_query)
        .astype(bfloat)
        .reshape(head_shape)
    )
    key_heads = (
        jnp.dot(hidden_one, key_full, preferred_element_type=jnp.float32)
        .astype(bfloat)
        .reshape(head_shape)
    )
    value_heads = (
        (jnp.dot(hidden_one, value_full, preferred_element_type=jnp.float32) + b_value)
        .astype(bfloat)
        .reshape(head_shape)
    )
    tile_of = jnp.arange(length, dtype=jnp.int32) // TILE

    def scores_for(seq_index, block_start):
        seq_start = seq_index * length
        block_query = query_heads[seq_start + block_start : seq_start + block_start + block_rows]
        seq_keys = key_heads[seq_start : seq_start + length]
        block_tiles = tile_mask[seq_index][block_start // TILE : (block_start + block_rows) // TILE]
        expanded = jnp.broadcast_to(
            block_tiles[:, None, :, None], (block_rows // TILE, TILE, tile_count, TILE)
        ).reshape(block_rows, length)
        seg_row = segment_ids[seq_index]
        same_image = seg_row[block_start : block_start + block_rows][:, None] == seg_row[None, :]
        diagonal = tile_of[block_start : block_start + block_rows][:, None] == tile_of[None, :]
        allowed = same_image & ((expanded > 0) | diagonal)
        raw = (
            jnp.einsum("qhd,khd->hqk", block_query, seq_keys, preferred_element_type=jnp.float32)
            * scaling
        )
        return (jnp.where(allowed[None], raw, MASKED_SCORE), block_query, seq_keys)

    attended_parts = []
    log_totals = []
    for seq_index in range(seq_count):
        seq_values = value_heads[seq_index * length : (seq_index + 1) * length]
        for block_start in range(0, length, block_rows):
            scores, block_query, seq_keys = scores_for(seq_index, block_start)
            top_score = jnp.max(scores, axis=-1, keepdims=True)
            log_total = top_score + jnp.log(
                jnp.sum(jnp.exp(scores - top_score), axis=-1, keepdims=True)
            )
            probs_low = jnp.exp(scores - log_total).astype(bfloat)
            attended_parts.append(
                jnp.einsum(
                    "hqk,khd->qhd", probs_low, seq_values, preferred_element_type=jnp.float32
                )
            )
            log_totals.append(log_total)
    attended = (
        jnp.concatenate(attended_parts, axis=0)
        .reshape(group_rows, local_heads * HEAD_DIM)
        .astype(bfloat)
    )
    branch_one = (
        lax.psum_scatter(
            contract_last(attended, out_full), "heads", scatter_dimension=0, tiled=True
        )
        + b_out
    )
    middle = token_full + gate_one * branch_one
    normed_two, inverse_two = layer_norm(middle)
    hidden_own_two = (normed_two * (1.0 + scale_two) + shift_two).astype(bfloat)
    up_all, down_all = (
        lax.all_gather(up_full, "heads", axis=1, tiled=True),
        lax.all_gather(down_full, "heads", axis=1, tiled=True),
    )
    pre_act = jnp.dot(hidden_own_two, up_all, preferred_element_type=jnp.float32) + up_bias_all[0]
    activated = jax.nn.gelu(pre_act, approximate=True).astype(bfloat)
    branch_two = contract_last(activated, down_all) + b_down
    output = (middle + gate_two * branch_two).astype(bfloat)
    query_back, key_back, value_back, out_back, up_back, down_back = gather_weights()
    hidden_one_back = spread_first(hidden_own_one)
    grad_out = cotangent.astype(jnp.float32)
    grad_branch_two = (grad_out * gate_two).astype(bfloat)
    grad_gate_two = grad_out * branch_two
    grad_down_all = contract_first(grad_branch_two, activated)
    grad_act = jnp.dot(grad_branch_two, down_all, preferred_element_type=jnp.float32)
    _, gelu_back = jax.vjp(partial(jax.nn.gelu, approximate=True), pre_act)
    grad_pre = gelu_back(grad_act)[0].astype(bfloat)
    grad_up_all = contract_first(hidden_own_two, grad_pre)
    grad_bias_all = jnp.sum(grad_pre, axis=0, dtype=jnp.float32).reshape(1, -1)
    grad_hidden_two = contract_last(grad_pre, up_all)
    grad_w_up, grad_w_down, grad_bias_cols = (
        lax.psum_scatter(grad_up_all, "heads", scatter_dimension=1, tiled=True),
        lax.psum_scatter(grad_down_all, "heads", scatter_dimension=1, tiled=True),
        lax.psum_scatter(grad_bias_all, "heads", scatter_dimension=1, tiled=True),
    )
    grad_b_up = grad_bias_cols[0]
    grad_scale_two = grad_hidden_two * normed_two
    grad_middle = grad_out + norm_back(normed_two, inverse_two, grad_hidden_two * (1.0 + scale_two))
    grad_branch_one = (grad_middle * gate_one).astype(bfloat)
    grad_gate_one = grad_middle * branch_one
    grad_one_full = lax.all_gather(grad_branch_one, "heads", axis=0, tiled=True)
    grad_w_out = contract_first(grad_one_full, attended)
    grad_attended = (
        jnp.dot(grad_one_full, out_back, preferred_element_type=jnp.float32)
        .astype(bfloat)
        .reshape(head_shape)
    )
    grad_query_parts = []
    grad_key_parts = []
    grad_value_parts = []
    block_number = 0
    for seq_index in range(seq_count):
        seq_start = seq_index * length
        seq_values = value_heads[seq_start : seq_start + length]
        key_total = jnp.zeros((length, local_heads, HEAD_DIM), jnp.float32)
        value_total = jnp.zeros((length, local_heads, HEAD_DIM), jnp.float32)
        for block_start in range(0, length, block_rows):
            scores, block_query, seq_keys = scores_for(seq_index, block_start)
            probs = jnp.exp(scores - log_totals[block_number])
            block_number += 1
            grad_block = grad_attended[
                seq_start + block_start : seq_start + block_start + block_rows
            ]
            grad_probs = jnp.einsum(
                "qhd,khd->hqk", grad_block, seq_values, preferred_element_type=jnp.float32
            )
            centre = jnp.sum(probs * grad_probs, axis=-1, keepdims=True)
            grad_scores = (probs * (grad_probs - centre)).astype(bfloat)
            grad_query_parts.append(
                (
                    jnp.einsum(
                        "hqk,khd->qhd", grad_scores, seq_keys, preferred_element_type=jnp.float32
                    )
                    * scaling
                ).astype(bfloat)
            )
            key_total = (
                key_total
                + jnp.einsum(
                    "hqk,qhd->khd", grad_scores, block_query, preferred_element_type=jnp.float32
                )
                * scaling
            )
            value_total = value_total + jnp.einsum(
                "hqk,qhd->khd", probs.astype(bfloat), grad_block, preferred_element_type=jnp.float32
            )
        grad_key_parts.append(key_total.astype(bfloat))
        grad_value_parts.append(value_total.astype(bfloat))
    flat_shape = (group_rows, local_heads * HEAD_DIM)
    grad_queries = jnp.concatenate(grad_query_parts, axis=0).reshape(flat_shape)
    grad_keys = jnp.concatenate(grad_key_parts, axis=0).reshape(flat_shape)
    grad_values = jnp.concatenate(grad_value_parts, axis=0).reshape(flat_shape)
    grad_w_query = contract_first(hidden_one_back, grad_queries)
    grad_w_key = contract_first(hidden_one_back, grad_keys)
    grad_w_value = contract_first(hidden_one_back, grad_values)
    grad_b_query = jnp.sum(grad_queries, axis=0, dtype=jnp.float32)
    grad_b_value = jnp.sum(grad_values, axis=0, dtype=jnp.float32)
    total = contract_last(grad_queries, query_back)
    total = total + contract_last(grad_keys, key_back)
    grad_hidden_one = lax.psum_scatter(
        total + contract_last(grad_values, value_back), "heads", scatter_dimension=0, tiled=True
    )
    grad_scale_one = grad_hidden_one * normed_one
    grad_tokens = grad_middle + norm_back(
        normed_one, inverse_one, grad_hidden_one * (1.0 + scale_one)
    )
    grad_mod_tokens = jnp.concatenate(
        [
            grad_hidden_one,
            grad_scale_one,
            grad_gate_one,
            grad_hidden_two,
            grad_scale_two,
            grad_gate_two,
        ],
        axis=1,
    )
    grad_mod_images = lax.dot_general(
        image_onehot,
        grad_mod_tokens,
        (((0,), (0,)), ((), ())),
        precision=PRECISE,
        preferred_element_type=jnp.float32,
    )
    bias_parts = jnp.stack(
        [
            jnp.sum(grad_branch_one, axis=0, dtype=jnp.float32),
            jnp.sum(grad_branch_two, axis=0, dtype=jnp.float32),
        ],
        axis=0,
    )
    grad_mod_cols, bias_cols = (
        lax.psum_scatter(grad_mod_images, "heads", scatter_dimension=1, tiled=True),
        lax.psum_scatter(bias_parts, "heads", scatter_dimension=1, tiled=True),
    )
    grad_w_ada = lax.dot_general(
        silu_cond,
        grad_mod_cols,
        (((0,), (0,)), ((), ())),
        precision=PRECISE,
        preferred_element_type=jnp.float32,
    )
    grad_b_ada = jnp.sum(grad_mod_cols, axis=0)
    grad_silu = lax.dot_general(
        grad_mod_cols,
        w_ada,
        (((1,), (1,)), ((), ())),
        precision=PRECISE,
        preferred_element_type=jnp.float32,
    )
    grad_silu = lax.psum(grad_silu, "heads")
    _, silu_back = jax.vjp(jax.nn.silu, cond_full)
    grad_condition = silu_back(grad_silu)[0]
    grad_w_ada, grad_b_ada, grad_b_query, grad_b_value, grad_b_up, bias_cols = lax.psum(
        (grad_w_ada, grad_b_ada, grad_b_query, grad_b_value, grad_b_up, bias_cols), "rows"
    )
    grad_w_query, grad_w_key, grad_w_value, grad_w_out, grad_w_up, grad_w_down = (
        lax.psum_scatter(grad_w_query, "rows", scatter_dimension=0, tiled=True),
        lax.psum_scatter(grad_w_key, "rows", scatter_dimension=0, tiled=True),
        lax.psum_scatter(grad_w_value, "rows", scatter_dimension=0, tiled=True),
        lax.psum_scatter(grad_w_out, "rows", scatter_dimension=0, tiled=True),
        lax.psum_scatter(grad_w_up, "rows", scatter_dimension=0, tiled=True),
        lax.psum_scatter(grad_w_down, "rows", scatter_dimension=0, tiled=True),
    )
    return (
        output,
        grad_tokens,
        grad_condition,
        grad_w_ada,
        grad_b_ada,
        grad_w_query,
        grad_w_key,
        grad_w_value,
        grad_b_query,
        grad_b_value,
        grad_w_out,
        bias_cols[0],
        grad_w_up,
        grad_b_up,
        grad_w_down,
        bias_cols[1],
    )


LOG2E = 1.4426950408889634
GELU_SLOPE = 0.7978845608028654
GELU_CUBE = 0.044715
BF = jnp.bfloat16
F32 = jnp.float32
MIB = 2**20


def rows_by_columns(left, right):
    return jnp.dot(left, right, preferred_element_type=F32)


def shape(dims, dtype):
    return jax.ShapeDtypeStruct(dims, dtype)


def params(mib=56):
    return pltpu.CompilerParams(vmem_limit_bytes=mib * MIB)


def cost(flops, bytes_accessed, transcendentals=0):
    return pl.CostEstimate(
        flops=int(flops), bytes_accessed=int(bytes_accessed), transcendentals=int(transcendentals)
    )


def three_parts(values):
    high = lax.reduce_precision(values, 8, 7)
    rest = values - high
    middle = lax.reduce_precision(rest, 8, 7)
    return jnp.concatenate([high, middle, rest - middle], axis=-2).astype(BF)


def collect_kernel(here, *refs):
    sources, whole, sems = refs[:10], refs[10], refs[11]
    levels, xs = whole.shape[2:4]
    count = sources[0].shape[-1]
    y, level, x, core = (here[k] for k in range(4))
    flip = lambda bit, other: bit + other - 2 * bit * other
    copies = []
    for dc in range(2):
        x_near, x_far, y_near, y_far, last = sources[5 * dc : 5 * dc + 5]
        for dz in range(levels):
            for i in range(2):
                for j in range(2):
                    at = (flip(y, i), lax.rem(level + dz, levels), flip(x, j), flip(core, dc))
                    found = (
                        (x_near, x_far)[i].at[j, dz],
                        (y_near, y_far)[j].at[i, dz],
                        last.at[dz, i, j],
                    )
                    for k, source in enumerate(found):
                        place = whole.at[(slice(None), *at, slice(None), pl.ds(k * count, count))]
                        copies.append(pltpu.make_async_copy(source, place, sems.at[len(copies)]))
                        copies[-1].start()
    for copy in copies:
        copy.wait()


def collected(here, sources):
    levels, heads, xs, parts, piece, count = sources[4].shape
    whole = (parts, heads, levels, xs, 2, piece, 3 * count)
    anywhere = pl.BlockSpec(memory_space=pl.ANY)
    return pl.pallas_call(
        collect_kernel,
        grid_spec=pltpu.PrefetchScalarGridSpec(
            num_scalar_prefetch=1,
            grid=(1,),
            in_specs=[anywhere] * 10,
            out_specs=anywhere,
            scratch_shapes=[pltpu.SemaphoreType.DMA((6 * heads * levels * xs,))],
        ),
        out_shape=shape(whole, BF),
        compiler_params=params(16),
        cost_estimate=cost(0, 24 * parts * heads * levels * xs * piece * count),
    )(here, *sources)


def turn_in_order(places, turned_ref, values):
    turned = values.astype(F32).T
    piece = turned_ref.shape[1]
    for k in range(turned_ref.shape[0]):
        turned_ref[places[1 + k]] = turned[k * piece : (k + 1) * piece].astype(BF)


def norm_kernel(side, tok_ref, hot_ref, parts_ref, h_ref, half_ref, ht_ref):
    width = tok_ref.shape[1]
    normed, _ = layer_norm(tok_ref[...].astype(F32))
    mod = rows_by_columns(hot_ref[...], parts_ref[0, :, : 2 * width])
    hidden = (normed * (1.0 + mod[:, width:]) + mod[:, :width]).astype(BF)
    turn_in_order(side, ht_ref, hidden)

    @pl.when(pl.program_id(0) < 2)
    def _():
        h_ref[...] = hidden

    @pl.when(pl.program_id(0) == 2)
    def _():
        half_ref[...] = hidden


def first_norm(side, tokens, hot, parts, block):
    ring = side.shape[0] // 2
    rows, width = tokens.shape
    return pl.pallas_call(
        norm_kernel,
        grid_spec=pltpu.PrefetchScalarGridSpec(
            num_scalar_prefetch=1,
            grid=(rows // block,),
            in_specs=[
                pl.BlockSpec((block, width), lambda i, y: ((i + y[0]) % 3, 0)),
                pl.BlockSpec((block, hot.shape[1]), lambda i, y: (i, 0)),
                pl.BlockSpec((1,) + parts.shape[1:], lambda i, y: (0, 0, 0)),
            ],
            out_specs=[
                pl.BlockSpec((block, width), lambda i, y: (jnp.minimum(i, 1), 0)),
                pl.BlockSpec((block, width), lambda i, y: (0, 0)),
                pl.BlockSpec((ring, width // ring, block), lambda i, y: (0, 0, i)),
            ],
        ),
        out_shape=[
            shape((2 * block, width), BF),
            shape((block, width), BF),
            shape((ring, width // ring, rows), BF),
        ],
        compiler_params=params(),
        cost_estimate=cost(2 * rows * width * (width + 512), rows * width * 6),
    )(side, tokens, hot, parts)


def project_kernel(side, first_in, second_in, w_ref, bias_ref, first, second):
    padded = first.shape[2]
    cols = bias_ref.shape[2]
    for hidden, ref in ((first_in, first), (second_in, second)):
        value = (rows_by_columns(hidden[...], w_ref[0, :, :cols]) + bias_ref[0]).astype(BF)
        ref[0] = jnp.concatenate([value, jnp.zeros((value.shape[0], padded - cols), BF)], axis=1)


def project(side, first, second, weights, bias, padded, block, groups):
    width = first.shape[1]
    pick = lambda a, y: a + y[0] - 2 * a * y[0]
    last = second.shape[0] // block - 1
    pair = pl.BlockSpec((1, block, padded), lambda a, y: (a, 0, 0))
    return pl.pallas_call(
        project_kernel,
        grid_spec=pltpu.PrefetchScalarGridSpec(
            num_scalar_prefetch=1,
            grid=(groups,),
            in_specs=[
                pl.BlockSpec((block, width), lambda a, y: (0, 0)),
                pl.BlockSpec((block, width), lambda a, y: (last, 0)),
                pl.BlockSpec((1,) + weights.shape[1:], lambda a, y: (pick(a, y), 0, 0)),
                pl.BlockSpec((1,) + bias.shape[1:], lambda a, y: (pick(a, y), 0, 0)),
            ],
            out_specs=[pair, pair],
        ),
        out_shape=[shape((groups, block, padded), BF)] * 2,
        compiler_params=params(60),
        cost_estimate=cost(
            4 * groups * block * width * padded, 4 * groups * (block + width) * padded
        ),
    )(side, first, second, weights, bias)


MARKS = 16
DEPTH = 128
LSE_AT = HEAD_DIM + MARKS - 4
STEEP = HEAD_DIM**-0.5 * LOG2E


def marks_kernel(*refs):
    count = len(refs) // 4
    for n in range(count):
        seg_ref, open_ref = refs[2 * n : 2 * n + 2]
        query_ref, key_ref = refs[2 * count + 2 * n : 2 * count + 2 * n + 2]
        tiles, length = open_ref.shape
        slots = MARKS - 4 - tiles
        slot = lax.broadcasted_iota(jnp.int32, (slots, length), 0)
        own_slot = slot == seg_ref[...]
        tile = lax.broadcasted_iota(jnp.int32, (tiles, length), 0)
        own_tile = tile == lax.broadcasted_iota(jnp.int32, (tiles, length), 1) // TILE
        seen = jnp.concatenate(
            [jnp.where(own_slot, 0.0, MASKED_SCORE), jnp.where(open_ref[...] > 0, 0.0, MASKED_SCORE)],
            axis=0,
        )
        chosen = jnp.concatenate(
            [jnp.where(own_slot, 1.0, 0.0), jnp.where(own_tile, 1.0, 0.0)], axis=0
        )
        rest = (MARKS - slots - tiles, length)
        query_ref[...] = jnp.concatenate([chosen, jnp.zeros(rest, F32)], axis=0).T.astype(BF)
        key_ref[...] = jnp.concatenate([seen, jnp.ones(rest, F32)], axis=0).T.astype(BF)


def marks_of(*rows):
    length = rows[1].shape[1]
    return pl.pallas_call(
        marks_kernel,
        out_shape=[shape((length, MARKS), BF)] * len(rows),
        compiler_params=params(16),
    )(*rows)


def split_three(values):
    high = values.astype(BF)
    rest = values - high.astype(F32)
    middle = rest.astype(BF)
    return jnp.concatenate([high, middle, (rest - middle.astype(F32)).astype(BF)], axis=1)


def at_head(h, part, heads):
    start = (part * heads + h) * HEAD_DIM
    return slice(start, start + HEAD_DIM)


def both_halves(first, second, columns):
    return jnp.concatenate([first[0, :, columns], second[0, :, columns]], axis=0)


def padded_columns(parts, width):
    found = jnp.concatenate(parts, axis=1)
    gap = width - found.shape[1]
    return jnp.concatenate([found, jnp.zeros((found.shape[0], gap), found.dtype)], axis=1)


def attend_kernel(
    heads, first, second, qm_ref, km_ref, o_first, o_second, l_first, l_second, keys, values, queries
):
    i = pl.program_id(1)

    @pl.when((i == 0) & (pl.program_id(0) == 0))
    def _():
        keys[...] = jnp.zeros_like(keys)
        queries[...] = jnp.zeros_like(queries)

    @pl.when(i == 0)
    def _():
        for h in range(heads):
            keys[h, :, :HEAD_DIM] = both_halves(first, second, at_head(h, 1, heads))
            keys[h, :, HEAD_DIM : HEAD_DIM + MARKS] = km_ref[...]
            value = both_halves(first, second, at_head(h, 2, heads))
            values[h] = value.astype(F32).T.astype(BF)

    for h in range(heads):
        columns = at_head(h, 0, heads)
        queries[h, :, :HEAD_DIM] = jnp.where(i == 0, first[0, :, columns], second[0, :, columns])
        queries[h, :, HEAD_DIM : HEAD_DIM + MARKS] = qm_ref[...]
    parts = []
    totals = []
    probs = None
    scores = contract_last(keys[0], queries[0])
    for h in range(heads):
        later = contract_last(keys[h + 1], queries[h + 1]) if h + 1 < heads else None
        top = jnp.max(scores, axis=0, keepdims=True)
        powers = jnp.exp2((scores - top) * STEEP)
        total = jnp.sum(powers, axis=0, keepdims=True)
        totals.append(top + jnp.log2(total) * (1.0 / STEEP))
        if h > 0:
            parts.append(rows_by_columns(values[h - 1], probs).T.astype(BF))
        probs = (powers * (1.0 / total)).astype(BF)
        scores = later
    parts.append(rows_by_columns(values[heads - 1], probs).T.astype(BF))
    out = padded_columns(parts, o_first.shape[2])
    log_totals = jnp.concatenate(totals, axis=0)

    @pl.when(i == 0)
    def _():
        o_first[0] = out
        l_first[0] = log_totals

    @pl.when(i == 1)
    def _():
        o_second[0] = out
        l_second[0] = log_totals


def attend(first, second, query_marks, key_marks, out_width, group):
    groups = 1
    _, half, padded = first.shape
    heads = out_width // HEAD_DIM
    pair = lambda *dims: pl.BlockSpec((1,) + dims, lambda a, i: (a, 0, 0))
    return pl.pallas_call(
        partial(attend_kernel, heads),
        grid=(groups, 2),
        in_specs=[
            pl.BlockSpec((1, half, padded), lambda a, i: (group, 0, 0)),
            pl.BlockSpec((1, half, padded), lambda a, i: (group, 0, 0)),
            pl.BlockSpec((half, MARKS), lambda a, i: (i, 0)),
            pl.BlockSpec((2 * half, MARKS), lambda a, i: (0, 0)),
        ],
        out_specs=[pair(half, out_width)] * 2 + [pair(heads, half)] * 2,
        out_shape=[shape((groups, half, out_width), BF)] * 2 + [shape((groups, heads, half), F32)] * 2,
        scratch_shapes=[
            pltpu.VMEM((heads, 2 * half, DEPTH), BF),
            pltpu.VMEM((heads, HEAD_DIM, 2 * half), BF),
            pltpu.VMEM((heads, half, DEPTH), BF),
        ],
        compiler_params=params(),
        cost_estimate=cost(groups * 15e9, groups * half * padded * 6, groups * heads * half * half),
    )(first, second, query_marks, key_marks)


def attend_back_kernel(
    heads, first, second, do_first, do_second, l_first, l_second, qm_ref, km_ref,
    out_first, out_second, keys, values, turned, queries, dk, dv,
):
    i = pl.program_id(1)
    half, padded = first.shape[1:]
    width = heads * HEAD_DIM
    scaling = HEAD_DIM**-0.5

    @pl.when((i == 0) & (pl.program_id(0) == 0))
    def _():
        keys[...] = jnp.zeros_like(keys)
        queries[...] = jnp.zeros_like(queries)

    @pl.when(i == 0)
    def _():
        for h in range(heads):
            key = both_halves(first, second, at_head(h, 1, heads))
            keys[h, :, :HEAD_DIM] = key
            keys[h, :, HEAD_DIM : HEAD_DIM + MARKS] = km_ref[...]
            turned[h] = key.astype(F32).T.astype(BF)
            values[h] = both_halves(first, second, at_head(h, 2, heads))
        dk[...] = jnp.zeros_like(dk)
        dv[...] = jnp.zeros_like(dv)

    log_totals = jnp.where(i == 0, l_first[0], l_second[0]).T
    plain = []
    for h in range(heads):
        columns = at_head(h, 0, heads)
        query = jnp.where(i == 0, first[0, :, columns], second[0, :, columns])
        grad = jnp.where(i == 0, do_first[0, :, columns], do_second[0, :, columns])
        queries[h, :, :HEAD_DIM] = query
        queries[h, :, HEAD_DIM : HEAD_DIM + MARKS] = qm_ref[...]
        queries[h, :, LSE_AT : LSE_AT + 3] = split_three(-log_totals[:, h : h + 1])
        plain.append((query, grad))

    def scores_of(h):
        return contract_last(keys[h], queries[h]), contract_last(values[h], plain[h][1])

    def finish(h, probs, grad_scores):
        query, grad = plain[h]
        dv[h] += rows_by_columns(probs, grad)
        dk[h] += rows_by_columns(grad_scores, query)
        return (rows_by_columns(turned[h], grad_scores) * scaling).T.astype(BF)

    parts = []
    before = None
    scores, grad_probs = scores_of(0)
    for h in range(heads):
        later = scores_of(h + 1) if h + 1 < heads else (None, None)
        probs = jnp.exp2(scores * STEEP)
        centre = jnp.sum(probs * grad_probs, axis=0, keepdims=True)
        grad_scores = (probs * (grad_probs - centre)).astype(BF)
        if before is not None:
            parts.append(finish(h - 1, *before))
        before = (probs.astype(BF), grad_scores)
        scores, grad_probs = later
    parts.append(finish(heads - 1, *before))
    grad_queries = jnp.concatenate(parts, axis=1)

    @pl.when(i == 0)
    def _():
        out_first[0, :, :width] = grad_queries

    @pl.when(i == 1)
    def _():
        out_second[0, :, :width] = grad_queries
        for start, ref in ((0, out_first), (half, out_second)):
            rows = slice(start, start + half)
            ref[0, :, width:] = padded_columns(
                [(dk[h, rows] * scaling).astype(BF) for h in range(heads)]
                + [dv[h, rows].astype(BF) for h in range(heads)],
                padded - width,
            )


def attend_back(first, second, do_first, do_second, l_first, l_second, query_marks, key_marks):
    groups, half, padded = first.shape
    heads = l_first.shape[1]
    out_width = do_first.shape[2]
    pair = lambda *dims: pl.BlockSpec((1,) + dims, lambda a, i: (a, 0, 0))
    return pl.pallas_call(
        partial(attend_back_kernel, heads),
        grid=(groups, 2),
        in_specs=[pair(half, padded)] * 2
        + [pair(half, out_width)] * 2
        + [pair(heads, half)] * 2
        + [
            pl.BlockSpec((half, MARKS), lambda a, i: (i, 0)),
            pl.BlockSpec((2 * half, MARKS), lambda a, i: (0, 0)),
        ],
        out_specs=[pair(half, padded)] * 2,
        out_shape=[shape((groups, half, padded), BF)] * 2,
        scratch_shapes=[
            pltpu.VMEM((heads, 2 * half, DEPTH), BF),
            pltpu.VMEM((heads, 2 * half, HEAD_DIM), BF),
            pltpu.VMEM((heads, HEAD_DIM, 2 * half), BF),
            pltpu.VMEM((heads, half, DEPTH), BF),
            pltpu.VMEM((heads, 2 * half, HEAD_DIM), F32),
            pltpu.VMEM((heads, 2 * half, HEAD_DIM), F32),
        ],
        compiler_params=params(60),
        cost_estimate=cost(groups * 12e9, groups * half * padded * 12, groups * heads * half * half),
    )(first, second, do_first, do_second, l_first, l_second, query_marks, key_marks)


def image_sums(hot_turned, values):
    high = values.astype(BF)
    low = (values - high.astype(F32)).astype(BF)
    return rows_by_columns(hot_turned, high) + rows_by_columns(hot_turned, low)


def add_up(ref, value):
    @pl.when(pl.program_id(0) == 0)
    def _():
        ref[...] = value

    @pl.when(pl.program_id(0) != 0)
    def _():
        ref[...] += value


def third_of(first, second, own, other, i, per):
    half = jnp.stack([own[0], other[0]], axis=0)
    return jnp.where(i < per, first[...], jnp.where(i < 2 * per, second[...], half))


def thirds_of(first, second, half, i, per):
    return [
        jnp.where(i < per, a[0], jnp.where(i < 2 * per, b[0], c[0]))
        for a, b, c in zip(first, second, half)
    ]


def single_specs(block, columns, per):
    return [
        pl.BlockSpec(
            (1, block, columns), lambda i, y, k=k: (0, jnp.clip(i - k * per, 0, per - 1), 0)
        )
        for k in (0, 0, 1, 1, 2, 2)
    ]


def third_specs(block, columns, per):
    full = lambda low: pl.BlockSpec(
        (2, block, columns), lambda i, y: (0, jnp.clip(i - low * per, 0, per - 1), 0)
    )
    single = pl.BlockSpec((1, block, columns), lambda i, y: (0, jnp.clip(i - 2 * per, 0, per - 1), 0))
    return [full(0), full(1), single, single]


def out_weight_specs(width, columns):
    last = columns // (2 * width // 3) - 1
    return [
        pl.BlockSpec((1, width, 2 * width // 3), lambda i, y: (y[0], 0, last)),
        pl.BlockSpec((1, width, 2 * width // 3), lambda i, y: (1 - y[0], 0, last)),
    ]


def middle_kernel(
    side, tok_ref, dy_ref, first, first_other, second, second_other, own, other, w_own, w_other, b_ref, hot_ref,
    parts_ref, branch_ref, h_ref, g_ref, ht_ref, gt_ref, gb_ref,
):
    i = pl.program_id(0)
    width = tok_ref.shape[1]
    used = width // 2
    per = pl.num_programs(0) // 3
    att = thirds_of((first, first_other), (second, second_other), (own, other), i, per)
    skip = w_own.shape[2] - used
    branch = (
        contract_last(att[0][:, :used], w_own[0, :, skip:])
        + contract_last(att[1][:, :used], w_other[0, :, skip:])
        + b_ref[...]
    )
    branch_ref[...] = branch
    hot = hot_ref[...]
    gate = rows_by_columns(hot, parts_ref[0, :, 2 * width :])
    mod = rows_by_columns(hot, parts_ref[1])
    normed, _ = layer_norm(tok_ref[...].astype(F32) + gate * branch)
    hidden = (normed * (1.0 + mod[:, width : 2 * width]) + mod[:, :width]).astype(BF)
    grad = (dy_ref[...].astype(F32) * mod[:, 2 * width :]).astype(BF)
    h_ref[...] = hidden
    g_ref[...] = grad
    turn_in_order(side, ht_ref, hidden)
    turn_in_order(side, gt_ref, grad)
    add_up(gb_ref, jnp.sum(grad.astype(F32), axis=0, keepdims=True))


def middle_part(side, tokens, cotangent, thirds, weights, b_out, hot, parts, block):
    ring = side.shape[0] // 2
    rows, width = tokens.shape
    per = rows // 3 // block
    spec = lambda dims: pl.BlockSpec(dims, lambda i, y: (0,) * len(dims))
    placed = pl.BlockSpec(
        (block, width), lambda i, y: (((i // per + y[0]) % 3) * per + i % per, 0)
    )
    plain = pl.BlockSpec((block, width), lambda i, y: (i, 0))
    turned = pl.BlockSpec((ring, width // ring, block), lambda i, y: (0, 0, i))
    return pl.pallas_call(
        middle_kernel,
        grid_spec=pltpu.PrefetchScalarGridSpec(
            num_scalar_prefetch=1,
            grid=(rows // block,),
            in_specs=[
                placed,
                placed,
                *single_specs(block, thirds[0].shape[2], per),
                *out_weight_specs(width, weights.shape[2]),
                spec((1, width)),
                pl.BlockSpec((block, hot.shape[1]), lambda i, y: (i, 0)),
                spec(parts.shape),
            ],
            out_specs=[plain, plain, plain, turned, turned, spec((1, width))],
        ),
        out_shape=[
            shape((rows, width), F32),
            shape((rows, width), BF),
            shape((rows, width), BF),
            shape((ring, width // ring, rows), BF),
            shape((ring, width // ring, rows), BF),
            shape((1, width), F32),
        ],
        compiler_params=params(),
        cost_estimate=cost(2 * rows * width * (3 * width + 1024), rows * width * 22),
    )(side, tokens, cotangent, *thirds, weights, weights, b_out, hot, parts)


def feed_kernel(
    chunk, pick, h_ref, g_ref, ht_ref, gt_ref, up_ref, down_ref, bias_ref,
    branch_ref, back_ref, mine_ref, near_ref, far_ref, gb_ref, act, pre,
):
    j = pl.program_id(0)
    rows = h_ref.shape[0]
    half = ht_ref.shape[0] // 2
    up = up_ref[0, 0]
    down = down_ref[0, 0]
    total = jnp.zeros(gb_ref.shape, F32)
    for start in range(0, rows, chunk):
        at = slice(start, start + chunk)
        u = rows_by_columns(h_ref[at], up) + bias_ref[0]
        grad = rows_by_columns(g_ref[at], down)
        cube = GELU_CUBE * u * u
        bent = jnp.tanh(GELU_SLOPE * (u + cube * u))
        part = 0.5 * (1.0 + bent)
        slope = part + 0.5 * u * (1.0 - bent * bent) * (GELU_SLOPE * (1.0 + 3.0 * cube))
        low = (u * part).astype(BF)
        back = (grad * slope).astype(BF)
        act[at] = low
        pre[at] = back
        total += jnp.sum(back.astype(F32), axis=0, keepdims=True)
        branch_part = contract_last(low, down)
        back_part = contract_last(back, up)

        @pl.when(j == 0)
        def _():
            branch_ref[at] = branch_part
            back_ref[at] = back_part

        @pl.when(j != 0)
        def _():
            branch_ref[at] += branch_part
            back_ref[at] += back_part

    gb_ref[...] = total
    quarter = half // 2
    for k, (turned, value) in enumerate(((ht_ref, pre), (gt_ref, act))):
        theirs = rows_by_columns(turned[half:], value[...]).astype(BF)
        near_ref[k] = theirs[:quarter]
        far_ref[k] = theirs[quarter:]
        mine_ref[k] = rows_by_columns(turned[:half], value[...])


def feed(pick, hidden, grad, hidden_turned, grad_turned, weights, bias, chunk, cols):
    rows, width = hidden.shape
    units = weights.shape[3]
    half = width // 2
    whole = lambda dims: pl.BlockSpec(dims, lambda j, y: (0, 0), pipeline_mode=pl.Buffered(1))
    columns = lambda k: pl.BlockSpec((1, 1, width, cols), lambda j, y: (k, y[0], 0, j))
    return pl.pallas_call(
        partial(feed_kernel, chunk),
        grid_spec=pltpu.PrefetchScalarGridSpec(
            num_scalar_prefetch=1,
            grid=(units // cols,),
            in_specs=[
                whole((rows, width)),
                whole((rows, width)),
                whole((width, rows)),
                whole((width, rows)),
                columns(0),
                columns(1),
                pl.BlockSpec((1, 1, cols), lambda j, y: (y[0], 0, j)),
            ],
            out_specs=[
                whole((rows, width)),
                whole((rows, width)),
                pl.BlockSpec((2, half, cols), lambda j, y: (0, 0, j)),
                pl.BlockSpec((2, half // 2, cols), lambda j, y: (0, 0, j)),
                pl.BlockSpec((2, half // 2, cols), lambda j, y: (0, 0, j)),
                pl.BlockSpec((1, cols), lambda j, y: (0, j)),
            ],
            scratch_shapes=[pltpu.VMEM((rows, cols), BF), pltpu.VMEM((rows, cols), BF)],
        ),
        out_shape=[
            shape((rows, width), F32),
            shape((rows, width), F32),
            shape((2, half, units), F32),
            shape((2, half // 2, units), BF),
            shape((2, half // 2, units), BF),
            shape((1, units), F32),
        ],
        compiler_params=params(60),
        cost_estimate=cost(
            12 * rows * width * units, rows * width * 16 + width * units * 10, rows * units
        ),
    )(pick, hidden, grad, hidden_turned, grad_turned, weights, weights, bias)


def back_two_kernel(
    side, tok_ref, dy_ref, branch_ref, two_a, two_b, b_ref, back_a, back_b, w_own, w_other, hot_ref,
    turn_ref, parts_ref, first, first_other, second, second_other, half_own, half_other, out_ref, middle_ref, a_first, a_second,
    a_own, a_other, sums_ref, gb_ref, mine_ref, theirs_ref, outer_ref,
):
    width = tok_ref.shape[1]
    hot = hot_ref[...]
    turn = turn_ref[...]
    gate = rows_by_columns(hot, parts_ref[0, :, 2 * width :])
    mod = rows_by_columns(hot, parts_ref[1])
    branch = branch_ref[...]
    middle = tok_ref[...].astype(F32) + gate * branch
    branch_two = two_a[...] + two_b[...] + b_ref[...]
    grad_hidden = back_a[...] + back_b[...]
    dy = dy_ref[...].astype(F32)
    out_ref[...] = (middle + mod[:, 2 * width :] * branch_two).astype(BF)
    normed, inverse = layer_norm(middle)
    grad_middle = dy + norm_back(normed, inverse, grad_hidden * (1.0 + mod[:, width : 2 * width]))
    middle_ref[...] = grad_middle
    grad = (grad_middle * gate).astype(BF)
    turned = grad.astype(F32).T.astype(BF)
    att = thirds_of(
        (first, first_other),
        (second, second_other),
        (half_own, half_other),
        pl.program_id(0),
        pl.num_programs(0) // 3,
    )
    for k in range(2):
        product = rows_by_columns(turned, att[k])

        @pl.when(pl.program_id(0) == 0)
        def _():
            outer_ref[k] = product

        @pl.when(pl.program_id(0) != 0)
        def _():
            outer_ref[k] += product

    @pl.when(pl.program_id(0) == pl.num_programs(0) - 1)
    def _():
        ring = side.shape[0] // 2
        piece = width // ring
        for k in range(2):
            pieces = [
                outer_ref[k, pl.ds(pl.multiple_of(side[1 + ring + j] * piece, 8), piece)]
                for j in range(ring)
            ]
            mine_ref[k] = jnp.concatenate(pieces[: ring // 2], axis=0)
            theirs_ref[k] = jnp.concatenate(pieces[ring // 2 :], axis=0).astype(BF)

    skip = w_own.shape[2] - width // 2
    ours = padded_columns([rows_by_columns(grad, w_own[0, :, skip:]).astype(BF)], a_own.shape[2])
    theirs = padded_columns([rows_by_columns(grad, w_other[0, :, skip:]).astype(BF)], a_own.shape[2])
    i = pl.program_id(0)
    per = pl.num_programs(0) // 3
    for k, ref in enumerate((a_first, a_second)):

        @pl.when(i // per == k)
        def _(ref=ref):
            ref[0] = ours
            ref[1] = theirs

    @pl.when(i // per == 2)
    def _():
        a_own[0] = ours
        a_other[0] = theirs

    sums = [
        image_sums(turn, grad_middle * branch),
        image_sums(turn, grad_hidden),
        image_sums(turn, grad_hidden * normed),
        image_sums(turn, dy * branch_two),
    ]
    add_up(sums_ref, jnp.stack(sums, axis=0))
    add_up(gb_ref, jnp.sum(grad.astype(F32), axis=0, keepdims=True))


def back_two(
    side, tokens, cotangent, branch, two_a, two_b, b_down, back_a, back_b, weights, hot, turn, parts,
    attended, block, images, out_width,
):
    rows, width = tokens.shape
    third = rows // 3
    per = rows // 3 // block
    spec = lambda dims: pl.BlockSpec(dims, lambda i, y: (0,) * len(dims))
    placed = pl.BlockSpec(
        (block, width), lambda i, y: (((i // per + y[0]) % 3) * per + i % per, 0)
    )
    plain = pl.BlockSpec((block, width), lambda i, y: (i, 0))
    return pl.pallas_call(
        back_two_kernel,
        grid_spec=pltpu.PrefetchScalarGridSpec(
            num_scalar_prefetch=1,
            grid=(rows // block,),
            in_specs=[
                placed,
                placed,
                plain,
                plain,
                plain,
                spec((1, width)),
                plain,
                plain,
                *out_weight_specs(width, weights.shape[2]),
                pl.BlockSpec((block, hot.shape[1]), lambda i, y: (i, 0)),
                pl.BlockSpec((images, block), lambda i, y: (0, i)),
                spec(parts.shape),
                *single_specs(block, out_width, per),
            ],
            out_specs=[
                placed,
                plain,
                *third_specs(block, out_width, per),
                spec((4, images, width)),
                spec((1, width)),
                spec((2, width // 2, out_width)),
                spec((2, width // 2, out_width)),
            ],
            scratch_shapes=[pltpu.VMEM((2, width, out_width), F32)],
        ),
        out_shape=[
            shape((rows, width), BF),
            shape((rows, width), F32),
            *[shape((2, third, out_width), BF)] * 2,
            *[shape((1, third, out_width), BF)] * 2,
            shape((4, images, width), F32),
            shape((1, width), F32),
            shape((2, width // 2, out_width), F32),
            shape((2, width // 2, out_width), BF),
        ],
        compiler_params=params(62),
        cost_estimate=cost(2 * rows * width * (4 * width + 1024), rows * width * 34),
    )(side, tokens, cotangent, branch, two_a, two_b, b_down, back_a, back_b, weights, weights, hot, turn, parts, *attended)


def outer_kernel(ht_ref, first, second, rest, mine_ref, theirs_ref, sums_ref):
    third = first.shape[1]
    grads = (first[0], second[0], rest[0])
    found = sum(
        rows_by_columns(ht_ref[:, k * third : (k + 1) * third], grad)
        for k, grad in enumerate(grads)
    )

    @pl.when(pl.program_id(0) == 0)
    def _():
        theirs_ref[...] = found.astype(BF)
        sums_ref[...] = sum(jnp.sum(grad.astype(F32), axis=0, keepdims=True) for grad in grads)

    @pl.when(pl.program_id(0) == 1)
    def _():
        mine_ref[...] = found


def outer(turned, first, second, rest, group):
    width, rows = turned.shape
    _, third, cols = first.shape
    block = pl.BlockSpec((width // 2, cols), lambda k: (0, 0))
    pair = pl.BlockSpec((1, third, cols), lambda k: (group, 0, 0))
    single = pl.BlockSpec((1, third, cols), lambda k: (0, 0, 0))
    return pl.pallas_call(
        outer_kernel,
        grid=(2,),
        in_specs=[pl.BlockSpec((width // 2, rows), lambda k: (1 - k, 0)), pair, pair, single],
        out_specs=[block, block, pl.BlockSpec((1, cols), lambda k: (0, 0))],
        out_shape=[shape((width // 2, cols), F32), shape((width // 2, cols), BF), shape((1, cols), F32)],
        compiler_params=params(60),
        cost_estimate=cost(2 * rows * width * cols, rows * width * 2 + rows * cols * 4),
    )(turned, first, second, rest)


def back_one_kernel(
    side, first, second, own, other, w_own, w_other, tok_ref, middle_ref, hot_ref, turn_ref, parts_ref,
    out_ref, sums_ref,
):
    width = tok_ref.shape[1]
    cols = 3 * width // 2
    scale = rows_by_columns(hot_ref[...], parts_ref[0, :, width : 2 * width])
    grads = third_of(first, second, own, other, pl.program_id(0), pl.num_programs(0) // 3)[:, :, :cols]
    grad_hidden = contract_last(grads[0], w_own[0, :, :cols]) + contract_last(
        grads[1], w_other[0, :, :cols]
    )
    normed, inverse = layer_norm(tok_ref[...].astype(F32))
    out_ref[...] = middle_ref[...] + norm_back(normed, inverse, grad_hidden * (1.0 + scale))
    turn = turn_ref[...]
    sums = [image_sums(turn, grad_hidden), image_sums(turn, grad_hidden * normed)]
    add_up(sums_ref, jnp.stack(sums, axis=0))


def back_one(side, thirds, weights, tokens, middle, hot, turn, parts, block, images):
    rows, width = tokens.shape
    cols = thirds[0].shape[2]
    per = rows // 3 // block
    spec = lambda dims: pl.BlockSpec(dims, lambda i, y: (0,) * len(dims))
    once = pl.Buffered(1)
    placed = pl.BlockSpec(
        (block, width), lambda i, y: (((i // per + y[0]) % 3) * per + i % per, 0)
    )
    return pl.pallas_call(
        back_one_kernel,
        grid_spec=pltpu.PrefetchScalarGridSpec(
            num_scalar_prefetch=1,
            grid=(rows // block,),
            in_specs=[
                *third_specs(block, cols, per),
                pl.BlockSpec(
                    (1,) + weights.shape[1:], lambda i, y: (y[0], 0, 0), pipeline_mode=once
                ),
                pl.BlockSpec(
                    (1,) + weights.shape[1:], lambda i, y: (1 - y[0], 0, 0), pipeline_mode=once
                ),
                placed,
                pl.BlockSpec((block, width), lambda i, y: (i, 0)),
                pl.BlockSpec((block, hot.shape[1]), lambda i, y: (i, 0)),
                pl.BlockSpec((images, block), lambda i, y: (0, i)),
                spec(parts.shape),
            ],
            out_specs=[placed, spec((2, images, width))],
        ),
        out_shape=[shape((rows, width), F32), shape((2, images, width), F32)],
        compiler_params=params(),
        cost_estimate=cost(4 * rows * width * cols, rows * width * 10 + rows * cols * 4),
    )(side, *thirds, weights, weights, tokens, middle, hot, turn, parts)


def fast_body(mesh):
    ring = mesh.shape["rows"]
    both = ("rows", "heads")

    def moves(row_of, other_heads):
        pairs = []
        for r in range(ring):
            for y in range(2):
                pairs.append((2 * r + y, 2 * row_of(r) + (1 - y if other_heads else y)))
        return pairs

    to_core = moves(lambda r: r ^ 1, False)
    to_heads = moves(lambda r: r, True)
    to_x = moves(lambda r: r ^ 2, False)
    to_corner = moves(lambda r: r ^ 2, True)
    levels = ring // 4
    to_level = [moves(lambda r, k=k: (r + 4 * k) % ring, False) for k in range(levels)]

    def send(values, pairs):
        return lax.ppermute(values, both, pairs)

    def after(*values):
        return lax.optimization_barrier(values)

    def body(
        tokens,
        condition,
        segment_ids,
        tile_mask,
        image_index,
        w_ada,
        b_ada,
        w_query,
        w_key,
        w_value,
        b_query,
        b_value,
        w_out,
        b_out,
        w_up,
        b_up,
        w_down,
        b_down,
        cotangent,
    ):
        y = lax.axis_index("heads")
        r = lax.axis_index("rows")
        rows, width = tokens.shape
        length = segment_ids.shape[1]
        third = rows // 3
        images = condition.shape[0]
        units = w_up.shape[1]
        cols = w_query.shape[1]

        tiles = length // TILE
        slots = image_index.shape[1]

        def open_to(tiles_on):
            on = (tiles_on > 0) | jnp.eye(tiles, dtype=bool)
            return jnp.repeat(on.astype(jnp.int32), TILE, axis=1)

        seg_full = lax.dynamic_index_in_dim(segment_ids, 2 * y, 0, keepdims=False)
        tile_full = lax.dynamic_index_in_dim(tile_mask, 2 * y, 0, keepdims=False)
        seg_half = jnp.where(y == 0, segment_ids[1], jnp.roll(segment_ids[1], -third))
        shift = third // TILE
        tile_half = jnp.where(
            y == 0, tile_mask[1], jnp.roll(tile_mask[1], (-shift, -shift), axis=(0, 1))
        )
        marks = marks_of(seg_full[None], open_to(tile_full), seg_half[None], open_to(tile_half))

        def image_of(seg, index):
            slot = jnp.arange(slots, dtype=jnp.int32)
            return jnp.sum(jnp.where(seg[:, None] == slot[None, :], index[None, :], 0), axis=1)

        own_image = jnp.concatenate(
            [
                image_of(seg_full, lax.dynamic_index_in_dim(image_index, 2 * y, 0, keepdims=False)),
                image_of(seg_half[:third], image_index[1]),
            ]
        )
        chosen = jnp.arange(images, dtype=jnp.int32)
        hot = (own_image[:, None] == jnp.tile(chosen, 3)[None, :]).astype(BF)
        turn = (chosen[:, None] == own_image[None, :]).astype(BF)

        order = jnp.arange(ring, dtype=jnp.int32)
        core_of, x_of, level_of = order // (ring // 2), (order // levels) % 2, order % levels
        owner = ((r // 4 + level_of) % levels) * 4 + ((r // 2 % 2) ^ x_of) * 2 + ((r % 2) ^ core_of)
        piece = width // ring
        place = jnp.sum(jnp.where(owner[None, :] == order[:, None], order[None, :], 0), axis=1)
        side = jnp.concatenate([y.reshape(1), place, owner])

        padded = -(-3 * cols // 128) * 128
        out_width = -(-cols // 128) * 128
        here = jnp.stack([y, r // 4, (r // 2) % 2, r % 2]).astype(jnp.int32)
        next_level = to_level[levels - 1]

        class Tree:
            def __init__(self, shard):
                self.count = shard.shape[-1] // 3
                self.first = [shard[..., : 2 * self.count]]
                self.last = [shard[..., 2 * self.count :]]
                self.step = 0

            def sends(self):
                moves = (
                    (next_level, to_x),
                    (next_level, to_heads),
                    (next_level, next_level),
                    (to_x, to_heads, next_level),
                    (to_heads, to_x, next_level),
                    (to_core,) * 5,
                )[self.step]
                if self.step < 3:
                    self.sent = (self.first[-1], self.last[-1])
                elif self.step < 5:
                    self.sent = (self.over_x, self.over_y, self.last[-1])
                else:
                    self.sent = (*self.over_x, *self.over_y, self.last)
                return [send(value, move) for value, move in zip(self.sent, moves)]

            def take(self, got):
                if self.step < 2:
                    self.first.append(got[0])
                    self.last = [jnp.stack([self.last[0], got[1]])]
                elif self.step == 2:
                    whole = jnp.stack([*self.first, got[0]])
                    self.over_x, self.over_y = whole[..., : self.count], whole[..., self.count :]
                    self.last.append(got[1])
                elif self.step == 3:
                    self.over_x = jnp.stack([self.over_x, got[0]])
                    self.over_y = jnp.stack([self.over_y, got[1]])
                    self.last.append(got[2])
                elif self.step == 4:
                    self.over_x = (self.over_x, got[0])
                    self.over_y = (self.over_y, got[1])
                    self.last = jnp.stack([*self.last, got[2]])
                else:
                    self.whole = collected(here, (*self.sent, *got))
                self.step += 1

        shard = jnp.concatenate([w_query, w_key, w_value, w_out], axis=1).astype(BF)
        tree = Tree(shard[None])
        cond = condition.astype(F32)
        mod_cols, *got = after(
            jnp.dot(jax.nn.silu(cond), w_ada, precision=PRECISE) + b_ada, *tree.sends()
        )
        tree.take(got)
        biases = jnp.concatenate([b_up, b_query, b_value])[None]
        own_spread = jnp.concatenate([mod_cols, biases], axis=0)
        got_spread, hot, turn, side, *joined = after(
            send(own_spread, to_heads), hot, turn, side, *marks, *tree.sends()
        )
        marks_full, marks_half = joined[:2], joined[2:4]
        tree.take(joined[4:])
        spread = jnp.where(
            y == 0, jnp.stack([own_spread, got_spread]), jnp.stack([got_spread, own_spread])
        )
        parts = three_parts(spread[:, :images])
        up_bias = spread[:, images:, :units]
        qkv_bias = jnp.concatenate(
            [
                spread[:, images:, units : units + cols],
                jnp.zeros((2, 1, cols), F32),
                spread[:, images:, units + cols :],
            ],
            axis=2,
        )
        hidden_full, hidden_half, hidden_one_turned, qkv_bias, up_bias, *got = after(
            *first_norm(side, tokens, hot, parts, third), qkv_bias, up_bias, *tree.sends()
        )
        tree.take(got)
        feed_shard = jnp.stack([w_up, w_down]).astype(BF)
        hidden_full, hidden_half, feed_shard, *got = after(
            hidden_full, hidden_half, feed_shard, *tree.sends()
        )
        tree.take(got)
        hidden_full, hidden_half, *got = after(hidden_full, hidden_half, *tree.sends())
        tree.take(got)
        feed_weights = lax.all_gather(
            feed_shard, ("heads", "rows"), axis=1, tiled=True
        ).reshape(2, 2, width, units)
        hidden_full, hidden_half, *got = after(hidden_full, hidden_half, *tree.sends())
        tree.take(got)
        attention_weights = tree.whole.reshape(2, width, shard.shape[1])

        qkv_first, qkv_second = project(
            side, hidden_full, hidden_full, attention_weights, qkv_bias, padded, third, 2
        )
        qkv_full = (qkv_first, qkv_second)
        qkv_first, hidden_half, condition = after(qkv_first, hidden_half, condition)
        first_0, second_0, l_first_0, l_second_0, hidden_got, *got = after(
            *attend(qkv_first, qkv_second, *marks_full, out_width, 0),
            send(hidden_half, to_heads),
            *(send(condition, to_level[k]) for k in range(1, levels)),
        )
        flat = jnp.stack([condition, *got])
        qkv_half = project(
            side, hidden_half, hidden_got, attention_weights, qkv_bias, padded, third, 1
        )
        out_own, out_theirs, l_own, l_other, got = after(
            *attend(*qkv_half, *marks_half, out_width, 0), send(flat, to_x)
        )
        lse_half = (l_own, l_other)
        flat = jnp.concatenate([flat, got], axis=0)
        qkv_first, out_theirs, flat = after(qkv_first, out_theirs, flat)
        first_1, second_1, l_first_1, l_second_1, out_other = after(
            *attend(qkv_first, qkv_second, *marks_full, out_width, 1), send(out_theirs, to_heads)
        )
        lse_full = (
            jnp.concatenate([l_first_0, l_first_1], axis=0),
            jnp.concatenate([l_second_0, l_second_1], axis=0),
        )
        attended = (first_0, first_1, second_0, second_1, out_own, out_other)
        branch_one, hidden_two, grad_two, hidden_two_turned, grad_two_turned, grad_b_down, got = after(
            *middle_part(
                side, tokens, cotangent, attended, attention_weights, b_out[None], hot, parts, third // 2
            ),
            send(flat, to_core),
        )
        flat = jnp.concatenate([flat, got], axis=0)
        silu_all = jax.nn.silu(flat.reshape(ring * images, width).astype(F32))

        def added(mine, got):
            return mine + got.astype(F32)

        def level_pieces(values):
            part = lambda k: values[..., k * piece : (k + 1) * piece, :]
            return part(0), *(part(k).astype(BF) for k in range(1, levels))

        def all_added(kept, got):
            for part in got:
                kept = added(kept, part)
            return kept

        quarter = width // 4

        def plane_pieces(mine_own, got_own, mine_other, got_other):
            near = lambda mine, got: added(mine[:quarter], got[:quarter])
            far = lambda mine, got: added(mine[quarter:], got[quarter:]).astype(BF)
            return (
                near(mine_own, got_own),
                far(mine_own, got_own),
                near(mine_other, got_other).astype(BF),
                far(mine_other, got_other),
            )

        flat_turned = lambda values: values.reshape(width, rows)
        hidden_one_turned = flat_turned(hidden_one_turned)
        feed_args = (flat_turned(hidden_two_turned), flat_turned(grad_two_turned), feed_weights, up_bias, rows // 2, 768)
        two_b, back_b, mine_b, near_b, far_b, grad_b_up_b = feed(
            1 - y.reshape(1), hidden_two, grad_two, *feed_args
        )
        far_b = added(mine_b[:, quarter:], send(far_b, to_core)).astype(BF)
        hidden_two, far_b, near_b = after(hidden_two, far_b, near_b)
        two_a, back_a, mine_a, near_a, far_a, grad_b_up_a, near_b, far_b = after(
            *feed(y.reshape(1), hidden_two, grad_two, *feed_args),
            send(near_b, to_core),
            send(far_b, to_x),
        )
        over_b = added(added(mine_b[:, :quarter], near_b), far_b).astype(BF)
        far_a = added(mine_a[:, quarter:], send(far_a, to_core)).astype(BF)
        two_a, over_b, far_a, near_a = after(two_a, over_b, far_a, near_a)

        output, grad_middle, *grad_attended, sums_two, grad_b_out, out_mine, out_theirs_sum, over_b, far_a, near_a = after(
            *back_two(
                side, tokens, cotangent, branch_one, two_a, two_b, b_down[None], back_a, back_b, attention_weights,
                hot, turn, parts, attended, third // 2, images, out_width,
            ),
            send(over_b, to_heads),
            send(far_a, to_x),
            send(near_a, to_core),
        )
        grad_first, grad_second, grad_own, grad_theirs = grad_attended
        grad_other = send(grad_theirs, to_heads)
        out_got = send(out_theirs_sum, to_core)
        out_pieces = plane_pieces(out_mine[0], out_got[0], out_mine[1], out_got[1])
        feed_kept, *feed_sent = level_pieces(
            added(added(added(mine_a[:, :quarter], near_a), far_a), over_b)
        )
        grad_own, feed_kept, *joined = after(grad_own, feed_kept, *feed_sent, *out_pieces)
        feed_sent, out_pieces = joined[: levels - 1], joined[levels - 1 :]
        grad_qkv_own, grad_qkv_theirs, *got = after(
            *attend_back(*qkv_half, grad_own, grad_other, *lse_half, *marks_half),
            send(out_pieces[1], to_x),
            send(out_pieces[2], to_heads),
            send(out_pieces[3], to_corner),
        )
        out_kept, *out_sent = level_pieces(all_added(out_pieces[0], got))
        grad_first, grad_qkv_theirs, feed_kept, out_kept, *joined = after(
            grad_first, grad_qkv_theirs, feed_kept, out_kept, *feed_sent, *out_sent
        )
        feed_sent, out_sent = joined[: levels - 1], joined[levels - 1 :]
        grad_qkv_first, grad_qkv_second, grad_qkv_other, *got = after(
            *attend_back(*qkv_full, grad_first, grad_second, *lse_full, *marks_full),
            send(grad_qkv_theirs, to_heads),
            *(send(part, to_level[k + 1]) for k, part in enumerate(feed_sent)),
        )
        grad_w_up, grad_w_down = all_added(feed_kept, got)
        qkv_mine_b, qkv_theirs_b, grad_qkv_bias_b, *got = after(
            *outer(hidden_one_turned, grad_qkv_first, grad_qkv_second, grad_qkv_other, 1),
            *(send(part, to_level[k + 1]) for k, part in enumerate(out_sent)),
        )
        grad_w_out = all_added(out_kept, got)
        hidden_one_turned, qkv_theirs_b = after(hidden_one_turned, qkv_theirs_b)
        qkv_mine_a, qkv_theirs_a, grad_qkv_bias_a, qkv_got_b = after(
            *outer(hidden_one_turned, grad_qkv_first, grad_qkv_second, grad_qkv_own, 0),
            send(qkv_theirs_b, to_core),
        )
        near, *sent = plane_pieces(qkv_mine_a, send(qkv_theirs_a, to_core), qkv_mine_b, qkv_got_b)
        grad_middle, near, *sent = after(grad_middle, near, *sent)
        grad_qkv = (grad_qkv_first, grad_qkv_second, grad_qkv_own, grad_qkv_other)
        grad_tokens, sums_one, *got = after(
            *back_one(
                side, grad_qkv, attention_weights, tokens, grad_middle, hot, turn, parts, third // 2, images
            ),
            send(sent[0], to_x),
            send(sent[1], to_heads),
            send(sent[2], to_corner),
        )
        qkv_kept, *qkv_sent = level_pieces(all_added(near, got))

        sums = jnp.concatenate([sums_one, sums_two], axis=0).reshape(2, 3, images, width)
        sums = sums.transpose(0, 2, 1, 3).reshape(2, images, 3 * width)
        narrow = jnp.concatenate([grad_b_out, grad_b_down], axis=0).reshape(2, 2, cols)

        def packet(which, up_sum, qkv_sum):
            second = lax.dynamic_index_in_dim(narrow, which, 1, keepdims=False).reshape(-1)
            short = [up_sum[0], qkv_sum[:cols], qkv_sum[2 * cols : 3 * cols], second]
            short = jnp.concatenate(short).reshape(images, -1)
            chunk = lax.dynamic_index_in_dim(sums, which, 0, keepdims=False)
            gap = -(chunk.shape[1] + short.shape[1]) % 128
            return jnp.concatenate([chunk, short, jnp.zeros((images, gap), F32)], axis=1)

        own_packet = packet(y, grad_b_up_a, grad_qkv_bias_a[0]) + send(
            packet(1 - y, grad_b_up_b, grad_qkv_bias_b[0]), to_heads
        )
        own_packet, qkv_kept, *qkv_sent = after(own_packet, qkv_kept, *qkv_sent)
        grad_silu = lax.dot_general(
            own_packet[:, : 3 * width],
            w_ada,
            (((1,), (1,)), ((), ())),
            precision=PRECISE,
            preferred_element_type=F32,
        )
        grad_silu, *got = after(
            grad_silu, *(send(own_packet, to_level[k]) for k in range(1, levels))
        )
        flat = jnp.concatenate([own_packet, *got], axis=0)
        flat, *qkv_sent = after(flat, *qkv_sent)
        silu_got, flat_got, *got = after(
            send(grad_silu, to_heads),
            send(flat, to_x),
            *(send(part, to_level[k + 1]) for k, part in enumerate(qkv_sent)),
        )
        grad_w_qkv = all_added(qkv_kept, got)
        flat = jnp.concatenate([flat, flat_got], axis=0)
        packets = jnp.concatenate([flat, send(flat, to_core)], axis=0)
        grad_mod = packets[:, : 3 * width]
        count = units + 4 * cols
        short = packets[:, 3 * width : 3 * width + count // images]
        bias_sums = jnp.sum(short.reshape(ring, images, count // images), axis=0).reshape(-1)
        s1, s2, _ = jnp.split(three_parts(silu_all), 3, axis=0)
        g1, g2, _ = jnp.split(three_parts(grad_mod), 3, axis=0)
        grad_w_ada = contract_first(
            jnp.concatenate([s1, s1, s2], axis=0), jnp.concatenate([g1, g2, g1], axis=0)
        )
        grad_b_ada = jnp.sum(grad_mod, axis=0)
        grad_silu = grad_silu + silu_got
        _, silu_back = jax.vjp(jax.nn.silu, cond)
        grad_condition = silu_back(grad_silu)[0]
        return (
            output,
            grad_tokens,
            grad_condition,
            grad_w_ada,
            grad_b_ada,
            grad_w_qkv[:, :cols],
            grad_w_qkv[:, cols : 2 * cols],
            grad_w_qkv[:, 2 * cols : 3 * cols],
            bias_sums[units : units + cols],
            bias_sums[units + cols : units + 2 * cols],
            grad_w_out[:, :cols],
            bias_sums[units + 2 * cols : units + 3 * cols],
            grad_w_up,
            bias_sums[:units],
            grad_w_down,
            bias_sums[units + 3 * cols :],
        )

    return body


def solution(mesh):
    body = fast_body(mesh) if mesh.shape["heads"] == 2 and mesh.shape["rows"] == 16 else general_body
    placed = (
        P(("rows", "heads"), None),
        P("rows", None),
        P("rows", None),
        P("rows", None, None),
        P("rows", None),
        P(None, "heads"),
        P("heads"),
        P("rows", "heads"),
        P("rows", "heads"),
        P("rows", "heads"),
        P("heads"),
        P("heads"),
        P("rows", "heads"),
        P(),
        P("rows", "heads"),
        P("heads"),
        P("rows", "heads"),
        P(),
        P(("rows", "heads"), None),
    )
    return jax.shard_map(
        body,
        mesh=mesh,
        in_specs=placed,
        out_specs=(
            P(("rows", "heads"), None),
            P(("rows", "heads"), None),
            P("rows", None),
            P(None, "heads"),
            P("heads"),
            P("rows", "heads"),
            P("rows", "heads"),
            P("rows", "heads"),
            P("heads"),
            P("heads"),
            P("rows", "heads"),
            P("heads"),
            P("rows", "heads"),
            P("heads"),
            P("rows", "heads"),
            P("heads"),
        ),
        check_vma=False,
    )
```

```python
from functools import partial

import jax
import jax.numpy as jnp
from jax import lax
from jax.experimental import pallas as pl
from jax.experimental.pallas import tpu as pltpu
from jax.sharding import PartitionSpec as P

HEAD_DIM = 72
TILE = 128


EPSILON = 1e-06
MASKED_SCORE = -1e30
PRECISE = lax.Precision.HIGHEST


def layer_norm(values):
    centred = values - jnp.mean(values, axis=-1, keepdims=True)
    inverse = lax.rsqrt(jnp.mean(centred * centred, axis=-1, keepdims=True) + EPSILON)
    return (centred * inverse, inverse)


def norm_back(normed, inverse, grad):
    return inverse * (
        grad
        - jnp.mean(grad, axis=-1, keepdims=True)
        - normed * jnp.mean(grad * normed, axis=-1, keepdims=True)
    )


def contract_last(left, right):
    return lax.dot_general(
        left, right, (((1,), (1,)), ((), ())), preferred_element_type=jnp.float32
    )


def contract_first(left, right):
    return lax.dot_general(
        left, right, (((0,), (0,)), ((), ())), preferred_element_type=jnp.float32
    )


def general_body(
    tokens,
    condition,
    segment_ids,
    tile_mask,
    image_index,
    w_ada,
    b_ada,
    w_query,
    w_key,
    w_value,
    b_query,
    b_value,
    w_out,
    b_out,
    w_up,
    b_up,
    w_down,
    b_down,
    cotangent,
):
    scaling = HEAD_DIM ** (-0.5)
    own_rows = tokens.shape[0]
    seq_count = segment_ids.shape[0]
    length = segment_ids.shape[1]
    group_rows = seq_count * length
    own_start = lax.axis_index("heads") * own_rows
    img_count = condition.shape[0]
    slot_count = image_index.shape[1]
    local_heads = w_query.shape[1] // HEAD_DIM
    block_rows = min(512, length)
    tile_count = length // TILE
    bfloat = jnp.bfloat16
    own_segments = lax.dynamic_slice_in_dim(segment_ids.reshape(group_rows), own_start, own_rows)
    own_seqs = (own_start + jnp.arange(own_rows, dtype=jnp.int32)) // length
    seq_match = own_seqs[:, None] == jnp.arange(seq_count, dtype=jnp.int32)[None, :]
    slot_match = own_segments[:, None] == jnp.arange(slot_count, dtype=jnp.int32)[None, :]
    own_image = jnp.sum(
        jnp.where(seq_match[:, :, None] & slot_match[:, None, :], image_index[None, :, :], 0),
        axis=(1, 2),
    )
    image_onehot = (own_image[:, None] == jnp.arange(img_count, dtype=jnp.int32)[None, :]).astype(
        jnp.float32
    )
    cond_full = condition.astype(jnp.float32)
    silu_cond = jax.nn.silu(cond_full)
    mod_cols = jnp.dot(silu_cond, w_ada, precision=PRECISE) + b_ada
    mod_full, up_bias_all = (
        lax.all_gather(mod_cols, "heads", axis=1, tiled=True),
        lax.all_gather(b_up.reshape(1, -1), "heads", axis=1, tiled=True),
    )
    per_token = jnp.dot(image_onehot, mod_full, precision=PRECISE)
    shift_one, scale_one, gate_one, shift_two, scale_two, gate_two = jnp.split(per_token, 6, axis=1)

    def gather_weights():
        return (
            lax.all_gather(w_query.astype(bfloat), "rows", axis=0, tiled=True),
            lax.all_gather(w_key.astype(bfloat), "rows", axis=0, tiled=True),
            lax.all_gather(w_value.astype(bfloat), "rows", axis=0, tiled=True),
            lax.all_gather(w_out.astype(bfloat), "rows", axis=0, tiled=True),
            lax.all_gather(w_up.astype(bfloat), "rows", axis=0, tiled=True),
            lax.all_gather(w_down.astype(bfloat), "rows", axis=0, tiled=True),
        )

    def spread_first(values):
        return lax.all_gather(values, "heads", axis=0, tiled=True)

    query_full, key_full, value_full, out_full, up_full, down_full = gather_weights()
    token_full = tokens.astype(jnp.float32)
    normed_one, inverse_one = layer_norm(token_full)
    hidden_own_one = (normed_one * (1.0 + scale_one) + shift_one).astype(bfloat)
    hidden_one = spread_first(hidden_own_one)
    head_shape = (group_rows, local_heads, HEAD_DIM)
    query_heads = (
        (jnp.dot(hidden_one, query_full, preferred_element_type=jnp.float32) + b_query)
        .astype(bfloat)
        .reshape(head_shape)
    )
    key_heads = (
        jnp.dot(hidden_one, key_full, preferred_element_type=jnp.float32)
        .astype(bfloat)
        .reshape(head_shape)
    )
    value_heads = (
        (jnp.dot(hidden_one, value_full, preferred_element_type=jnp.float32) + b_value)
        .astype(bfloat)
        .reshape(head_shape)
    )
    tile_of = jnp.arange(length, dtype=jnp.int32) // TILE

    def scores_for(seq_index, block_start):
        seq_start = seq_index * length
        block_query = query_heads[seq_start + block_start : seq_start + block_start + block_rows]
        seq_keys = key_heads[seq_start : seq_start + length]
        block_tiles = tile_mask[seq_index][block_start // TILE : (block_start + block_rows) // TILE]
        expanded = jnp.broadcast_to(
            block_tiles[:, None, :, None], (block_rows // TILE, TILE, tile_count, TILE)
        ).reshape(block_rows, length)
        seg_row = segment_ids[seq_index]
        same_image = seg_row[block_start : block_start + block_rows][:, None] == seg_row[None, :]
        diagonal = tile_of[block_start : block_start + block_rows][:, None] == tile_of[None, :]
        allowed = same_image & ((expanded > 0) | diagonal)
        raw = (
            jnp.einsum("qhd,khd->hqk", block_query, seq_keys, preferred_element_type=jnp.float32)
            * scaling
        )
        return (jnp.where(allowed[None], raw, MASKED_SCORE), block_query, seq_keys)

    attended_parts = []
    log_totals = []
    for seq_index in range(seq_count):
        seq_values = value_heads[seq_index * length : (seq_index + 1) * length]
        for block_start in range(0, length, block_rows):
            scores, block_query, seq_keys = scores_for(seq_index, block_start)
            top_score = jnp.max(scores, axis=-1, keepdims=True)
            log_total = top_score + jnp.log(
                jnp.sum(jnp.exp(scores - top_score), axis=-1, keepdims=True)
            )
            probs_low = jnp.exp(scores - log_total).astype(bfloat)
            attended_parts.append(
                jnp.einsum(
                    "hqk,khd->qhd", probs_low, seq_values, preferred_element_type=jnp.float32
                )
            )
            log_totals.append(log_total)
    attended = (
        jnp.concatenate(attended_parts, axis=0)
        .reshape(group_rows, local_heads * HEAD_DIM)
        .astype(bfloat)
    )
    branch_one = (
        lax.psum_scatter(
            contract_last(attended, out_full), "heads", scatter_dimension=0, tiled=True
        )
        + b_out
    )
    middle = token_full + gate_one * branch_one
    normed_two, inverse_two = layer_norm(middle)
    hidden_own_two = (normed_two * (1.0 + scale_two) + shift_two).astype(bfloat)
    up_all, down_all = (
        lax.all_gather(up_full, "heads", axis=1, tiled=True),
        lax.all_gather(down_full, "heads", axis=1, tiled=True),
    )
    pre_act = jnp.dot(hidden_own_two, up_all, preferred_element_type=jnp.float32) + up_bias_all[0]
    activated = jax.nn.gelu(pre_act, approximate=True).astype(bfloat)
    branch_two = contract_last(activated, down_all) + b_down
    output = (middle + gate_two * branch_two).astype(bfloat)
    query_back, key_back, value_back, out_back, up_back, down_back = gather_weights()
    hidden_one_back = spread_first(hidden_own_one)
    grad_out = cotangent.astype(jnp.float32)
    grad_branch_two = (grad_out * gate_two).astype(bfloat)
    grad_gate_two = grad_out * branch_two
    grad_down_all = contract_first(grad_branch_two, activated)
    grad_act = jnp.dot(grad_branch_two, down_all, preferred_element_type=jnp.float32)
    _, gelu_back = jax.vjp(partial(jax.nn.gelu, approximate=True), pre_act)
    grad_pre = gelu_back(grad_act)[0].astype(bfloat)
    grad_up_all = contract_first(hidden_own_two, grad_pre)
    grad_bias_all = jnp.sum(grad_pre, axis=0, dtype=jnp.float32).reshape(1, -1)
    grad_hidden_two = contract_last(grad_pre, up_all)
    grad_w_up, grad_w_down, grad_bias_cols = (
        lax.psum_scatter(grad_up_all, "heads", scatter_dimension=1, tiled=True),
        lax.psum_scatter(grad_down_all, "heads", scatter_dimension=1, tiled=True),
        lax.psum_scatter(grad_bias_all, "heads", scatter_dimension=1, tiled=True),
    )
    grad_b_up = grad_bias_cols[0]
    grad_scale_two = grad_hidden_two * normed_two
    grad_middle = grad_out + norm_back(normed_two, inverse_two, grad_hidden_two * (1.0 + scale_two))
    grad_branch_one = (grad_middle * gate_one).astype(bfloat)
    grad_gate_one = grad_middle * branch_one
    grad_one_full = lax.all_gather(grad_branch_one, "heads", axis=0, tiled=True)
    grad_w_out = contract_first(grad_one_full, attended)
    grad_attended = (
        jnp.dot(grad_one_full, out_back, preferred_element_type=jnp.float32)
        .astype(bfloat)
        .reshape(head_shape)
    )
    grad_query_parts = []
    grad_key_parts = []
    grad_value_parts = []
    block_number = 0
    for seq_index in range(seq_count):
        seq_start = seq_index * length
        seq_values = value_heads[seq_start : seq_start + length]
        key_total = jnp.zeros((length, local_heads, HEAD_DIM), jnp.float32)
        value_total = jnp.zeros((length, local_heads, HEAD_DIM), jnp.float32)
        for block_start in range(0, length, block_rows):
            scores, block_query, seq_keys = scores_for(seq_index, block_start)
            probs = jnp.exp(scores - log_totals[block_number])
            block_number += 1
            grad_block = grad_attended[
                seq_start + block_start : seq_start + block_start + block_rows
            ]
            grad_probs = jnp.einsum(
                "qhd,khd->hqk", grad_block, seq_values, preferred_element_type=jnp.float32
            )
            centre = jnp.sum(probs * grad_probs, axis=-1, keepdims=True)
            grad_scores = (probs * (grad_probs - centre)).astype(bfloat)
            grad_query_parts.append(
                (
                    jnp.einsum(
                        "hqk,khd->qhd", grad_scores, seq_keys, preferred_element_type=jnp.float32
                    )
                    * scaling
                ).astype(bfloat)
            )
            key_total = (
                key_total
                + jnp.einsum(
                    "hqk,qhd->khd", grad_scores, block_query, preferred_element_type=jnp.float32
                )
                * scaling
            )
            value_total = value_total + jnp.einsum(
                "hqk,qhd->khd", probs.astype(bfloat), grad_block, preferred_element_type=jnp.float32
            )
        grad_key_parts.append(key_total.astype(bfloat))
        grad_value_parts.append(value_total.astype(bfloat))
    flat_shape = (group_rows, local_heads * HEAD_DIM)
    grad_queries = jnp.concatenate(grad_query_parts, axis=0).reshape(flat_shape)
    grad_keys = jnp.concatenate(grad_key_parts, axis=0).reshape(flat_shape)
    grad_values = jnp.concatenate(grad_value_parts, axis=0).reshape(flat_shape)
    grad_w_query = contract_first(hidden_one_back, grad_queries)
    grad_w_key = contract_first(hidden_one_back, grad_keys)
    grad_w_value = contract_first(hidden_one_back, grad_values)
    grad_b_query = jnp.sum(grad_queries, axis=0, dtype=jnp.float32)
    grad_b_value = jnp.sum(grad_values, axis=0, dtype=jnp.float32)
    total = contract_last(grad_queries, query_back)
    total = total + contract_last(grad_keys, key_back)
    grad_hidden_one = lax.psum_scatter(
        total + contract_last(grad_values, value_back), "heads", scatter_dimension=0, tiled=True
    )
    grad_scale_one = grad_hidden_one * normed_one
    grad_tokens = grad_middle + norm_back(
        normed_one, inverse_one, grad_hidden_one * (1.0 + scale_one)
    )
    grad_mod_tokens = jnp.concatenate(
        [
            grad_hidden_one,
            grad_scale_one,
            grad_gate_one,
            grad_hidden_two,
            grad_scale_two,
            grad_gate_two,
        ],
        axis=1,
    )
    grad_mod_images = lax.dot_general(
        image_onehot,
        grad_mod_tokens,
        (((0,), (0,)), ((), ())),
        precision=PRECISE,
        preferred_element_type=jnp.float32,
    )
    bias_parts = jnp.stack(
        [
            jnp.sum(grad_branch_one, axis=0, dtype=jnp.float32),
            jnp.sum(grad_branch_two, axis=0, dtype=jnp.float32),
        ],
        axis=0,
    )
    grad_mod_cols, bias_cols = (
        lax.psum_scatter(grad_mod_images, "heads", scatter_dimension=1, tiled=True),
        lax.psum_scatter(bias_parts, "heads", scatter_dimension=1, tiled=True),
    )
    grad_w_ada = lax.dot_general(
        silu_cond,
        grad_mod_cols,
        (((0,), (0,)), ((), ())),
        precision=PRECISE,
        preferred_element_type=jnp.float32,
    )
    grad_b_ada = jnp.sum(grad_mod_cols, axis=0)
    grad_silu = lax.dot_general(
        grad_mod_cols,
        w_ada,
        (((1,), (1,)), ((), ())),
        precision=PRECISE,
        preferred_element_type=jnp.float32,
    )
    grad_silu = lax.psum(grad_silu, "heads")
    _, silu_back = jax.vjp(jax.nn.silu, cond_full)
    grad_condition = silu_back(grad_silu)[0]
    grad_w_ada, grad_b_ada, grad_b_query, grad_b_value, grad_b_up, bias_cols = lax.psum(
        (grad_w_ada, grad_b_ada, grad_b_query, grad_b_value, grad_b_up, bias_cols), "rows"
    )
    grad_w_query, grad_w_key, grad_w_value, grad_w_out, grad_w_up, grad_w_down = (
        lax.psum_scatter(grad_w_query, "rows", scatter_dimension=0, tiled=True),
        lax.psum_scatter(grad_w_key, "rows", scatter_dimension=0, tiled=True),
        lax.psum_scatter(grad_w_value, "rows", scatter_dimension=0, tiled=True),
        lax.psum_scatter(grad_w_out, "rows", scatter_dimension=0, tiled=True),
        lax.psum_scatter(grad_w_up, "rows", scatter_dimension=0, tiled=True),
        lax.psum_scatter(grad_w_down, "rows", scatter_dimension=0, tiled=True),
    )
    return (
        output,
        grad_tokens,
        grad_condition,
        grad_w_ada,
        grad_b_ada,
        grad_w_query,
        grad_w_key,
        grad_w_value,
        grad_b_query,
        grad_b_value,
        grad_w_out,
        bias_cols[0],
        grad_w_up,
        grad_b_up,
        grad_w_down,
        bias_cols[1],
    )


LOG2E = 1.4426950408889634
GELU_SLOPE = 0.7978845608028654
GELU_CUBE = 0.044715
BF = jnp.bfloat16
F32 = jnp.float32
MIB = 2**20


def rows_by_columns(left, right):
    return jnp.dot(left, right, preferred_element_type=F32)


def shape(dims, dtype):
    return jax.ShapeDtypeStruct(dims, dtype)


def params(mib=56):
    return pltpu.CompilerParams(vmem_limit_bytes=mib * MIB)


def cost(flops, bytes_accessed, transcendentals=0):
    return pl.CostEstimate(
        flops=int(flops), bytes_accessed=int(bytes_accessed), transcendentals=int(transcendentals)
    )


def three_parts(values):
    high = lax.reduce_precision(values, 8, 7)
    rest = values - high
    middle = lax.reduce_precision(rest, 8, 7)
    return jnp.concatenate([high, middle, rest - middle], axis=-2).astype(BF)


def collect_kernel(here, *refs):
    sources, whole, sems = refs[:10], refs[10], refs[11]
    levels, xs = whole.shape[2:4]
    count = sources[0].shape[-1]
    y, level, x, core = (here[k] for k in range(4))
    flip = lambda bit, other: bit + other - 2 * bit * other
    copies = []
    for dc in range(2):
        x_near, x_far, y_near, y_far, last = sources[5 * dc : 5 * dc + 5]
        for dz in range(levels):
            for i in range(2):
                for j in range(2):
                    at = (flip(y, i), lax.rem(level + dz, levels), flip(x, j), flip(core, dc))
                    found = (
                        (x_near, x_far)[i].at[j, dz],
                        (y_near, y_far)[j].at[i, dz],
                        last.at[dz, i, j],
                    )
                    for k, source in enumerate(found):
                        place = whole.at[(slice(None), *at, slice(None), pl.ds(k * count, count))]
                        copies.append(pltpu.make_async_copy(source, place, sems.at[len(copies)]))
                        copies[-1].start()
    for copy in copies:
        copy.wait()


def collected(here, sources):
    levels, heads, xs, parts, piece, count = sources[4].shape
    whole = (parts, heads, levels, xs, 2, piece, 3 * count)
    anywhere = pl.BlockSpec(memory_space=pl.ANY)
    return pl.pallas_call(
        collect_kernel,
        grid_spec=pltpu.PrefetchScalarGridSpec(
            num_scalar_prefetch=1,
            grid=(1,),
            in_specs=[anywhere] * 10,
            out_specs=anywhere,
            scratch_shapes=[pltpu.SemaphoreType.DMA((6 * heads * levels * xs,))],
        ),
        out_shape=shape(whole, BF),
        compiler_params=params(16),
        cost_estimate=cost(0, 24 * parts * heads * levels * xs * piece * count),
    )(here, *sources)


def turn_in_order(places, turned_ref, values):
    turned = values.astype(F32).T
    piece = turned_ref.shape[1]
    for k in range(turned_ref.shape[0]):
        turned_ref[places[1 + k]] = turned[k * piece : (k + 1) * piece].astype(BF)


def norm_kernel(side, tok_ref, hot_ref, parts_ref, h_ref, half_ref, ht_ref):
    width = tok_ref.shape[1]
    normed, _ = layer_norm(tok_ref[...].astype(F32))
    mod = rows_by_columns(hot_ref[...], parts_ref[0, :, : 2 * width])
    hidden = (normed * (1.0 + mod[:, width:]) + mod[:, :width]).astype(BF)
    turn_in_order(side, ht_ref, hidden)

    @pl.when(pl.program_id(0) < 2)
    def _():
        h_ref[...] = hidden

    @pl.when(pl.program_id(0) == 2)
    def _():
        half_ref[...] = hidden


def first_norm(side, tokens, hot, parts, block):
    ring = side.shape[0] // 2
    rows, width = tokens.shape
    return pl.pallas_call(
        norm_kernel,
        grid_spec=pltpu.PrefetchScalarGridSpec(
            num_scalar_prefetch=1,
            grid=(rows // block,),
            in_specs=[
                pl.BlockSpec((block, width), lambda i, y: ((i + y[0]) % 3, 0)),
                pl.BlockSpec((block, hot.shape[1]), lambda i, y: (i, 0)),
                pl.BlockSpec((1,) + parts.shape[1:], lambda i, y: (0, 0, 0)),
            ],
            out_specs=[
                pl.BlockSpec((block, width), lambda i, y: (jnp.minimum(i, 1), 0)),
                pl.BlockSpec((block, width), lambda i, y: (0, 0)),
                pl.BlockSpec((ring, width // ring, block), lambda i, y: (0, 0, i)),
            ],
        ),
        out_shape=[
            shape((2 * block, width), BF),
            shape((block, width), BF),
            shape((ring, width // ring, rows), BF),
        ],
        compiler_params=params(),
        cost_estimate=cost(2 * rows * width * (width + 512), rows * width * 6),
    )(side, tokens, hot, parts)


def project_kernel(side, first_in, second_in, w_ref, bias_ref, first, second):
    padded = first.shape[2]
    cols = bias_ref.shape[2]
    for hidden, ref in ((first_in, first), (second_in, second)):
        value = (rows_by_columns(hidden[...], w_ref[0, :, :cols]) + bias_ref[0]).astype(BF)
        ref[0] = jnp.concatenate([value, jnp.zeros((value.shape[0], padded - cols), BF)], axis=1)


def project(side, first, second, weights, bias, padded, block, groups):
    width = first.shape[1]
    pick = lambda a, y: a + y[0] - 2 * a * y[0]
    last = second.shape[0] // block - 1
    pair = pl.BlockSpec((1, block, padded), lambda a, y: (a, 0, 0))
    return pl.pallas_call(
        project_kernel,
        grid_spec=pltpu.PrefetchScalarGridSpec(
            num_scalar_prefetch=1,
            grid=(groups,),
            in_specs=[
                pl.BlockSpec((block, width), lambda a, y: (0, 0)),
                pl.BlockSpec((block, width), lambda a, y: (last, 0)),
                pl.BlockSpec((1,) + weights.shape[1:], lambda a, y: (pick(a, y), 0, 0)),
                pl.BlockSpec((1,) + bias.shape[1:], lambda a, y: (pick(a, y), 0, 0)),
            ],
            out_specs=[pair, pair],
        ),
        out_shape=[shape((groups, block, padded), BF)] * 2,
        compiler_params=params(60),
        cost_estimate=cost(
            4 * groups * block * width * padded, 4 * groups * (block + width) * padded
        ),
    )(side, first, second, weights, bias)


MARKS = 16
DEPTH = 128
LSE_AT = HEAD_DIM + MARKS - 4
STEEP = HEAD_DIM**-0.5 * LOG2E


def marks_kernel(*refs):
    count = len(refs) // 4
    for n in range(count):
        seg_ref, open_ref = refs[2 * n : 2 * n + 2]
        query_ref, key_ref = refs[2 * count + 2 * n : 2 * count + 2 * n + 2]
        tiles, length = open_ref.shape
        slots = MARKS - 4 - tiles
        slot = lax.broadcasted_iota(jnp.int32, (slots, length), 0)
        own_slot = slot == seg_ref[...]
        tile = lax.broadcasted_iota(jnp.int32, (tiles, length), 0)
        own_tile = tile == lax.broadcasted_iota(jnp.int32, (tiles, length), 1) // TILE
        seen = jnp.concatenate(
            [jnp.where(own_slot, 0.0, MASKED_SCORE), jnp.where(open_ref[...] > 0, 0.0, MASKED_SCORE)],
            axis=0,
        )
        chosen = jnp.concatenate(
            [jnp.where(own_slot, 1.0, 0.0), jnp.where(own_tile, 1.0, 0.0)], axis=0
        )
        rest = (MARKS - slots - tiles, length)
        query_ref[...] = jnp.concatenate([chosen, jnp.zeros(rest, F32)], axis=0).T.astype(BF)
        key_ref[...] = jnp.concatenate([seen, jnp.ones(rest, F32)], axis=0).T.astype(BF)


def marks_of(*rows):
    length = rows[1].shape[1]
    return pl.pallas_call(
        marks_kernel,
        out_shape=[shape((length, MARKS), BF)] * len(rows),
        compiler_params=params(16),
    )(*rows)


def split_three(values):
    high = values.astype(BF)
    rest = values - high.astype(F32)
    middle = rest.astype(BF)
    return jnp.concatenate([high, middle, (rest - middle.astype(F32)).astype(BF)], axis=1)


def at_head(h, part, heads):
    start = (part * heads + h) * HEAD_DIM
    return slice(start, start + HEAD_DIM)


def both_halves(first, second, columns):
    return jnp.concatenate([first[0, :, columns], second[0, :, columns]], axis=0)


def padded_columns(parts, width):
    found = jnp.concatenate(parts, axis=1)
    gap = width - found.shape[1]
    return jnp.concatenate([found, jnp.zeros((found.shape[0], gap), found.dtype)], axis=1)


def attend_kernel(
    heads, first, second, qm_ref, km_ref, o_first, o_second, l_first, l_second, keys, values, queries
):
    i = pl.program_id(1)

    @pl.when((i == 0) & (pl.program_id(0) == 0))
    def _():
        keys[...] = jnp.zeros_like(keys)
        queries[...] = jnp.zeros_like(queries)

    @pl.when(i == 0)
    def _():
        for h in range(heads):
            keys[h, :, :HEAD_DIM] = both_halves(first, second, at_head(h, 1, heads))
            keys[h, :, HEAD_DIM : HEAD_DIM + MARKS] = km_ref[...]
            value = both_halves(first, second, at_head(h, 2, heads))
            values[h] = value.astype(F32).T.astype(BF)

    for h in range(heads):
        columns = at_head(h, 0, heads)
        queries[h, :, :HEAD_DIM] = jnp.where(i == 0, first[0, :, columns], second[0, :, columns])
        queries[h, :, HEAD_DIM : HEAD_DIM + MARKS] = qm_ref[...]
    parts = []
    totals = []
    probs = None
    scores = contract_last(keys[0], queries[0])
    for h in range(heads):
        later = contract_last(keys[h + 1], queries[h + 1]) if h + 1 < heads else None
        top = jnp.max(scores, axis=0, keepdims=True)
        powers = jnp.exp2((scores - top) * STEEP)
        total = jnp.sum(powers, axis=0, keepdims=True)
        totals.append(top + jnp.log2(total) * (1.0 / STEEP))
        if h > 0:
            parts.append(rows_by_columns(values[h - 1], probs).T.astype(BF))
        probs = (powers * (1.0 / total)).astype(BF)
        scores = later
    parts.append(rows_by_columns(values[heads - 1], probs).T.astype(BF))
    out = padded_columns(parts, o_first.shape[2])
    log_totals = jnp.concatenate(totals, axis=0)

    @pl.when(i == 0)
    def _():
        o_first[0] = out
        l_first[0] = log_totals

    @pl.when(i == 1)
    def _():
        o_second[0] = out
        l_second[0] = log_totals


def attend(first, second, query_marks, key_marks, out_width):
    groups, half, padded = first.shape
    heads = out_width // HEAD_DIM
    pair = lambda *dims: pl.BlockSpec((1,) + dims, lambda a, i: (a, 0, 0))
    return pl.pallas_call(
        partial(attend_kernel, heads),
        grid=(groups, 2),
        in_specs=[
            pair(half, padded),
            pair(half, padded),
            pl.BlockSpec((half, MARKS), lambda a, i: (i, 0)),
            pl.BlockSpec((2 * half, MARKS), lambda a, i: (0, 0)),
        ],
        out_specs=[pair(half, out_width)] * 2 + [pair(heads, half)] * 2,
        out_shape=[shape((groups, half, out_width), BF)] * 2 + [shape((groups, heads, half), F32)] * 2,
        scratch_shapes=[
            pltpu.VMEM((heads, 2 * half, DEPTH), BF),
            pltpu.VMEM((heads, HEAD_DIM, 2 * half), BF),
            pltpu.VMEM((heads, half, DEPTH), BF),
        ],
        compiler_params=params(),
        cost_estimate=cost(groups * 15e9, groups * half * padded * 6, groups * heads * half * half),
    )(first, second, query_marks, key_marks)


def attend_back_kernel(
    heads, first, second, do_first, do_second, l_first, l_second, qm_ref, km_ref,
    out_first, out_second, keys, values, turned, queries, dk, dv,
):
    i = pl.program_id(1)
    half, padded = first.shape[1:]
    width = heads * HEAD_DIM
    scaling = HEAD_DIM**-0.5

    @pl.when((i == 0) & (pl.program_id(0) == 0))
    def _():
        keys[...] = jnp.zeros_like(keys)
        queries[...] = jnp.zeros_like(queries)

    @pl.when(i == 0)
    def _():
        for h in range(heads):
            key = both_halves(first, second, at_head(h, 1, heads))
            keys[h, :, :HEAD_DIM] = key
            keys[h, :, HEAD_DIM : HEAD_DIM + MARKS] = km_ref[...]
            turned[h] = key.astype(F32).T.astype(BF)
            values[h] = both_halves(first, second, at_head(h, 2, heads))
        dk[...] = jnp.zeros_like(dk)
        dv[...] = jnp.zeros_like(dv)

    log_totals = jnp.where(i == 0, l_first[0], l_second[0]).T
    plain = []
    for h in range(heads):
        columns = at_head(h, 0, heads)
        query = jnp.where(i == 0, first[0, :, columns], second[0, :, columns])
        grad = jnp.where(i == 0, do_first[0, :, columns], do_second[0, :, columns])
        queries[h, :, :HEAD_DIM] = query
        queries[h, :, HEAD_DIM : HEAD_DIM + MARKS] = qm_ref[...]
        queries[h, :, LSE_AT : LSE_AT + 3] = split_three(-log_totals[:, h : h + 1])
        plain.append((query, grad))

    def scores_of(h):
        return contract_last(keys[h], queries[h]), contract_last(values[h], plain[h][1])

    def finish(h, probs, grad_scores):
        query, grad = plain[h]
        dv[h] += rows_by_columns(probs, grad)
        dk[h] += rows_by_columns(grad_scores, query)
        return (rows_by_columns(turned[h], grad_scores) * scaling).T.astype(BF)

    parts = []
    before = None
    scores, grad_probs = scores_of(0)
    for h in range(heads):
        later = scores_of(h + 1) if h + 1 < heads else (None, None)
        probs = jnp.exp2(scores * STEEP)
        centre = jnp.sum(probs * grad_probs, axis=0, keepdims=True)
        grad_scores = (probs * (grad_probs - centre)).astype(BF)
        if before is not None:
            parts.append(finish(h - 1, *before))
        before = (probs.astype(BF), grad_scores)
        scores, grad_probs = later
    parts.append(finish(heads - 1, *before))
    grad_queries = jnp.concatenate(parts, axis=1)

    @pl.when(i == 0)
    def _():
        out_first[0, :, :width] = grad_queries

    @pl.when(i == 1)
    def _():
        out_second[0, :, :width] = grad_queries
        for start, ref in ((0, out_first), (half, out_second)):
            rows = slice(start, start + half)
            ref[0, :, width:] = padded_columns(
                [(dk[h, rows] * scaling).astype(BF) for h in range(heads)]
                + [dv[h, rows].astype(BF) for h in range(heads)],
                padded - width,
            )


def attend_back(first, second, do_first, do_second, l_first, l_second, query_marks, key_marks):
    groups, half, padded = first.shape
    heads = l_first.shape[1]
    out_width = do_first.shape[2]
    pair = lambda *dims: pl.BlockSpec((1,) + dims, lambda a, i: (a, 0, 0))
    return pl.pallas_call(
        partial(attend_back_kernel, heads),
        grid=(groups, 2),
        in_specs=[pair(half, padded)] * 2
        + [pair(half, out_width)] * 2
        + [pair(heads, half)] * 2
        + [
            pl.BlockSpec((half, MARKS), lambda a, i: (i, 0)),
            pl.BlockSpec((2 * half, MARKS), lambda a, i: (0, 0)),
        ],
        out_specs=[pair(half, padded)] * 2,
        out_shape=[shape((groups, half, padded), BF)] * 2,
        scratch_shapes=[
            pltpu.VMEM((heads, 2 * half, DEPTH), BF),
            pltpu.VMEM((heads, 2 * half, HEAD_DIM), BF),
            pltpu.VMEM((heads, HEAD_DIM, 2 * half), BF),
            pltpu.VMEM((heads, half, DEPTH), BF),
            pltpu.VMEM((heads, 2 * half, HEAD_DIM), F32),
            pltpu.VMEM((heads, 2 * half, HEAD_DIM), F32),
        ],
        compiler_params=params(60),
        cost_estimate=cost(groups * 12e9, groups * half * padded * 12, groups * heads * half * half),
    )(first, second, do_first, do_second, l_first, l_second, query_marks, key_marks)


def image_sums(hot_turned, values):
    high = values.astype(BF)
    low = (values - high.astype(F32)).astype(BF)
    return rows_by_columns(hot_turned, high) + rows_by_columns(hot_turned, low)


def add_up(ref, value):
    @pl.when(pl.program_id(0) == 0)
    def _():
        ref[...] = value

    @pl.when(pl.program_id(0) != 0)
    def _():
        ref[...] += value


def third_of(first, second, own, other, i, per):
    half = jnp.stack([own[0], other[0]], axis=0)
    return jnp.where(i < per, first[...], jnp.where(i < 2 * per, second[...], half))


def third_specs(block, columns, per):
    full = lambda low: pl.BlockSpec(
        (2, block, columns), lambda i, y: (0, jnp.clip(i - low * per, 0, per - 1), 0)
    )
    single = pl.BlockSpec((1, block, columns), lambda i, y: (0, jnp.clip(i - 2 * per, 0, per - 1), 0))
    return [full(0), full(1), single, single]


def out_weight_specs(width, columns):
    last = columns // (2 * width // 3) - 1
    return [
        pl.BlockSpec((1, width, 2 * width // 3), lambda i, y: (y[0], 0, last)),
        pl.BlockSpec((1, width, 2 * width // 3), lambda i, y: (1 - y[0], 0, last)),
    ]


def middle_kernel(
    side, tok_ref, dy_ref, first, second, own, other, w_own, w_other, b_ref, hot_ref, parts_ref,
    branch_ref, h_ref, g_ref, ht_ref, gt_ref, gb_ref,
):
    i = pl.program_id(0)
    width = tok_ref.shape[1]
    used = width // 2
    att = third_of(first, second, own, other, i, pl.num_programs(0) // 3)[:, :, :used]
    skip = w_own.shape[2] - used
    branch = (
        contract_last(att[0], w_own[0, :, skip:])
        + contract_last(att[1], w_other[0, :, skip:])
        + b_ref[...]
    )
    branch_ref[...] = branch
    hot = hot_ref[...]
    gate = rows_by_columns(hot, parts_ref[0, :, 2 * width :])
    mod = rows_by_columns(hot, parts_ref[1])
    normed, _ = layer_norm(tok_ref[...].astype(F32) + gate * branch)
    hidden = (normed * (1.0 + mod[:, width : 2 * width]) + mod[:, :width]).astype(BF)
    grad = (dy_ref[...].astype(F32) * mod[:, 2 * width :]).astype(BF)
    h_ref[...] = hidden
    g_ref[...] = grad
    turn_in_order(side, ht_ref, hidden)
    turn_in_order(side, gt_ref, grad)
    add_up(gb_ref, jnp.sum(grad.astype(F32), axis=0, keepdims=True))


def middle_part(side, tokens, cotangent, thirds, weights, b_out, hot, parts, block):
    ring = side.shape[0] // 2
    rows, width = tokens.shape
    per = rows // 3 // block
    spec = lambda dims: pl.BlockSpec(dims, lambda i, y: (0,) * len(dims))
    placed = pl.BlockSpec(
        (block, width), lambda i, y: (((i // per + y[0]) % 3) * per + i % per, 0)
    )
    plain = pl.BlockSpec((block, width), lambda i, y: (i, 0))
    turned = pl.BlockSpec((ring, width // ring, block), lambda i, y: (0, 0, i))
    return pl.pallas_call(
        middle_kernel,
        grid_spec=pltpu.PrefetchScalarGridSpec(
            num_scalar_prefetch=1,
            grid=(rows // block,),
            in_specs=[
                placed,
                placed,
                *third_specs(block, thirds[0].shape[2], per),
                *out_weight_specs(width, weights.shape[2]),
                spec((1, width)),
                pl.BlockSpec((block, hot.shape[1]), lambda i, y: (i, 0)),
                spec(parts.shape),
            ],
            out_specs=[plain, plain, plain, turned, turned, spec((1, width))],
        ),
        out_shape=[
            shape((rows, width), F32),
            shape((rows, width), BF),
            shape((rows, width), BF),
            shape((ring, width // ring, rows), BF),
            shape((ring, width // ring, rows), BF),
            shape((1, width), F32),
        ],
        compiler_params=params(),
        cost_estimate=cost(2 * rows * width * (3 * width + 1024), rows * width * 22),
    )(side, tokens, cotangent, *thirds, weights, weights, b_out, hot, parts)


def feed_kernel(
    chunk, pick, h_ref, g_ref, ht_ref, gt_ref, up_ref, down_ref, bias_ref,
    branch_ref, back_ref, mine_ref, near_ref, far_ref, gb_ref, act, pre,
):
    j = pl.program_id(0)
    rows = h_ref.shape[0]
    half = ht_ref.shape[0] // 2
    up = up_ref[0, 0]
    down = down_ref[0, 0]
    total = jnp.zeros(gb_ref.shape, F32)
    for start in range(0, rows, chunk):
        at = slice(start, start + chunk)
        u = rows_by_columns(h_ref[at], up) + bias_ref[0]
        grad = rows_by_columns(g_ref[at], down)
        cube = GELU_CUBE * u * u
        bent = jnp.tanh(GELU_SLOPE * (u + cube * u))
        part = 0.5 * (1.0 + bent)
        slope = part + 0.5 * u * (1.0 - bent * bent) * (GELU_SLOPE * (1.0 + 3.0 * cube))
        low = (u * part).astype(BF)
        back = (grad * slope).astype(BF)
        act[at] = low
        pre[at] = back
        total += jnp.sum(back.astype(F32), axis=0, keepdims=True)
        branch_part = contract_last(low, down)
        back_part = contract_last(back, up)

        @pl.when(j == 0)
        def _():
            branch_ref[at] = branch_part
            back_ref[at] = back_part

        @pl.when(j != 0)
        def _():
            branch_ref[at] += branch_part
            back_ref[at] += back_part

    gb_ref[...] = total
    quarter = half // 2
    for k, (turned, value) in enumerate(((ht_ref, pre), (gt_ref, act))):
        theirs = rows_by_columns(turned[half:], value[...]).astype(BF)
        near_ref[k] = theirs[:quarter]
        far_ref[k] = theirs[quarter:]
        mine_ref[k] = rows_by_columns(turned[:half], value[...])


def feed(pick, hidden, grad, hidden_turned, grad_turned, weights, bias, chunk, cols):
    rows, width = hidden.shape
    units = weights.shape[3]
    half = width // 2
    whole = lambda dims: pl.BlockSpec(dims, lambda j, y: (0, 0), pipeline_mode=pl.Buffered(1))
    columns = lambda k: pl.BlockSpec((1, 1, width, cols), lambda j, y: (k, y[0], 0, j))
    return pl.pallas_call(
        partial(feed_kernel, chunk),
        grid_spec=pltpu.PrefetchScalarGridSpec(
            num_scalar_prefetch=1,
            grid=(units // cols,),
            in_specs=[
                whole((rows, width)),
                whole((rows, width)),
                whole((width, rows)),
                whole((width, rows)),
                columns(0),
                columns(1),
                pl.BlockSpec((1, 1, cols), lambda j, y: (y[0], 0, j)),
            ],
            out_specs=[
                whole((rows, width)),
                whole((rows, width)),
                pl.BlockSpec((2, half, cols), lambda j, y: (0, 0, j)),
                pl.BlockSpec((2, half // 2, cols), lambda j, y: (0, 0, j)),
                pl.BlockSpec((2, half // 2, cols), lambda j, y: (0, 0, j)),
                pl.BlockSpec((1, cols), lambda j, y: (0, j)),
            ],
            scratch_shapes=[pltpu.VMEM((rows, cols), BF), pltpu.VMEM((rows, cols), BF)],
        ),
        out_shape=[
            shape((rows, width), F32),
            shape((rows, width), F32),
            shape((2, half, units), F32),
            shape((2, half // 2, units), BF),
            shape((2, half // 2, units), BF),
            shape((1, units), F32),
        ],
        compiler_params=params(60),
        cost_estimate=cost(
            12 * rows * width * units, rows * width * 16 + width * units * 10, rows * units
        ),
    )(pick, hidden, grad, hidden_turned, grad_turned, weights, weights, bias)


def back_two_kernel(
    side, tok_ref, dy_ref, branch_ref, two_a, two_b, b_ref, back_a, back_b, w_own, w_other, hot_ref,
    turn_ref, parts_ref, first, second, half_own, half_other, out_ref, middle_ref, a_first, a_second,
    a_own, a_other, sums_ref, gb_ref, mine_ref, theirs_ref, outer_ref,
):
    width = tok_ref.shape[1]
    hot = hot_ref[...]
    turn = turn_ref[...]
    gate = rows_by_columns(hot, parts_ref[0, :, 2 * width :])
    mod = rows_by_columns(hot, parts_ref[1])
    branch = branch_ref[...]
    middle = tok_ref[...].astype(F32) + gate * branch
    branch_two = two_a[...] + two_b[...] + b_ref[...]
    grad_hidden = back_a[...] + back_b[...]
    dy = dy_ref[...].astype(F32)
    out_ref[...] = (middle + mod[:, 2 * width :] * branch_two).astype(BF)
    normed, inverse = layer_norm(middle)
    grad_middle = dy + norm_back(normed, inverse, grad_hidden * (1.0 + mod[:, width : 2 * width]))
    middle_ref[...] = grad_middle
    grad = (grad_middle * gate).astype(BF)
    turned = grad.astype(F32).T.astype(BF)
    att = third_of(first, second, half_own, half_other, pl.program_id(0), pl.num_programs(0) // 3)
    for k in range(2):
        product = rows_by_columns(turned, att[k])

        @pl.when(pl.program_id(0) == 0)
        def _():
            outer_ref[k] = product

        @pl.when(pl.program_id(0) != 0)
        def _():
            outer_ref[k] += product

    @pl.when(pl.program_id(0) == pl.num_programs(0) - 1)
    def _():
        ring = side.shape[0] // 2
        piece = width // ring
        for k in range(2):
            pieces = [
                outer_ref[k, pl.ds(pl.multiple_of(side[1 + ring + j] * piece, 8), piece)]
                for j in range(ring)
            ]
            mine_ref[k] = jnp.concatenate(pieces[: ring // 2], axis=0)
            theirs_ref[k] = jnp.concatenate(pieces[ring // 2 :], axis=0).astype(BF)

    skip = w_own.shape[2] - width // 2
    ours = padded_columns([rows_by_columns(grad, w_own[0, :, skip:]).astype(BF)], a_own.shape[2])
    theirs = padded_columns([rows_by_columns(grad, w_other[0, :, skip:]).astype(BF)], a_own.shape[2])
    i = pl.program_id(0)
    per = pl.num_programs(0) // 3
    for k, ref in enumerate((a_first, a_second)):

        @pl.when(i // per == k)
        def _(ref=ref):
            ref[0] = ours
            ref[1] = theirs

    @pl.when(i // per == 2)
    def _():
        a_own[0] = ours
        a_other[0] = theirs

    sums = [
        image_sums(turn, grad_middle * branch),
        image_sums(turn, grad_hidden),
        image_sums(turn, grad_hidden * normed),
        image_sums(turn, dy * branch_two),
    ]
    add_up(sums_ref, jnp.stack(sums, axis=0))
    add_up(gb_ref, jnp.sum(grad.astype(F32), axis=0, keepdims=True))


def back_two(
    side, tokens, cotangent, branch, two_a, two_b, b_down, back_a, back_b, weights, hot, turn, parts,
    attended, block, images, out_width,
):
    rows, width = tokens.shape
    third = rows // 3
    per = rows // 3 // block
    spec = lambda dims: pl.BlockSpec(dims, lambda i, y: (0,) * len(dims))
    placed = pl.BlockSpec(
        (block, width), lambda i, y: (((i // per + y[0]) % 3) * per + i % per, 0)
    )
    plain = pl.BlockSpec((block, width), lambda i, y: (i, 0))
    return pl.pallas_call(
        back_two_kernel,
        grid_spec=pltpu.PrefetchScalarGridSpec(
            num_scalar_prefetch=1,
            grid=(rows // block,),
            in_specs=[
                placed,
                placed,
                plain,
                plain,
                plain,
                spec((1, width)),
                plain,
                plain,
                *out_weight_specs(width, weights.shape[2]),
                pl.BlockSpec((block, hot.shape[1]), lambda i, y: (i, 0)),
                pl.BlockSpec((images, block), lambda i, y: (0, i)),
                spec(parts.shape),
                *third_specs(block, out_width, per),
            ],
            out_specs=[
                placed,
                plain,
                *third_specs(block, out_width, per),
                spec((4, images, width)),
                spec((1, width)),
                spec((2, width // 2, out_width)),
                spec((2, width // 2, out_width)),
            ],
            scratch_shapes=[pltpu.VMEM((2, width, out_width), F32)],
        ),
        out_shape=[
            shape((rows, width), BF),
            shape((rows, width), F32),
            *[shape((2, third, out_width), BF)] * 2,
            *[shape((1, third, out_width), BF)] * 2,
            shape((4, images, width), F32),
            shape((1, width), F32),
            shape((2, width // 2, out_width), F32),
            shape((2, width // 2, out_width), BF),
        ],
        compiler_params=params(62),
        cost_estimate=cost(2 * rows * width * (4 * width + 1024), rows * width * 34),
    )(side, tokens, cotangent, branch, two_a, two_b, b_down, back_a, back_b, weights, weights, hot, turn, parts, *attended)


def outer_kernel(ht_ref, first, second, rest, mine_ref, theirs_ref, sums_ref):
    third = first.shape[1]
    grads = (first[0], second[0], rest[0])
    found = sum(
        rows_by_columns(ht_ref[:, k * third : (k + 1) * third], grad)
        for k, grad in enumerate(grads)
    )

    @pl.when(pl.program_id(0) == 0)
    def _():
        theirs_ref[...] = found.astype(BF)
        sums_ref[...] = sum(jnp.sum(grad.astype(F32), axis=0, keepdims=True) for grad in grads)

    @pl.when(pl.program_id(0) == 1)
    def _():
        mine_ref[...] = found


def outer(turned, first, second, rest, group):
    width, rows = turned.shape
    _, third, cols = first.shape
    block = pl.BlockSpec((width // 2, cols), lambda k: (0, 0))
    pair = pl.BlockSpec((1, third, cols), lambda k: (group, 0, 0))
    single = pl.BlockSpec((1, third, cols), lambda k: (0, 0, 0))
    return pl.pallas_call(
        outer_kernel,
        grid=(2,),
        in_specs=[pl.BlockSpec((width // 2, rows), lambda k: (1 - k, 0)), pair, pair, single],
        out_specs=[block, block, pl.BlockSpec((1, cols), lambda k: (0, 0))],
        out_shape=[shape((width // 2, cols), F32), shape((width // 2, cols), BF), shape((1, cols), F32)],
        compiler_params=params(60),
        cost_estimate=cost(2 * rows * width * cols, rows * width * 2 + rows * cols * 4),
    )(turned, first, second, rest)


def back_one_kernel(
    side, first, second, own, other, w_own, w_other, tok_ref, middle_ref, hot_ref, turn_ref, parts_ref,
    out_ref, sums_ref,
):
    width = tok_ref.shape[1]
    cols = 3 * width // 2
    scale = rows_by_columns(hot_ref[...], parts_ref[0, :, width : 2 * width])
    grads = third_of(first, second, own, other, pl.program_id(0), pl.num_programs(0) // 3)[:, :, :cols]
    grad_hidden = contract_last(grads[0], w_own[0, :, :cols]) + contract_last(
        grads[1], w_other[0, :, :cols]
    )
    normed, inverse = layer_norm(tok_ref[...].astype(F32))
    out_ref[...] = middle_ref[...] + norm_back(normed, inverse, grad_hidden * (1.0 + scale))
    turn = turn_ref[...]
    sums = [image_sums(turn, grad_hidden), image_sums(turn, grad_hidden * normed)]
    add_up(sums_ref, jnp.stack(sums, axis=0))


def back_one(side, thirds, weights, tokens, middle, hot, turn, parts, block, images):
    rows, width = tokens.shape
    cols = thirds[0].shape[2]
    per = rows // 3 // block
    spec = lambda dims: pl.BlockSpec(dims, lambda i, y: (0,) * len(dims))
    once = pl.Buffered(1)
    placed = pl.BlockSpec(
        (block, width), lambda i, y: (((i // per + y[0]) % 3) * per + i % per, 0)
    )
    return pl.pallas_call(
        back_one_kernel,
        grid_spec=pltpu.PrefetchScalarGridSpec(
            num_scalar_prefetch=1,
            grid=(rows // block,),
            in_specs=[
                *third_specs(block, cols, per),
                pl.BlockSpec(
                    (1,) + weights.shape[1:], lambda i, y: (y[0], 0, 0), pipeline_mode=once
                ),
                pl.BlockSpec(
                    (1,) + weights.shape[1:], lambda i, y: (1 - y[0], 0, 0), pipeline_mode=once
                ),
                placed,
                pl.BlockSpec((block, width), lambda i, y: (i, 0)),
                pl.BlockSpec((block, hot.shape[1]), lambda i, y: (i, 0)),
                pl.BlockSpec((images, block), lambda i, y: (0, i)),
                spec(parts.shape),
            ],
            out_specs=[placed, spec((2, images, width))],
        ),
        out_shape=[shape((rows, width), F32), shape((2, images, width), F32)],
        compiler_params=params(),
        cost_estimate=cost(4 * rows * width * cols, rows * width * 10 + rows * cols * 4),
    )(side, *thirds, weights, weights, tokens, middle, hot, turn, parts)


def fast_body(mesh):
    ring = mesh.shape["rows"]
    both = ("rows", "heads")

    def moves(row_of, other_heads):
        pairs = []
        for r in range(ring):
            for y in range(2):
                pairs.append((2 * r + y, 2 * row_of(r) + (1 - y if other_heads else y)))
        return pairs

    to_core = moves(lambda r: r ^ 1, False)
    to_heads = moves(lambda r: r, True)
    to_x = moves(lambda r: r ^ 2, False)
    to_corner = moves(lambda r: r ^ 2, True)
    levels = ring // 4
    to_level = [moves(lambda r, k=k: (r + 4 * k) % ring, False) for k in range(levels)]

    def send(values, pairs):
        return lax.ppermute(values, both, pairs)

    def after(*values):
        return lax.optimization_barrier(values)

    def body(
        tokens,
        condition,
        segment_ids,
        tile_mask,
        image_index,
        w_ada,
        b_ada,
        w_query,
        w_key,
        w_value,
        b_query,
        b_value,
        w_out,
        b_out,
        w_up,
        b_up,
        w_down,
        b_down,
        cotangent,
    ):
        y = lax.axis_index("heads")
        r = lax.axis_index("rows")
        rows, width = tokens.shape
        length = segment_ids.shape[1]
        third = rows // 3
        images = condition.shape[0]
        units = w_up.shape[1]
        cols = w_query.shape[1]

        tiles = length // TILE
        slots = image_index.shape[1]

        def open_to(tiles_on):
            on = (tiles_on > 0) | jnp.eye(tiles, dtype=bool)
            return jnp.repeat(on.astype(jnp.int32), TILE, axis=1)

        seg_full = lax.dynamic_index_in_dim(segment_ids, 2 * y, 0, keepdims=False)
        tile_full = lax.dynamic_index_in_dim(tile_mask, 2 * y, 0, keepdims=False)
        seg_half = jnp.where(y == 0, segment_ids[1], jnp.roll(segment_ids[1], -third))
        shift = third // TILE
        tile_half = jnp.where(
            y == 0, tile_mask[1], jnp.roll(tile_mask[1], (-shift, -shift), axis=(0, 1))
        )
        marks = marks_of(seg_full[None], open_to(tile_full), seg_half[None], open_to(tile_half))

        def image_of(seg, index):
            slot = jnp.arange(slots, dtype=jnp.int32)
            return jnp.sum(jnp.where(seg[:, None] == slot[None, :], index[None, :], 0), axis=1)

        own_image = jnp.concatenate(
            [
                image_of(seg_full, lax.dynamic_index_in_dim(image_index, 2 * y, 0, keepdims=False)),
                image_of(seg_half[:third], image_index[1]),
            ]
        )
        chosen = jnp.arange(images, dtype=jnp.int32)
        hot = (own_image[:, None] == jnp.tile(chosen, 3)[None, :]).astype(BF)
        turn = (chosen[:, None] == own_image[None, :]).astype(BF)

        order = jnp.arange(ring, dtype=jnp.int32)
        core_of, x_of, level_of = order // (ring // 2), (order // levels) % 2, order % levels
        owner = ((r // 4 + level_of) % levels) * 4 + ((r // 2 % 2) ^ x_of) * 2 + ((r % 2) ^ core_of)
        piece = width // ring
        place = jnp.sum(jnp.where(owner[None, :] == order[:, None], order[None, :], 0), axis=1)
        side = jnp.concatenate([y.reshape(1), place, owner])

        padded = -(-3 * cols // 128) * 128
        out_width = -(-cols // 128) * 128
        here = jnp.stack([y, r // 4, (r // 2) % 2, r % 2]).astype(jnp.int32)
        next_level = to_level[levels - 1]

        class Tree:
            def __init__(self, shard):
                self.count = shard.shape[-1] // 3
                self.first = [shard[..., : 2 * self.count]]
                self.last = [shard[..., 2 * self.count :]]
                self.step = 0

            def sends(self):
                moves = (
                    (next_level, to_x),
                    (next_level, to_heads),
                    (next_level, next_level),
                    (to_x, to_heads, next_level),
                    (to_heads, to_x, next_level),
                    (to_core,) * 5,
                )[self.step]
                if self.step < 3:
                    self.sent = (self.first[-1], self.last[-1])
                elif self.step < 5:
                    self.sent = (self.over_x, self.over_y, self.last[-1])
                else:
                    self.sent = (*self.over_x, *self.over_y, self.last)
                return [send(value, move) for value, move in zip(self.sent, moves)]

            def take(self, got):
                if self.step < 2:
                    self.first.append(got[0])
                    self.last = [jnp.stack([self.last[0], got[1]])]
                elif self.step == 2:
                    whole = jnp.stack([*self.first, got[0]])
                    self.over_x, self.over_y = whole[..., : self.count], whole[..., self.count :]
                    self.last.append(got[1])
                elif self.step == 3:
                    self.over_x = jnp.stack([self.over_x, got[0]])
                    self.over_y = jnp.stack([self.over_y, got[1]])
                    self.last.append(got[2])
                elif self.step == 4:
                    self.over_x = (self.over_x, got[0])
                    self.over_y = (self.over_y, got[1])
                    self.last = jnp.stack([*self.last, got[2]])
                else:
                    self.whole = collected(here, (*self.sent, *got))
                self.step += 1

        shard = jnp.concatenate([w_query, w_key, w_value, w_out], axis=1).astype(BF)
        tree = Tree(shard[None])
        cond = condition.astype(F32)
        mod_cols, *got = after(
            jnp.dot(jax.nn.silu(cond), w_ada, precision=PRECISE) + b_ada, *tree.sends()
        )
        tree.take(got)
        biases = jnp.concatenate([b_up, b_query, b_value])[None]
        own_spread = jnp.concatenate([mod_cols, biases], axis=0)
        got_spread, hot, turn, side, *joined = after(
            send(own_spread, to_heads), hot, turn, side, *marks, *tree.sends()
        )
        marks_full, marks_half = joined[:2], joined[2:4]
        tree.take(joined[4:])
        spread = jnp.where(
            y == 0, jnp.stack([own_spread, got_spread]), jnp.stack([got_spread, own_spread])
        )
        parts = three_parts(spread[:, :images])
        up_bias = spread[:, images:, :units]
        qkv_bias = jnp.concatenate(
            [
                spread[:, images:, units : units + cols],
                jnp.zeros((2, 1, cols), F32),
                spread[:, images:, units + cols :],
            ],
            axis=2,
        )
        hidden_full, hidden_half, hidden_one_turned, qkv_bias, up_bias, *got = after(
            *first_norm(side, tokens, hot, parts, third), qkv_bias, up_bias, *tree.sends()
        )
        tree.take(got)
        feed_shard = jnp.stack([w_up, w_down]).astype(BF)
        hidden_full, hidden_half, feed_shard, *got = after(
            hidden_full, hidden_half, feed_shard, *tree.sends()
        )
        tree.take(got)
        hidden_full, hidden_half, *got = after(hidden_full, hidden_half, *tree.sends())
        tree.take(got)
        feed_weights = lax.all_gather(
            feed_shard, ("heads", "rows"), axis=1, tiled=True
        ).reshape(2, 2, width, units)
        hidden_full, hidden_half, *got = after(hidden_full, hidden_half, *tree.sends())
        tree.take(got)
        attention_weights = tree.whole.reshape(2, width, shard.shape[1])

        qkv_first, qkv_second, hidden_got = after(
            *project(
                side, hidden_full, hidden_full, attention_weights, qkv_bias, padded, third, 2
            ),
            send(hidden_half, to_heads),
        )
        qkv_full = (qkv_first, qkv_second)
        qkv_half = project(
            side, hidden_half, hidden_got, attention_weights, qkv_bias, padded, third, 1
        )
        qkv_own, qkv_got, condition = after(*qkv_half, condition)
        qkv_half = (qkv_own, qkv_got)
        out_own, out_theirs, l_own, l_other, *got = after(
            *attend(*qkv_half, *marks_half, out_width),
            *(send(condition, to_level[k]) for k in range(1, levels)),
        )
        lse_half = (l_own, l_other)
        qkv_first, out_theirs, flat = after(qkv_first, out_theirs, jnp.stack([condition, *got]))
        out_first, out_second, *lse_full, out_other, got = after(
            *attend(qkv_first, qkv_second, *marks_full, out_width),
            send(out_theirs, to_heads),
            send(flat, to_x),
        )
        out_first, flat = after(out_first, jnp.concatenate([flat, got], axis=0))
        attended = (out_first, out_second, out_own, out_other)
        branch_one, hidden_two, grad_two, hidden_two_turned, grad_two_turned, grad_b_down, got = after(
            *middle_part(
                side, tokens, cotangent, attended, attention_weights, b_out[None], hot, parts, third // 2
            ),
            send(flat, to_core),
        )
        flat = jnp.concatenate([flat, got], axis=0)
        silu_all = jax.nn.silu(flat.reshape(ring * images, width).astype(F32))

        def added(mine, got):
            return mine + got.astype(F32)

        def level_pieces(values):
            part = lambda k: values[..., k * piece : (k + 1) * piece, :]
            return part(0), *(part(k).astype(BF) for k in range(1, levels))

        def all_added(kept, got):
            for part in got:
                kept = added(kept, part)
            return kept

        quarter = width // 4

        def plane_pieces(mine_own, got_own, mine_other, got_other):
            near = lambda mine, got: added(mine[:quarter], got[:quarter])
            far = lambda mine, got: added(mine[quarter:], got[quarter:]).astype(BF)
            return (
                near(mine_own, got_own),
                far(mine_own, got_own),
                near(mine_other, got_other).astype(BF),
                far(mine_other, got_other),
            )

        flat_turned = lambda values: values.reshape(width, rows)
        hidden_one_turned = flat_turned(hidden_one_turned)
        feed_args = (flat_turned(hidden_two_turned), flat_turned(grad_two_turned), feed_weights, up_bias, rows // 2, 768)
        two_b, back_b, mine_b, near_b, far_b, grad_b_up_b = feed(
            1 - y.reshape(1), hidden_two, grad_two, *feed_args
        )
        far_b = added(mine_b[:, quarter:], send(far_b, to_core)).astype(BF)
        hidden_two, far_b, near_b = after(hidden_two, far_b, near_b)
        two_a, back_a, mine_a, near_a, far_a, grad_b_up_a, near_b, far_b = after(
            *feed(y.reshape(1), hidden_two, grad_two, *feed_args),
            send(near_b, to_core),
            send(far_b, to_x),
        )
        over_b = added(added(mine_b[:, :quarter], near_b), far_b).astype(BF)
        far_a = added(mine_a[:, quarter:], send(far_a, to_core)).astype(BF)
        two_a, over_b, far_a, near_a = after(two_a, over_b, far_a, near_a)

        output, grad_middle, *grad_attended, sums_two, grad_b_out, out_mine, out_theirs_sum, over_b, far_a, near_a = after(
            *back_two(
                side, tokens, cotangent, branch_one, two_a, two_b, b_down[None], back_a, back_b, attention_weights,
                hot, turn, parts, attended, third // 2, images, out_width,
            ),
            send(over_b, to_heads),
            send(far_a, to_x),
            send(near_a, to_core),
        )
        grad_first, grad_second, grad_own, grad_theirs = grad_attended
        grad_other = send(grad_theirs, to_heads)
        out_got = send(out_theirs_sum, to_core)
        out_pieces = plane_pieces(out_mine[0], out_got[0], out_mine[1], out_got[1])
        feed_kept, *feed_sent = level_pieces(
            added(added(added(mine_a[:, :quarter], near_a), far_a), over_b)
        )
        grad_own, feed_kept, *joined = after(grad_own, feed_kept, *feed_sent, *out_pieces)
        feed_sent, out_pieces = joined[: levels - 1], joined[levels - 1 :]
        grad_qkv_own, grad_qkv_theirs, *got = after(
            *attend_back(*qkv_half, grad_own, grad_other, *lse_half, *marks_half),
            send(out_pieces[1], to_x),
            send(out_pieces[2], to_heads),
            send(out_pieces[3], to_corner),
        )
        out_kept, *out_sent = level_pieces(all_added(out_pieces[0], got))
        grad_first, grad_qkv_theirs, feed_kept, out_kept, *joined = after(
            grad_first, grad_qkv_theirs, feed_kept, out_kept, *feed_sent, *out_sent
        )
        feed_sent, out_sent = joined[: levels - 1], joined[levels - 1 :]
        grad_qkv_first, grad_qkv_second, grad_qkv_other, *got = after(
            *attend_back(*qkv_full, grad_first, grad_second, *lse_full, *marks_full),
            send(grad_qkv_theirs, to_heads),
            *(send(part, to_level[k + 1]) for k, part in enumerate(feed_sent)),
        )
        grad_w_up, grad_w_down = all_added(feed_kept, got)
        qkv_mine_b, qkv_theirs_b, grad_qkv_bias_b, *got = after(
            *outer(hidden_one_turned, grad_qkv_first, grad_qkv_second, grad_qkv_other, 1),
            *(send(part, to_level[k + 1]) for k, part in enumerate(out_sent)),
        )
        grad_w_out = all_added(out_kept, got)
        hidden_one_turned, qkv_theirs_b = after(hidden_one_turned, qkv_theirs_b)
        qkv_mine_a, qkv_theirs_a, grad_qkv_bias_a, qkv_got_b = after(
            *outer(hidden_one_turned, grad_qkv_first, grad_qkv_second, grad_qkv_own, 0),
            send(qkv_theirs_b, to_core),
        )
        near, *sent = plane_pieces(qkv_mine_a, send(qkv_theirs_a, to_core), qkv_mine_b, qkv_got_b)
        grad_middle, near, *sent = after(grad_middle, near, *sent)
        grad_qkv = (grad_qkv_first, grad_qkv_second, grad_qkv_own, grad_qkv_other)
        grad_tokens, sums_one, *got = after(
            *back_one(
                side, grad_qkv, attention_weights, tokens, grad_middle, hot, turn, parts, third // 2, images
            ),
            send(sent[0], to_x),
            send(sent[1], to_heads),
            send(sent[2], to_corner),
        )
        qkv_kept, *qkv_sent = level_pieces(all_added(near, got))

        sums = jnp.concatenate([sums_one, sums_two], axis=0).reshape(2, 3, images, width)
        sums = sums.transpose(0, 2, 1, 3).reshape(2, images, 3 * width)
        narrow = jnp.concatenate([grad_b_out, grad_b_down], axis=0).reshape(2, 2, cols)

        def packet(which, up_sum, qkv_sum):
            second = lax.dynamic_index_in_dim(narrow, which, 1, keepdims=False).reshape(-1)
            short = [up_sum[0], qkv_sum[:cols], qkv_sum[2 * cols : 3 * cols], second]
            short = jnp.concatenate(short).reshape(images, -1)
            chunk = lax.dynamic_index_in_dim(sums, which, 0, keepdims=False)
            gap = -(chunk.shape[1] + short.shape[1]) % 128
            return jnp.concatenate([chunk, short, jnp.zeros((images, gap), F32)], axis=1)

        own_packet = packet(y, grad_b_up_a, grad_qkv_bias_a[0]) + send(
            packet(1 - y, grad_b_up_b, grad_qkv_bias_b[0]), to_heads
        )
        own_packet, qkv_kept, *qkv_sent = after(own_packet, qkv_kept, *qkv_sent)
        grad_silu = lax.dot_general(
            own_packet[:, : 3 * width],
            w_ada,
            (((1,), (1,)), ((), ())),
            precision=PRECISE,
            preferred_element_type=F32,
        )
        grad_silu, *got = after(
            grad_silu, *(send(own_packet, to_level[k]) for k in range(1, levels))
        )
        flat = jnp.concatenate([own_packet, *got], axis=0)
        flat, *qkv_sent = after(flat, *qkv_sent)
        silu_got, flat_got, *got = after(
            send(grad_silu, to_heads),
            send(flat, to_x),
            *(send(part, to_level[k + 1]) for k, part in enumerate(qkv_sent)),
        )
        grad_w_qkv = all_added(qkv_kept, got)
        flat = jnp.concatenate([flat, flat_got], axis=0)
        packets = jnp.concatenate([flat, send(flat, to_core)], axis=0)
        grad_mod = packets[:, : 3 * width]
        count = units + 4 * cols
        short = packets[:, 3 * width : 3 * width + count // images]
        bias_sums = jnp.sum(short.reshape(ring, images, count // images), axis=0).reshape(-1)
        s1, s2, _ = jnp.split(three_parts(silu_all), 3, axis=0)
        g1, g2, _ = jnp.split(three_parts(grad_mod), 3, axis=0)
        grad_w_ada = contract_first(
            jnp.concatenate([s1, s1, s2], axis=0), jnp.concatenate([g1, g2, g1], axis=0)
        )
        grad_b_ada = jnp.sum(grad_mod, axis=0)
        grad_silu = grad_silu + silu_got
        _, silu_back = jax.vjp(jax.nn.silu, cond)
        grad_condition = silu_back(grad_silu)[0]
        return (
            output,
            grad_tokens,
            grad_condition,
            grad_w_ada,
            grad_b_ada,
            grad_w_qkv[:, :cols],
            grad_w_qkv[:, cols : 2 * cols],
            grad_w_qkv[:, 2 * cols : 3 * cols],
            bias_sums[units : units + cols],
            bias_sums[units + cols : units + 2 * cols],
            grad_w_out[:, :cols],
            bias_sums[units + 2 * cols : units + 3 * cols],
            grad_w_up,
            bias_sums[:units],
            grad_w_down,
            bias_sums[units + 3 * cols :],
        )

    return body


def solution(mesh):
    body = fast_body(mesh) if mesh.shape["heads"] == 2 and mesh.shape["rows"] == 16 else general_body
    placed = (
        P(("rows", "heads"), None),
        P("rows", None),
        P("rows", None),
        P("rows", None, None),
        P("rows", None),
        P(None, "heads"),
        P("heads"),
        P("rows", "heads"),
        P("rows", "heads"),
        P("rows", "heads"),
        P("heads"),
        P("heads"),
        P("rows", "heads"),
        P(),
        P("rows", "heads"),
        P("heads"),
        P("rows", "heads"),
        P(),
        P(("rows", "heads"), None),
    )
    return jax.shard_map(
        body,
        mesh=mesh,
        in_specs=placed,
        out_specs=(
            P(("rows", "heads"), None),
            P(("rows", "heads"), None),
            P("rows", None),
            P(None, "heads"),
            P("heads"),
            P("rows", "heads"),
            P("rows", "heads"),
            P("rows", "heads"),
            P("heads"),
            P("heads"),
            P("rows", "heads"),
            P("heads"),
            P("rows", "heads"),
            P("heads"),
            P("rows", "heads"),
            P("heads"),
        ),
        check_vma=False,
    )
```
